32 devices in a mesh: tile: 8 (over y, x, core), section: 4 (over z).
Axes of the slice: x: 2, y: 2, z: 4, core: 2. Of those that a mesh axis runs over, the one named last changes fastest.
Arguments:
- state: float32 [5, 2, 192, 1536], P(None, None, 'tile', 'section'), may hold values from -6 to 6
- courant: float32 [2, 2, 192, 1536], P(None, None, 'tile', 'section'), may hold values from -0.4 to 0.4
- nest_offset: int32 [1], replicated, may hold values from 24 to 95
Outputs:
- new_state: float32 [5, 2, 192, 1536], P(None, None, 'tile', 'section')
The draws below stay inside these ranges and needn't reach their ends.
All inputs are finite; a program needn't handle non-finite values.
Results may differ from the reference program's by a relative error of at most 0.000053.
Values sent between devices are 32-bit elements; how exact they have to be, the bound alone decides.
No kernel may reach another device: no remote copies, remote signals or barrier semaphores. Data moves between devices by JAX's collectives and lax.ppermute only.
A program may use at most 64 MiB of HBM per device.

```python
import jax
import jax.numpy as jnp
from jax import lax

FIELDS = 5
LEVELS = 2
ROWS_DEV = 24
RATIO = 3
ZONE = 5
NY = 192
NXA = 1536
NXP = 384
NXN = 1152
NEST_H = 64
N_TILE = 8


def block_levels(key, shape, shards, low, top_value):
    factor_of = 1.0
    for dim, blocks in shards:
        steps = jax.random.uniform(jax.random.fold_in(jax.random.fold_in(key, 6), dim), (blocks,), jnp.float32, low / len(shards), top_value / len(shards))
        factor_of = factor_of * jnp.repeat(jnp.exp(steps), shape[dim] // blocks).reshape((-1,) + (1,) * (len(shape) - 1 - dim))
    return factor_of


def normal_values(key, shape, scale, most, cuts=(), kind=jnp.bfloat16):
    result = jax.random.normal(key, shape, jnp.float32) * scale
    if len(cuts) > 0:
        result = block_levels(key, shape, cuts, -0.22, 0.18) * result
    return jnp.clip(result, min=-most, max=most).astype(kind)


def setup_inputs(seed: int = 0) -> dict:
    seeds = jax.random.split(jax.random.key(seed), 4)
    return {
        "state": normal_values(seeds[0], (FIELDS, LEVELS, NY, NXA), 1.0, 6.0, ((2, 8), (3, 4)), jnp.float32),
        "courant": jnp.clip(jax.random.uniform(seeds[1], (2, LEVELS, NY, NXA), jnp.float32, -0.4, 0.4) * block_levels(seeds[1], (2, LEVELS, NY, NXA), ((2, 8), (3, 4)), -0.4, 0.0), -0.4, 0.4),
        "nest_offset": jax.random.randint(seeds[2], (1,), ROWS_DEV, min(NY - NEST_H - 3, ROWS_DEV * max(N_TILE // 6 - 1, 4))).astype(jnp.int32),
    }


diffusion = 0.02
mixing = 0.05


def advance(values, courant):
    padded = jnp.pad(values, ((0, 0), (1, 1), (1, 1), (1, 1)), mode="edge")
    level_below = padded[:, :-2, 1:-1, 1:-1]
    level_above = padded[:, 2:, 1:-1, 1:-1]
    south_side = padded[:, 1:-1, :-2, 1:-1]
    north_side = padded[:, 1:-1, 2:, 1:-1]
    west_side = padded[:, 1:-1, 1:-1, :-2]
    east_side = padded[:, 1:-1, 1:-1, 2:]
    speed_y = courant[0]
    speed_x = courant[1]
    transport = (jnp.maximum(speed_y, 0.0) * (values - south_side) + jnp.minimum(speed_y, 0.0) * (north_side - values)
                 + jnp.maximum(speed_x, 0.0) * (values - west_side) + jnp.minimum(speed_x, 0.0) * (east_side - values))
    spread = south_side + north_side + west_side + east_side - 4.0 * values
    column = level_below + level_above - 2.0 * values
    return values - transport + diffusion * spread + mixing * column


def upsample(values):
    return jnp.repeat(jnp.repeat(values, RATIO, axis=2), RATIO, axis=3)


def reference(state, courant, nest_offset):
    offset = nest_offset[0]
    parent = state[:, :, :, :NXP]
    nest_field = state[:, :, :, NXP:]
    parent_new = advance(parent, courant[:, :, :, :NXP])
    nest_courant = courant[:, :, :, NXP:]
    fine_old = upsample(lax.dynamic_slice_in_dim(parent, offset, NEST_H, 2))
    fine_new = upsample(lax.dynamic_slice_in_dim(parent_new, offset, NEST_H, 2))
    row_index = jnp.arange(NY)
    col_index = jnp.arange(NXN)
    row_depth = jnp.minimum(row_index, NY - 1 - row_index)
    col_depth = jnp.minimum(col_index, NXN - 1 - col_index)
    depth = jnp.minimum(row_depth[:, None], col_depth[None, :])
    weight = (jnp.maximum(ZONE - depth, 0) / ZONE).astype(state.dtype)
    for substep in range(RATIO):
        moved = advance(nest_field, nest_courant)
        fraction = (substep + 1) / RATIO
        target = fine_old + fraction * (fine_new - fine_old)
        nest_field = moved + weight * (target - moved)
    fields = state.shape[0]
    levels = state.shape[1]
    averaged = nest_field.reshape(fields, levels, NEST_H, RATIO, NXP, RATIO).sum(axis=(3, 5)) / (RATIO * RATIO)
    parent_final = lax.dynamic_update_slice_in_dim(parent_new, averaged, offset, 2)
    return jnp.concatenate([parent_final, nest_field], axis=3)
```

```python
import functools

import jax
import jax.numpy as jnp
from jax import lax
from jax.experimental import pallas as pl
from jax.experimental.pallas import tpu as pltpu
from jax.sharding import PartitionSpec as P

RATIO = 3
ZONE = 5


diffusion = 0.02
mixing = 0.05


def shifted(value, axis, steps):
    count = lax.axis_size(axis)
    leading, last = (max(0, -steps), min(count, count - steps))
    return lax.ppermute(value, axis, [(source, source + steps) for source in range(leading, last)])


def with_halo(block, sides, width):
    for axis, dim in sides:
        count = lax.axis_size(axis)
        forward = [(i, i + 1) for i in range(count - 1)]
        backward = [(target, source) for source, target in forward]
        low = lax.ppermute(
            lax.slice_in_dim(block, block.shape[dim] - width, None, axis=dim), axis, forward
        )
        high = lax.ppermute(lax.slice_in_dim(block, 0, width, axis=dim), axis, backward)
        block = jnp.concatenate([low, block, high], axis=dim)
    return block


def advance(values, courant, padded, low_row, high_row, low_col, high_col):
    row_count = values.shape[2]
    col_count = values.shape[3]
    row_index = lax.broadcasted_iota(jnp.int32, (1, 1, row_count, col_count), 2)
    column_index = lax.broadcasted_iota(jnp.int32, (1, 1, row_count, col_count), 3)
    south_side = jnp.where(low_row & (row_index == 0), values, padded[:, :, :-2, 1:-1])
    north_side = jnp.where(high_row & (row_index == row_count - 1), values, padded[:, :, 2:, 1:-1])
    west_side = jnp.where(low_col & (column_index == 0), values, padded[:, :, 1:-1, :-2])
    east_side = jnp.where(
        high_col & (column_index == col_count - 1), values, padded[:, :, 1:-1, 2:]
    )
    stacked = jnp.pad(values, ((0, 0), (1, 1), (0, 0), (0, 0)), mode="edge")
    level_below = stacked[:, :-2]
    level_above = stacked[:, 2:]
    speed_y = courant[0]
    speed_x = courant[1]
    transport = (
        jnp.maximum(speed_y, 0.0) * (values - south_side)
        + jnp.minimum(speed_y, 0.0) * (north_side - values)
        + jnp.maximum(speed_x, 0.0) * (values - west_side)
        + jnp.minimum(speed_x, 0.0) * (east_side - values)
    )
    spread = south_side + north_side + west_side + east_side - 4.0 * values
    column = level_below + level_above - 2.0 * values
    return values - transport + diffusion * spread + mixing * column


def send_rims(values, distance):
    return shifted(values, "section", distance)


def general_on_device(state, courant, nest_offset):
    fields, levels, row_count, col_count = state.shape
    tile_count = lax.axis_size("tile")
    section_count = lax.axis_size("section")
    parent_count = section_count // 4
    tile_index = lax.axis_index("tile")
    section = lax.axis_index("section")
    offset = nest_offset[0]
    total_rows = row_count * tile_count
    nest_height = total_rows // RATIO
    third_width = col_count // RATIO
    coarse_rows = row_count // RATIO
    parent_width = parent_count * col_count
    nest_width = section_count * col_count - parent_width
    is_parent = section < parent_count
    low_row = tile_index == 0
    high_row = tile_index == tile_count - 1
    low_col = (section == 0) | (section == parent_count)
    high_col = (section == parent_count - 1) | (section == section_count - 1)

    def step(values):
        padded = with_halo(values, (("tile", 2), ("section", 3)), 1)
        return advance(values, courant, padded, low_row, high_row, low_col, high_col)

    stepped = step(state)
    local_rows = tile_index * row_count + jnp.arange(row_count, dtype=jnp.int32)
    rim_coarse = jnp.array([0, 1, nest_height - 2, nest_height - 1], dtype=jnp.int32)
    wanted = offset + rim_coarse
    pick_rows = (wanted[:, None] == local_rows[None, :]).astype(jnp.float32)
    parent_flag = is_parent.astype(jnp.float32)
    both_states = jnp.stack([state, stepped]) * parent_flag
    rim_part = jnp.einsum(
        "jr,tflrc->tfljc", pick_rows, both_states, precision=lax.Precision.HIGHEST
    )
    edge_cols = jnp.array([0, 1, parent_width - 2, parent_width - 1], dtype=jnp.int32)
    global_cols = section * col_count + jnp.arange(col_count, dtype=jnp.int32)
    pick_edge = (global_cols[:, None] == edge_cols[None, :]).astype(jnp.float32)
    edge_local = jnp.einsum(
        "tflrc,ck->tflrk", both_states, pick_edge, precision=lax.Precision.HIGHEST
    )
    span_rows = offset + jnp.arange(nest_height, dtype=jnp.int32)
    pick_span = (span_rows[:, None] == local_rows[None, :]).astype(jnp.float32)
    edge_part = jnp.einsum(
        "nr,tflrk->tflnk", pick_span, edge_local, precision=lax.Precision.HIGHEST
    )
    packed = jnp.concatenate(
        [
            rim_part.reshape(2 * fields * levels, 4 * col_count),
            edge_part.reshape(2 * fields * levels, nest_height * 4),
        ],
        axis=1,
    )
    summed = lax.psum(packed, "tile")
    nest_index = jnp.maximum(section - parent_count, 0)
    source_parent = nest_index // RATIO
    received = jnp.zeros_like(summed)
    for distance in range(parent_count, 3 * parent_count + 1):
        arrived = send_rims(summed, distance)
        hit = jnp.logical_not(is_parent) & (section - distance == source_parent)
        received = jnp.where(hit, arrived, received)
    rim_rows = received[:, : 4 * col_count].reshape(2, fields, levels, 4, col_count)
    edges = received[:, 4 * col_count :].reshape(2, fields, levels, nest_height, 4)
    rim_strip = lax.dynamic_slice_in_dim(rim_rows, nest_index % RATIO * third_width, third_width, 4)
    rim_strip = jnp.repeat(rim_strip, RATIO, axis=4)
    row_choice = ((local_rows // RATIO)[:, None] == rim_coarse[None, :]).astype(jnp.float32)
    forcing_rows = jnp.einsum(
        "rj,tfljc->tflrc", row_choice, rim_strip, precision=lax.Precision.HIGHEST
    )
    nest_cols = nest_index * col_count + jnp.arange(col_count, dtype=jnp.int32)
    col_choice = (edge_cols[:, None] == (nest_cols // RATIO)[None, :]).astype(jnp.float32)
    coarse_choice = (
        (local_rows // RATIO)[:, None] == jnp.arange(nest_height, dtype=jnp.int32)[None, :]
    ).astype(jnp.float32)
    edge_rows = jnp.einsum("rn,tflnk->tflrk", coarse_choice, edges, precision=lax.Precision.HIGHEST)
    forcing_cols = jnp.einsum(
        "tflrk,kc->tflrc", edge_rows, col_choice, precision=lax.Precision.HIGHEST
    )
    row_depth = jnp.minimum(local_rows, total_rows - 1 - local_rows)
    col_depth = jnp.minimum(nest_cols, nest_width - 1 - nest_cols)
    row_zone = (row_depth < ZONE)[:, None]
    forcing = jnp.where(row_zone, forcing_rows, forcing_cols)
    depth = jnp.minimum(row_depth[:, None], col_depth[None, :])
    weight = jnp.maximum(ZONE - depth, 0).astype(jnp.float32) / ZONE

    def relax(values, substep):
        fraction = (substep + 1) / RATIO
        target = forcing[0] + fraction * (forcing[1] - forcing[0])
        return values + weight * (target - values)

    nest_field = relax(stepped, 0)
    for substep in range(1, RATIO):
        nest_field = relax(step(nest_field), substep)
    block_means = nest_field.reshape(fields, levels, coarse_rows, RATIO, third_width, RATIO).sum(
        axis=(3, 5)
    ) / (RATIO * RATIO)
    wanted_nest = local_rows - offset
    portion = lax.all_gather(block_means, "tile", axis=2, tiled=True)
    row_span = portion.shape[2]
    select = (wanted_nest[:, None] == jnp.arange(row_span, dtype=jnp.int32)[None, :]).astype(
        jnp.float32
    )
    gathered = jnp.einsum("rs,flsc->flrc", select, portion, precision=lax.Precision.HIGHEST)
    target_slot = jnp.where(is_parent, -1, (section - parent_count) // RATIO)
    slot_index = jnp.arange(section_count, dtype=jnp.int32)
    outbound = jnp.where(
        (slot_index == target_slot)[None, None, None, :, None], gathered[:, :, :, None, :], 0.0
    )
    outbound = outbound.reshape(fields, levels, row_count, section_count * third_width)
    received_means = lax.all_to_all(outbound, "section", split_axis=3, concat_axis=3, tiled=True)
    start_col = (parent_count + RATIO * jnp.minimum(section, parent_count - 1)) * third_width
    feedback = lax.dynamic_slice_in_dim(received_means, start_col, col_count, 3)
    covered = ((wanted_nest >= 0) & (wanted_nest < nest_height))[:, None]
    parent_final = jnp.where(covered, feedback, stepped)
    return jnp.where(is_parent, parent_final, nest_field)


ROWS = 24
COLS = 384
LANE = 128
STATES = 10
PLANES = 14
SLOTS = 4 * PLANES
NEST_MARK = 1.0
PARENT_MARK = 2.0
EXACT = lax.Precision.HIGHEST


def device(tile, section):
    return tile * 4 + section


def third(value):
    return (value * 43) >> 7


def iota(shape, dim):
    return lax.broadcasted_iota(jnp.int32, shape, dim)


def dot(a, b):
    return jnp.dot(a, b, precision=EXACT, preferred_element_type=jnp.float32)


def turn(value, steps, dim):
    size = value.shape[dim]
    steps = steps % size
    return pltpu.roll(value, steps, dim) if steps else value


def plane_of(state_ref, courant_ref, p):
    return state_ref[p] if p < STATES else courant_ref[p - STATES]


def pack_kernel(offset_ref, state_ref, courant_ref, west_ref, middle_ref, east_ref):
    tile = lax.axis_index("tile")
    section = lax.axis_index("section")
    offset = offset_ref[0]
    first = tile * ROWS
    lane = iota((ROWS, LANE), 1)
    left = jnp.zeros((ROWS, LANE), jnp.float32)
    right = jnp.zeros((ROWS, LANE), jnp.float32)
    for p in range(PLANES):
        source = plane_of(state_ref, courant_ref, p)
        mine = (lane >= 3 * p) & (lane < 3 * p + 3)
        left = jnp.where(mine, turn(source[:, :LANE], 3 * p, 1), left)
        right = jnp.where(mine, turn(source[:, COLS - LANE :], 3 * p - (LANE - 3), 1), right)
    top = (first <= offset + 2) & (first + ROWS - 1 >= offset - 1)
    base = jnp.where(top, offset - 1, offset + 61) - first

    def chosen(start, count):
        slot = iota((4 * count, ROWS * count), 0)
        column = iota((4 * count, ROWS * count), 1)
        local = base + (slot & 3)
        hit = (local >= 0) & (local < ROWS) & (column == (slot >> 2) * ROWS + local)
        return hit.astype(jnp.float32)

    rows = jnp.concatenate(
        [
            dot(chosen(0, STATES), state_ref[...].reshape(STATES * ROWS, COLS)),
            dot(chosen(0, 4), courant_ref[...].reshape(4 * ROWS, COLS)),
        ],
        axis=0,
    )
    lane = iota((SLOTS, LANE), 1)
    mark = jnp.where(section == 0, PARENT_MARK, NEST_MARK)
    blank = jnp.zeros((SLOTS, LANE), jnp.float32)
    outs = ((west_ref, left), (middle_ref, left), (east_ref, right))
    for s, (out_ref, edge) in enumerate(outs):
        before = rows[:, LANE * (s - 1) : LANE * s] if s > 0 else blank
        after = rows[:, LANE * (s + 1) : LANE * (s + 2)] if s < 2 else blank
        extra = turn(jnp.where(lane < 2, after, before), 44, 1)
        side = jnp.where(
            (lane >= 42) & (lane < 46), extra, jnp.where(lane == LANE - 1, mark, 0.0)
        )
        out_ref[:, :LANE] = rows[:, LANE * s : LANE * (s + 1)]
        out_ref[:ROWS, LANE:] = jnp.where(lane[:ROWS] < 42, edge, side[:ROWS])
        out_ref[ROWS:, LANE:] = side[ROWS:]


def relay_kernel(*refs):
    state_ref, courant_ref = refs[:2]
    to_west, to_middle, to_east = refs[2:5], refs[5:6], refs[6:9]
    west_ref, east_ref, rims_ref, pair_ref, cross_ref = refs[9:]
    even = lax.axis_index("tile") % 2 == 0

    def marked(sources, mark):
        total = None
        for ref in sources:
            value = ref[...]
            value = jnp.where(value[:, 2 * LANE - 1 :] == mark, value, 0.0)
            total = value if total is None else total + value
        return total

    east = marked(to_west, NEST_MARK)[:ROWS, LANE:]
    west = marked(to_east, NEST_MARK)[:ROWS, LANE:]
    rims = marked(to_west + to_middle + to_east, PARENT_MARK)
    west_ref[...] = west
    east_ref[...] = east
    rims_ref[...] = rims

    def put(rows, lanes, value):
        head, tail = value[:4], value[ROWS - 4 :]
        pair_ref[rows, lanes] = jnp.where(even, tail, head)
        cross_ref[rows, lanes] = jnp.where(even, head, tail)

    for p in range(PLANES):
        put(slice(4 * p, 4 * p + 4), slice(None), plane_of(state_ref, courant_ref, p))
    put(slice(SLOTS, SLOTS + 4), slice(0, LANE), west)
    put(slice(SLOTS, SLOTS + 4), slice(LANE, 2 * LANE), east)
    pair_ref[SLOTS + 8 :, : 2 * LANE] = rims


def flux(value, south, north, west, east, other, cy, cx):
    transport = (
        jnp.maximum(cy, 0.0) * (value - south)
        + jnp.minimum(cy, 0.0) * (north - value)
        + jnp.maximum(cx, 0.0) * (value - west)
        + jnp.minimum(cx, 0.0) * (east - value)
    )
    spread = south + north + west + east - 4.0 * value
    return diffusion * spread + mixing * (other - value) - transport


def main_kernel(
    offset_ref,
    state_ref,
    courant_ref,
    west_ref,
    east_ref,
    rims_ref,
    pair_ref,
    cross_ref,
    out_ref,
    means_ref,
    here,
    there,
    factors,
    base_force,
    step_force,
    narrowed,
):
    tile = lax.axis_index("tile")
    section = lax.axis_index("section")
    offset = offset_ref[0]
    even = tile % 2 == 0
    is_nest = section > 0
    full = (32, 4 * LANE)

    after = jnp.where(even, pair_ref[: SLOTS + 8], cross_ref[...])
    before = jnp.where(even, cross_ref[...], pair_ref[: SLOTS + 8])
    wests = jnp.concatenate(
        [west_ref[...], after[SLOTS : SLOTS + 4, :LANE], before[SLOTS : SLOTS + 4, :LANE]], axis=0
    )
    easts = jnp.concatenate(
        [
            east_ref[...],
            after[SLOTS : SLOTS + 4, LANE : 2 * LANE],
            before[SLOTS : SLOTS + 4, LANE : 2 * LANE],
        ],
        axis=0,
    )
    lane = iota((32, LANE), 1)

    def ring(p):
        tail = jnp.concatenate([after[4 * p : 4 * p + 4], before[4 * p : 4 * p + 4]], axis=0)
        cells = jnp.concatenate([plane_of(state_ref, courant_ref, p), tail], axis=0)
        outside = jnp.where(
            lane < 3,
            turn(easts, -3 * p, 1),
            jnp.where(lane >= LANE - 3, turn(wests, LANE - 3 - 3 * p, 1), 0.0),
        )
        return jnp.concatenate([cells, outside], axis=1)

    for p in range(STATES):
        here[p] = ring(p)

    row = iota(full, 0)
    column = iota(full, 1)
    near_row = jnp.where(row < 28, row, row - 32)
    near_column = jnp.where(column < 448, column, column - 512)
    grid_row = near_row + tile * ROWS
    grid_column = near_column + (section - 1) * COLS
    row_depth = jnp.minimum(grid_row, 8 * ROWS - 1 - grid_row)
    column_depth = jnp.minimum(grid_column, 3 * COLS - 1 - grid_column)
    depth = jnp.maximum(jnp.minimum(row_depth, column_depth), 0)
    weight = jnp.maximum(ZONE - depth, 0).astype(jnp.float32) / ZONE
    weight = jnp.where(is_nest, weight, 0.0)
    keep = 1.0 - weight
    no_south = row == jnp.where(tile == 0, 0, -1)
    no_north = row == jnp.where(tile == 7, ROWS - 1, -1)
    no_west = column == jnp.where(section < 2, 0, -1)
    no_east = column == jnp.where((section == 0) | (section == 3), COLS - 1, -1)
    for level in range(2):
        cy = ring(STATES + level)
        cx = ring(STATES + 2 + level)
        from_south = jnp.maximum(cy, 0.0) + diffusion
        from_north = diffusion - jnp.minimum(cy, 0.0)
        from_west = jnp.maximum(cx, 0.0) + diffusion
        from_east = diffusion - jnp.minimum(cx, 0.0)
        from_south = jnp.where(no_south, 0.0, from_south)
        from_north = jnp.where(no_north, 0.0, from_north)
        from_west = jnp.where(no_west, 0.0, from_west)
        from_east = jnp.where(no_east, 0.0, from_east)
        own = (1.0 - mixing) - (from_south + from_north + from_west + from_east)
        factors[level, 0] = own * keep
        factors[level, 1] = from_south * keep
        factors[level, 2] = from_north * keep
        factors[level, 3] = from_west * keep
        factors[level, 4] = from_east * keep
    factors[0, 5] = mixing * keep

    base_force[...] = jnp.zeros(base_force.shape, jnp.float32)
    step_force[...] = jnp.zeros(step_force.shape, jnp.float32)
    other_rims = pair_ref[SLOTS + 8 :, : 2 * LANE]
    lower = jnp.where(even, rims_ref[...], other_rims)
    upper = jnp.where(even, other_rims, rims_ref[...])

    @pl.when((section == 1) | (section == 3))
    def _():
        on_left = section == 1
        edges = jnp.concatenate([lower[:ROWS, LANE:], upper[:ROWS, LANE:]], axis=0)
        source_tile = ((offset - 2) // 8 + (tile // 2) * 2) // 3
        pick = iota((96, 2 * ROWS), 0)
        part = pick >> 5
        near = pick & 31
        near = jnp.where(near < 28, near, near - 32)
        coarse = offset + tile * 8 + third(near + 6) - 2 + part - 1 - source_tile * ROWS
        picked = dot((iota((96, 2 * ROWS), 1) == coarse).astype(jnp.float32), edges)
        south, value, north = picked[:32], picked[32:64], picked[64:]
        place = lane - 3 * third(lane)
        west = jnp.where(place == jnp.where(on_left, 0, -1), value, turn(value, 1, 1))
        east = jnp.where(place == jnp.where(on_left, -1, 2), value, turn(value, -1, 1))
        other = jnp.where((third(lane) & 1) == 0, turn(value, -3, 1), turn(value, 3, 1))
        cy = jnp.zeros((32, LANE), jnp.float32)
        cx = jnp.zeros((32, LANE), jnp.float32)
        for field in range(STATES // 2):
            mine = (lane >= 6 * field) & (lane < 6 * field + 6)
            cy = jnp.where(mine, turn(value, 6 * field - 3 * STATES, 1), cy)
            cx = jnp.where(mine, turn(value, 6 * field - 3 * STATES - 6, 1), cx)
        change = flux(value, south, north, west, east, other, cy, cx) / RATIO
        out = iota((LANE, STATES * LANE), 1)
        spot = out & (LANE - 1)
        wanted = 3 * (out >> 7) + jnp.where(on_left, third(spot), third(spot - 119))
        start = jnp.where(on_left, 0, LANE - 6)
        valid = (spot >= start) & (spot < start + 6)
        spread = (valid & (iota((LANE, STATES * LANE), 0) == wanted)).astype(jnp.float32)
        forced = dot(jnp.concatenate([value, change], axis=0), spread)

        def place_side(lanes):
            for p in range(STATES):
                block = forced[:, p * LANE : (p + 1) * LANE]
                base_force[p, :, lanes] = weight[:, lanes] * block[:32]
                step_force[p, :, lanes] = weight[:, lanes] * block[32:]

        @pl.when(on_left)
        def _():
            place_side(slice(0, LANE))

        @pl.when(jnp.logical_not(on_left))
        def _():
            place_side(slice(2 * LANE, 3 * LANE))

    @pl.when(is_nest & ((tile == 0) | (tile == 7)))
    def _():
        rows = lower + upper
        wide = iota((8, 2 * LANE), 1)
        narrow = iota((SLOTS, LANE), 1)
        outside = turn(rows[:, LANE:], 84, 1)
        outside = jnp.where((narrow < 2) | (narrow >= LANE - 2), outside, 0.0)
        rows = jnp.concatenate([rows[:, :LANE], outside], axis=1)
        cy = rows[4 * STATES : 4 * STATES + 8]
        cx = rows[4 * STATES + 8 :]
        changes = []
        for field in range(STATES // 2):
            value = rows[8 * field : 8 * field + 8]
            west = jnp.where(wide == jnp.where(section == 1, 0, -1), value, turn(value, 1, 1))
            east = jnp.where(wide == jnp.where(section == 3, LANE - 1, -1), value, turn(value, -1, 1))
            changes.append(
                flux(
                    value,
                    turn(value, 1, 0),
                    turn(value, -1, 0),
                    west,
                    east,
                    turn(value, 4, 0),
                    cy,
                    cx,
                )
                / RATIO
            )
        both = jnp.concatenate([rows[: 4 * STATES]] + changes, axis=0)
        target = iota((2 * LANE, 4 * LANE), 1)
        target = jnp.where(target < 448, target, target - 512)
        coarse = (((target + 66) * 171) >> 9) - 22
        spread = (iota((2 * LANE, 4 * LANE), 0) == (coarse & (2 * LANE - 1))).astype(jnp.float32)
        forced = dot(both, spread)
        eight = iota((8, 4 * LANE), 0)

        def place_rows(rows, split):
            zone = jnp.where(split == 3, eight < ZONE, eight >= 8 - ZONE)
            for p in range(STATES):
                for ref, start in ((base_force, 0), (step_force, 4 * STATES)):
                    spot = start + 4 * p
                    value = jnp.where(eight < split, forced[spot + 1 : spot + 2], forced[spot + 2 : spot + 3])
                    ref[p, rows, :] = jnp.where(zone, weight[rows] * value, ref[p, rows, :])

        @pl.when(tile == 0)
        def _():
            place_rows(slice(0, 8), 3)

        @pl.when(tile == 7)
        def _():
            place_rows(slice(16, 24), 5)

    def substep(source, target, number):
        def per_field(field, carry):
            values = [source[2 * field + level] for level in range(2)]
            for level in range(2):
                value = values[level]
                result = factors[level, 0] * value + factors[0, 5] * values[1 - level]
                result += factors[level, 1] * turn(value, 1, 0)
                result += factors[level, 2] * turn(value, -1, 0)
                result += factors[level, 3] * turn(value, 1, 1)
                result += factors[level, 4] * turn(value, -1, 1)
                p = 2 * field + level
                result += base_force[p] + float(number) * step_force[p]
                target[p] = result
            return carry

        lax.fori_loop(0, STATES // 2, per_field, 0)

    substep(here, there, 1)

    @pl.when(is_nest)
    def _():
        substep(there, here, 2)
        substep(here, there, 3)

    out_ref[...] = there[:, :ROWS, :COLS]
    columns = iota((COLS, LANE), 1) * RATIO
    source = iota((COLS, LANE), 0)
    gather = ((source >= columns) & (source < columns + RATIO)).astype(jnp.float32)
    narrowed[...] = dot(out_ref[...].reshape(STATES * ROWS, COLS), gather)
    total = sum(narrowed[pl.ds(i, STATES * 8, stride=RATIO), :] for i in range(RATIO))
    means_ref[...] = total / (RATIO * RATIO)


def merge_kernel(offset_ref, first_ref, second_ref, third_ref, fourth_ref, block_ref, out_ref):
    tile = lax.axis_index("tile")
    section = lax.axis_index("section")
    offset = offset_ref[0]
    rest = offset % 8

    @pl.when(section > 0)
    def _():
        out_ref[...] = block_ref[...]

    @pl.when(section == 0)
    def _():
        nest_row = tile * ROWS + iota((ROWS, COLS), 0) - offset
        covered = (nest_row >= 0) & (nest_row < 64)
        for p in range(STATES):
            parts = [r[8 * p : 8 * p + 8] for r in (first_ref, second_ref, third_ref, fourth_ref)]
            moved = pltpu.roll(jnp.concatenate(parts, axis=0), rest + 24, 0)
            out_ref[p] = jnp.where(covered, moved[:ROWS], block_ref[p])


VMEM = pl.BlockSpec(memory_space=pltpu.VMEM)
SMEM = pl.BlockSpec(memory_space=pltpu.SMEM)


def shaped(*shape):
    return jax.ShapeDtypeStruct(shape, jnp.float32)


def rim_pairs(start):
    groups = []
    for section, inner in ((1, ((2, 1), (3, 2))), (3, ((1, 2), (2, 3)))):
        lists = [[], [], []]
        sent = {}
        taken = {}
        for chip in range(4):
            source = (start + 2 * chip) // 3
            for core in range(2):
                color = sent.get(source + core, 0)
                sent[source + core] = color + 1
                taken[2 * chip + core] = color
                lists[color].append((device(source + core, 0), device(2 * chip + core, section)))
        for tile in range(8):
            for origin, target in inner:
                color = (taken[tile] + 1) % 3 if target == section else taken[tile]
                lists[color].append((device(tile, origin), device(tile, target)))
        groups.append(lists)
    middle = []
    for chip in (0, 3):
        source = (start + 2 * chip) // 3
        middle += [(device(source + core, 0), device(2 * chip + core, 2)) for core in range(2)]
    return groups[0], [middle], groups[1]


def mean_pairs(start):
    lists = []
    for step in range(4):
        pairs = []
        for tile in range(8):
            source = 3 * tile - start - 1 + step
            if 0 <= source < 8:
                pairs.append((device(source, 0), device(tile, 0)))
        lists.append(pairs)
    return lists


BOTH = ("tile", "section")


def on_device(state, courant, nest_offset):
    planes = state.reshape(STATES, ROWS, COLS)
    speeds = courant.reshape(4, ROWS, COLS)
    offset = nest_offset[0]
    payloads = pl.pallas_call(
        pack_kernel,
        out_shape=[shaped(SLOTS, 2 * LANE)] * 3,
        in_specs=[SMEM, VMEM, VMEM],
        out_specs=[VMEM] * 3,
        name="pack",
    )(nest_offset, planes, speeds)

    def send_rims(start, west, middle, east):
        groups = rim_pairs(start)
        return tuple(
            lax.ppermute(value, BOTH, pairs)
            for value, lists in zip((west, middle, east), groups)
            for pairs in lists
        )

    received = lax.switch(
        (offset - 2) // 8 - 2,
        [functools.partial(send_rims, start) for start in range(2, 12)],
        *payloads,
    )
    west, east, rims, to_pair, to_cross = pl.pallas_call(
        relay_kernel,
        out_shape=[
            shaped(ROWS, LANE),
            shaped(ROWS, LANE),
            shaped(SLOTS, 2 * LANE),
            shaped(2 * SLOTS + 8, COLS),
            shaped(SLOTS + 8, COLS),
        ],
        in_specs=[VMEM] * 9,
        out_specs=[VMEM] * 5,
        name="relay",
    )(planes, speeds, *received)
    pair_map = [(device(t, s), device(t ^ 1, s)) for t in range(8) for s in range(4)]
    cross_map = [
        (device(a, s), device(b, s))
        for low in (1, 3, 5)
        for a, b in ((low, low + 1), (low + 1, low))
        for s in range(4)
    ]
    from_cross = lax.ppermute(to_cross, BOTH, cross_map)
    from_pair = lax.ppermute(to_pair, BOTH, pair_map)
    block, means = pl.pallas_call(
        main_kernel,
        out_shape=[shaped(STATES, ROWS, COLS), shaped(STATES * 8, LANE)],
        in_specs=[SMEM] + [VMEM] * 7,
        out_specs=[VMEM] * 2,
        scratch_shapes=[
            pltpu.VMEM((STATES, 32, 4 * LANE), jnp.float32),
            pltpu.VMEM((STATES, 32, 4 * LANE), jnp.float32),
            pltpu.VMEM((2, 6, 32, 4 * LANE), jnp.float32),
            pltpu.VMEM((STATES, 32, 4 * LANE), jnp.float32),
            pltpu.VMEM((STATES, 32, 4 * LANE), jnp.float32),
            pltpu.VMEM((STATES * ROWS, LANE), jnp.float32),
        ],
        compiler_params=pltpu.CompilerParams(vmem_limit_bytes=32 * 1024 * 1024),
        name="nest",
    )(nest_offset, planes, speeds, west, east, rims, from_pair, from_cross)
    columns = jnp.concatenate(
        [
            lax.ppermute(means, BOTH, [(device(t, s), device(t, 0)) for t in range(8)])
            for s in (1, 2, 3)
        ],
        axis=1,
    )

    def send_means(start, value):
        return tuple(lax.ppermute(value, BOTH, pairs) for pairs in mean_pairs(start))

    blocks = lax.switch(
        offset // 8 - 3,
        [functools.partial(send_means, start) for start in range(3, 12)],
        columns,
    )
    merged = pl.pallas_call(
        merge_kernel,
        out_shape=shaped(STATES, ROWS, COLS),
        in_specs=[SMEM] + [VMEM] * 5,
        out_specs=VMEM,
        compiler_params=pltpu.CompilerParams(vmem_limit_bytes=32 * 1024 * 1024),
        name="merge",
    )(nest_offset, *blocks, block)
    return merged.reshape(state.shape)


def solution(mesh):
    small = mesh.shape["tile"] == 8 and mesh.shape["section"] == 4
    return jax.shard_map(
        on_device if small else general_on_device,
        mesh=mesh,
        in_specs=(P(None, None, "tile", "section"), P(None, None, "tile", "section"), P()),
        out_specs=P(None, None, "tile", "section"),
        check_vma=False,
    )
```

```python
import functools

import jax
import jax.numpy as jnp
from jax import lax
from jax.experimental import pallas as pl
from jax.experimental.pallas import tpu as pltpu
from jax.sharding import PartitionSpec as P

RATIO = 3
ZONE = 5


diffusion = 0.02
mixing = 0.05


def shifted(value, axis, steps):
    count = lax.axis_size(axis)
    leading, last = (max(0, -steps), min(count, count - steps))
    return lax.ppermute(value, axis, [(source, source + steps) for source in range(leading, last)])


def with_halo(block, sides, width):
    for axis, dim in sides:
        count = lax.axis_size(axis)
        forward = [(i, i + 1) for i in range(count - 1)]
        backward = [(target, source) for source, target in forward]
        low = lax.ppermute(
            lax.slice_in_dim(block, block.shape[dim] - width, None, axis=dim), axis, forward
        )
        high = lax.ppermute(lax.slice_in_dim(block, 0, width, axis=dim), axis, backward)
        block = jnp.concatenate([low, block, high], axis=dim)
    return block


def advance(values, courant, padded, low_row, high_row, low_col, high_col):
    row_count = values.shape[2]
    col_count = values.shape[3]
    row_index = lax.broadcasted_iota(jnp.int32, (1, 1, row_count, col_count), 2)
    column_index = lax.broadcasted_iota(jnp.int32, (1, 1, row_count, col_count), 3)
    south_side = jnp.where(low_row & (row_index == 0), values, padded[:, :, :-2, 1:-1])
    north_side = jnp.where(high_row & (row_index == row_count - 1), values, padded[:, :, 2:, 1:-1])
    west_side = jnp.where(low_col & (column_index == 0), values, padded[:, :, 1:-1, :-2])
    east_side = jnp.where(
        high_col & (column_index == col_count - 1), values, padded[:, :, 1:-1, 2:]
    )
    stacked = jnp.pad(values, ((0, 0), (1, 1), (0, 0), (0, 0)), mode="edge")
    level_below = stacked[:, :-2]
    level_above = stacked[:, 2:]
    speed_y = courant[0]
    speed_x = courant[1]
    transport = (
        jnp.maximum(speed_y, 0.0) * (values - south_side)
        + jnp.minimum(speed_y, 0.0) * (north_side - values)
        + jnp.maximum(speed_x, 0.0) * (values - west_side)
        + jnp.minimum(speed_x, 0.0) * (east_side - values)
    )
    spread = south_side + north_side + west_side + east_side - 4.0 * values
    column = level_below + level_above - 2.0 * values
    return values - transport + diffusion * spread + mixing * column


def send_rims(values, distance):
    return shifted(values, "section", distance)


def general_on_device(state, courant, nest_offset):
    fields, levels, row_count, col_count = state.shape
    tile_count = lax.axis_size("tile")
    section_count = lax.axis_size("section")
    parent_count = section_count // 4
    tile_index = lax.axis_index("tile")
    section = lax.axis_index("section")
    offset = nest_offset[0]
    total_rows = row_count * tile_count
    nest_height = total_rows // RATIO
    third_width = col_count // RATIO
    coarse_rows = row_count // RATIO
    parent_width = parent_count * col_count
    nest_width = section_count * col_count - parent_width
    is_parent = section < parent_count
    low_row = tile_index == 0
    high_row = tile_index == tile_count - 1
    low_col = (section == 0) | (section == parent_count)
    high_col = (section == parent_count - 1) | (section == section_count - 1)

    def step(values):
        padded = with_halo(values, (("tile", 2), ("section", 3)), 1)
        return advance(values, courant, padded, low_row, high_row, low_col, high_col)

    stepped = step(state)
    local_rows = tile_index * row_count + jnp.arange(row_count, dtype=jnp.int32)
    rim_coarse = jnp.array([0, 1, nest_height - 2, nest_height - 1], dtype=jnp.int32)
    wanted = offset + rim_coarse
    pick_rows = (wanted[:, None] == local_rows[None, :]).astype(jnp.float32)
    parent_flag = is_parent.astype(jnp.float32)
    both_states = jnp.stack([state, stepped]) * parent_flag
    rim_part = jnp.einsum(
        "jr,tflrc->tfljc", pick_rows, both_states, precision=lax.Precision.HIGHEST
    )
    edge_cols = jnp.array([0, 1, parent_width - 2, parent_width - 1], dtype=jnp.int32)
    global_cols = section * col_count + jnp.arange(col_count, dtype=jnp.int32)
    pick_edge = (global_cols[:, None] == edge_cols[None, :]).astype(jnp.float32)
    edge_local = jnp.einsum(
        "tflrc,ck->tflrk", both_states, pick_edge, precision=lax.Precision.HIGHEST
    )
    span_rows = offset + jnp.arange(nest_height, dtype=jnp.int32)
    pick_span = (span_rows[:, None] == local_rows[None, :]).astype(jnp.float32)
    edge_part = jnp.einsum(
        "nr,tflrk->tflnk", pick_span, edge_local, precision=lax.Precision.HIGHEST
    )
    packed = jnp.concatenate(
        [
            rim_part.reshape(2 * fields * levels, 4 * col_count),
            edge_part.reshape(2 * fields * levels, nest_height * 4),
        ],
        axis=1,
    )
    summed = lax.psum(packed, "tile")
    nest_index = jnp.maximum(section - parent_count, 0)
    source_parent = nest_index // RATIO
    received = jnp.zeros_like(summed)
    for distance in range(parent_count, 3 * parent_count + 1):
        arrived = send_rims(summed, distance)
        hit = jnp.logical_not(is_parent) & (section - distance == source_parent)
        received = jnp.where(hit, arrived, received)
    rim_rows = received[:, : 4 * col_count].reshape(2, fields, levels, 4, col_count)
    edges = received[:, 4 * col_count :].reshape(2, fields, levels, nest_height, 4)
    rim_strip = lax.dynamic_slice_in_dim(rim_rows, nest_index % RATIO * third_width, third_width, 4)
    rim_strip = jnp.repeat(rim_strip, RATIO, axis=4)
    row_choice = ((local_rows // RATIO)[:, None] == rim_coarse[None, :]).astype(jnp.float32)
    forcing_rows = jnp.einsum(
        "rj,tfljc->tflrc", row_choice, rim_strip, precision=lax.Precision.HIGHEST
    )
    nest_cols = nest_index * col_count + jnp.arange(col_count, dtype=jnp.int32)
    col_choice = (edge_cols[:, None] == (nest_cols // RATIO)[None, :]).astype(jnp.float32)
    coarse_choice = (
        (local_rows // RATIO)[:, None] == jnp.arange(nest_height, dtype=jnp.int32)[None, :]
    ).astype(jnp.float32)
    edge_rows = jnp.einsum("rn,tflnk->tflrk", coarse_choice, edges, precision=lax.Precision.HIGHEST)
    forcing_cols = jnp.einsum(
        "tflrk,kc->tflrc", edge_rows, col_choice, precision=lax.Precision.HIGHEST
    )
    row_depth = jnp.minimum(local_rows, total_rows - 1 - local_rows)
    col_depth = jnp.minimum(nest_cols, nest_width - 1 - nest_cols)
    row_zone = (row_depth < ZONE)[:, None]
    forcing = jnp.where(row_zone, forcing_rows, forcing_cols)
    depth = jnp.minimum(row_depth[:, None], col_depth[None, :])
    weight = jnp.maximum(ZONE - depth, 0).astype(jnp.float32) / ZONE

    def relax(values, substep):
        fraction = (substep + 1) / RATIO
        target = forcing[0] + fraction * (forcing[1] - forcing[0])
        return values + weight * (target - values)

    nest_field = relax(stepped, 0)
    for substep in range(1, RATIO):
        nest_field = relax(step(nest_field), substep)
    block_means = nest_field.reshape(fields, levels, coarse_rows, RATIO, third_width, RATIO).sum(
        axis=(3, 5)
    ) / (RATIO * RATIO)
    wanted_nest = local_rows - offset
    portion = lax.all_gather(block_means, "tile", axis=2, tiled=True)
    row_span = portion.shape[2]
    select = (wanted_nest[:, None] == jnp.arange(row_span, dtype=jnp.int32)[None, :]).astype(
        jnp.float32
    )
    gathered = jnp.einsum("rs,flsc->flrc", select, portion, precision=lax.Precision.HIGHEST)
    target_slot = jnp.where(is_parent, -1, (section - parent_count) // RATIO)
    slot_index = jnp.arange(section_count, dtype=jnp.int32)
    outbound = jnp.where(
        (slot_index == target_slot)[None, None, None, :, None], gathered[:, :, :, None, :], 0.0
    )
    outbound = outbound.reshape(fields, levels, row_count, section_count * third_width)
    received_means = lax.all_to_all(outbound, "section", split_axis=3, concat_axis=3, tiled=True)
    start_col = (parent_count + RATIO * jnp.minimum(section, parent_count - 1)) * third_width
    feedback = lax.dynamic_slice_in_dim(received_means, start_col, col_count, 3)
    covered = ((wanted_nest >= 0) & (wanted_nest < nest_height))[:, None]
    parent_final = jnp.where(covered, feedback, stepped)
    return jnp.where(is_parent, parent_final, nest_field)


ROWS = 24
COLS = 384
LANE = 128
STATES = 10
PLANES = 14
SLOTS = 4 * PLANES
HALO = SLOTS + 8
NEST_MARK = 1.0
PARENT_MARK = 2.0
RIMS = 3 * ROWS
EXACT = lax.Precision.HIGHEST


def device(tile, section):
    return tile * 4 + section


def third(value):
    return (value * 43) >> 7


def iota(shape, dim):
    return lax.broadcasted_iota(jnp.int32, shape, dim)


def dot(a, b):
    return jnp.dot(a, b, precision=EXACT, preferred_element_type=jnp.float32)


def turn(value, steps, dim):
    size = value.shape[dim]
    steps = steps % size
    return pltpu.roll(value, steps, dim) if steps else value


def plane_of(state_ref, courant_ref, p):
    return state_ref[p] if p < STATES else courant_ref[p - STATES]


def pack_kernel(offset_ref, state_ref, courant_ref, west_ref, middle_ref, east_ref):
    tile = lax.axis_index("tile")
    section = lax.axis_index("section")
    offset = offset_ref[0]
    first = tile * ROWS
    lane = iota((ROWS, LANE), 1)
    left = jnp.zeros((ROWS, LANE), jnp.float32)
    right = jnp.zeros((ROWS, LANE), jnp.float32)
    for p in range(PLANES):
        source = plane_of(state_ref, courant_ref, p)
        mine = (lane >= 3 * p) & (lane < 3 * p + 3)
        left = jnp.where(mine, turn(source[:, :LANE], 3 * p, 1), left)
        right = jnp.where(mine, turn(source[:, COLS - LANE :], 3 * p - (LANE - 3), 1), right)
    top = (first <= offset + 2) & (first + ROWS - 1 >= offset - 1)
    base = jnp.where(top, offset - 1, offset + 61) - first

    def chosen(start, count):
        slot = iota((4 * count, ROWS * count), 0)
        column = iota((4 * count, ROWS * count), 1)
        local = base + (slot & 3)
        hit = (local >= 0) & (local < ROWS) & (column == (slot >> 2) * ROWS + local)
        return hit.astype(jnp.float32)

    rows = jnp.concatenate(
        [
            dot(chosen(0, STATES), state_ref[...].reshape(STATES * ROWS, COLS)),
            dot(chosen(0, 4), courant_ref[...].reshape(4 * ROWS, COLS)),
        ],
        axis=0,
    )
    lane = iota((SLOTS, LANE), 1)
    mark = jnp.where(section == 0, PARENT_MARK + tile.astype(jnp.float32), NEST_MARK)
    blank = jnp.zeros((SLOTS, LANE), jnp.float32)
    outs = ((west_ref, left), (middle_ref, left), (east_ref, right))
    for s, (out_ref, edge) in enumerate(outs):
        before = rows[:, LANE * (s - 1) : LANE * s] if s > 0 else blank
        after = rows[:, LANE * (s + 1) : LANE * (s + 2)] if s < 2 else blank
        extra = turn(jnp.where(lane < 2, after, before), 44, 1)
        side = jnp.where(
            (lane >= 42) & (lane < 46), extra, jnp.where(lane == LANE - 1, mark, 0.0)
        )
        out_ref[:, :LANE] = rows[:, LANE * s : LANE * (s + 1)]
        out_ref[:ROWS, LANE:] = jnp.where(lane[:ROWS] < 42, edge, side[:ROWS])
        out_ref[ROWS:, LANE:] = side[ROWS:]


def first_source(offset, tile):
    return jnp.maximum((offset - 2) // ROWS, 1) - 1 + jnp.minimum(tile // 2, 2)


def relay_kernel(offset_ref, state_ref, courant_ref, *refs):
    to_west, middle, to_east = refs[:3], refs[3], refs[4:7]
    west_ref, east_ref, rims_ref, pair_ref, cross_ref = refs[7:]
    tile = lax.axis_index("tile")
    even = tile % 2 == 0
    source = first_source(offset_ref[0], tile).astype(jnp.float32) + PARENT_MARK
    lane = iota((ROWS, LANE), 1)

    def marked(sources, mark):
        total = jnp.zeros((ROWS, LANE), jnp.float32)
        for ref in sources:
            total += jnp.where(ref[:ROWS, 2 * LANE - 1 :] == mark, ref[:ROWS, LANE:], 0.0)
        return jnp.where(lane < 42, total, 0.0)

    east = marked(to_west, NEST_MARK)
    west = marked(to_east, NEST_MARK)
    west_ref[...] = west
    east_ref[...] = east
    rows = middle[...]
    for ref in to_west + to_east:
        value = ref[...]
        rows += jnp.where(value[:, 2 * LANE - 1 :] >= PARENT_MARK, value, 0.0)
    wide = iota((SLOTS, LANE), 1)
    rims_ref[:SLOTS, :LANE] = rows[:, :LANE]
    rims_ref[SLOTS:, :LANE] = jnp.zeros((RIMS - SLOTS, LANE), jnp.float32)
    extra = jnp.where((wide >= 42) & (wide < 46), rows[:, LANE:], 0.0)
    extra = jnp.concatenate([extra, jnp.zeros((RIMS - SLOTS, LANE), jnp.float32)], axis=0)
    edges = [marked(to_west + to_east, source + slot) for slot in range(3)]
    rims_ref[:, LANE:] = jnp.concatenate(edges, axis=0) + extra

    def put(rows, lanes, value):
        head, tail = value[:4], value[ROWS - 4 :]
        pair_ref[rows, lanes] = jnp.where(even, tail, head)
        cross_ref[rows, lanes] = jnp.where(even, head, tail)

    for p in range(PLANES):
        put(slice(4 * p, 4 * p + 4), slice(None), plane_of(state_ref, courant_ref, p))
    put(slice(SLOTS, SLOTS + 4), slice(0, LANE), west)
    put(slice(SLOTS, SLOTS + 4), slice(LANE, 2 * LANE), east)
    pair_ref[HALO:, : 2 * LANE] = rims_ref[...]
    cross_ref[HALO:, :LANE] = edges[0]


def flux(value, south, north, west, east, other, cy, cx):
    transport = (
        jnp.maximum(cy, 0.0) * (value - south)
        + jnp.minimum(cy, 0.0) * (north - value)
        + jnp.maximum(cx, 0.0) * (value - west)
        + jnp.minimum(cx, 0.0) * (east - value)
    )
    spread = south + north + west + east - 4.0 * value
    return diffusion * spread + mixing * (other - value) - transport


def main_kernel(
    offset_ref,
    state_ref,
    courant_ref,
    west_ref,
    east_ref,
    rims_ref,
    pair_ref,
    cross_ref,
    out_ref,
    means_ref,
    here,
    there,
    factors,
    base_force,
    step_force,
    narrowed,
):
    tile = lax.axis_index("tile")
    section = lax.axis_index("section")
    offset = offset_ref[0]
    even = tile % 2 == 0
    is_nest = section > 0
    full = (32, 4 * LANE)

    after = jnp.where(even, pair_ref[:HALO], cross_ref[:HALO])
    before = jnp.where(even, cross_ref[:HALO], pair_ref[:HALO])
    wests = jnp.concatenate(
        [west_ref[...], after[SLOTS : SLOTS + 4, :LANE], before[SLOTS : SLOTS + 4, :LANE]], axis=0
    )
    easts = jnp.concatenate(
        [
            east_ref[...],
            after[SLOTS : SLOTS + 4, LANE : 2 * LANE],
            before[SLOTS : SLOTS + 4, LANE : 2 * LANE],
        ],
        axis=0,
    )
    lane = iota((32, LANE), 1)

    def ring(p):
        tail = jnp.concatenate([after[4 * p : 4 * p + 4], before[4 * p : 4 * p + 4]], axis=0)
        cells = jnp.concatenate([plane_of(state_ref, courant_ref, p), tail], axis=0)
        outside = jnp.where(
            lane < 3,
            turn(easts, -3 * p, 1),
            jnp.where(lane >= LANE - 3, turn(wests, LANE - 3 - 3 * p, 1), 0.0),
        )
        return jnp.concatenate([cells, outside], axis=1)

    for p in range(STATES):
        here[p] = ring(p)

    row = iota(full, 0)
    column = iota(full, 1)
    near_row = jnp.where(row < 28, row, row - 32)
    near_column = jnp.where(column < 448, column, column - 512)
    grid_row = near_row + tile * ROWS
    grid_column = near_column + (section - 1) * COLS
    row_depth = jnp.minimum(grid_row, 8 * ROWS - 1 - grid_row)
    column_depth = jnp.minimum(grid_column, 3 * COLS - 1 - grid_column)
    depth = jnp.maximum(jnp.minimum(row_depth, column_depth), 0)
    weight = jnp.maximum(ZONE - depth, 0).astype(jnp.float32) / ZONE
    weight = jnp.where(is_nest, weight, 0.0)
    keep = 1.0 - weight
    no_south = row == jnp.where(tile == 0, 0, -1)
    no_north = row == jnp.where(tile == 7, ROWS - 1, -1)
    no_west = column == jnp.where(section < 2, 0, -1)
    no_east = column == jnp.where((section == 0) | (section == 3), COLS - 1, -1)
    for level in range(2):
        cy = ring(STATES + level)
        cx = ring(STATES + 2 + level)
        from_south = jnp.maximum(cy, 0.0) + diffusion
        from_north = diffusion - jnp.minimum(cy, 0.0)
        from_west = jnp.maximum(cx, 0.0) + diffusion
        from_east = diffusion - jnp.minimum(cx, 0.0)
        from_south = jnp.where(no_south, 0.0, from_south)
        from_north = jnp.where(no_north, 0.0, from_north)
        from_west = jnp.where(no_west, 0.0, from_west)
        from_east = jnp.where(no_east, 0.0, from_east)
        own = (1.0 - mixing) - (from_south + from_north + from_west + from_east)
        factors[level, 0] = own * keep
        factors[level, 1] = from_south * keep
        factors[level, 2] = from_north * keep
        factors[level, 3] = from_west * keep
        factors[level, 4] = from_east * keep
    factors[0, 5] = mixing * keep

    base_force[...] = jnp.zeros(base_force.shape, jnp.float32)
    step_force[...] = jnp.zeros(step_force.shape, jnp.float32)
    rims = rims_ref[...] + pair_ref[HALO:, : 2 * LANE]

    @pl.when((section == 1) | (section == 3))
    def _():
        on_left = section == 1
        before_six = jnp.where(tile == 6, cross_ref[HALO:, :LANE], 0.0)
        edges = jnp.concatenate([rims[:ROWS, LANE:] + before_six, rims[ROWS:, LANE:]], axis=0)
        source_tile = first_source(offset, tile)
        pick = iota((96, RIMS), 0)
        part = pick >> 5
        near = pick & 31
        near = jnp.where(near < 28, near, near - 32)
        coarse = offset + tile * 8 + third(near + 6) - 2 + part - 1 - source_tile * ROWS
        picked = dot((iota((96, RIMS), 1) == coarse).astype(jnp.float32), edges)
        south, value, north = picked[:32], picked[32:64], picked[64:]
        place = lane - 3 * third(lane)
        west = jnp.where(place == jnp.where(on_left, 0, -1), value, turn(value, 1, 1))
        east = jnp.where(place == jnp.where(on_left, -1, 2), value, turn(value, -1, 1))
        other = jnp.where((third(lane) & 1) == 0, turn(value, -3, 1), turn(value, 3, 1))
        cy = jnp.zeros((32, LANE), jnp.float32)
        cx = jnp.zeros((32, LANE), jnp.float32)
        for field in range(STATES // 2):
            mine = (lane >= 6 * field) & (lane < 6 * field + 6)
            cy = jnp.where(mine, turn(value, 6 * field - 3 * STATES, 1), cy)
            cx = jnp.where(mine, turn(value, 6 * field - 3 * STATES - 6, 1), cx)
        change = flux(value, south, north, west, east, other, cy, cx) / RATIO
        out = iota((LANE, STATES * LANE), 1)
        spot = out & (LANE - 1)
        wanted = 3 * (out >> 7) + jnp.where(on_left, third(spot), third(spot - 119))
        start = jnp.where(on_left, 0, LANE - 6)
        valid = (spot >= start) & (spot < start + 6)
        spread = (valid & (iota((LANE, STATES * LANE), 0) == wanted)).astype(jnp.float32)
        forced = dot(jnp.concatenate([value, change], axis=0), spread)

        def place_side(lanes):
            for p in range(STATES):
                block = forced[:, p * LANE : (p + 1) * LANE]
                base_force[p, :, lanes] = weight[:, lanes] * block[:32]
                step_force[p, :, lanes] = weight[:, lanes] * block[32:]

        @pl.when(on_left)
        def _():
            place_side(slice(0, LANE))

        @pl.when(jnp.logical_not(on_left))
        def _():
            place_side(slice(2 * LANE, 3 * LANE))

    @pl.when(is_nest & ((tile == 0) | (tile == 7)))
    def _():
        rows = rims[:SLOTS]
        wide = iota((8, 2 * LANE), 1)
        narrow = iota((SLOTS, LANE), 1)
        outside = turn(rows[:, LANE:], 84, 1)
        outside = jnp.where((narrow < 2) | (narrow >= LANE - 2), outside, 0.0)
        rows = jnp.concatenate([rows[:, :LANE], outside], axis=1)
        cy = rows[4 * STATES : 4 * STATES + 8]
        cx = rows[4 * STATES + 8 :]
        changes = []
        for field in range(STATES // 2):
            value = rows[8 * field : 8 * field + 8]
            west = jnp.where(wide == jnp.where(section == 1, 0, -1), value, turn(value, 1, 1))
            east = jnp.where(wide == jnp.where(section == 3, LANE - 1, -1), value, turn(value, -1, 1))
            changes.append(
                flux(
                    value,
                    turn(value, 1, 0),
                    turn(value, -1, 0),
                    west,
                    east,
                    turn(value, 4, 0),
                    cy,
                    cx,
                )
                / RATIO
            )
        both = jnp.concatenate([rows[: 4 * STATES]] + changes, axis=0)
        target = iota((2 * LANE, 4 * LANE), 1)
        target = jnp.where(target < 448, target, target - 512)
        coarse = (((target + 66) * 171) >> 9) - 22
        spread = (iota((2 * LANE, 4 * LANE), 0) == (coarse & (2 * LANE - 1))).astype(jnp.float32)
        forced = dot(both, spread)
        eight = iota((8, 4 * LANE), 0)

        def place_rows(rows, split):
            zone = jnp.where(split == 3, eight < ZONE, eight >= 8 - ZONE)
            for p in range(STATES):
                for ref, start in ((base_force, 0), (step_force, 4 * STATES)):
                    spot = start + 4 * p
                    value = jnp.where(eight < split, forced[spot + 1 : spot + 2], forced[spot + 2 : spot + 3])
                    ref[p, rows, :] = jnp.where(zone, weight[rows] * value, ref[p, rows, :])

        @pl.when(tile == 0)
        def _():
            place_rows(slice(0, 8), 3)

        @pl.when(tile == 7)
        def _():
            place_rows(slice(16, 24), 5)

    def substep(source, target, number):
        def per_field(field, carry):
            values = [source[2 * field + level] for level in range(2)]
            for level in range(2):
                value = values[level]
                result = factors[level, 0] * value + factors[0, 5] * values[1 - level]
                result += factors[level, 1] * turn(value, 1, 0)
                result += factors[level, 2] * turn(value, -1, 0)
                result += factors[level, 3] * turn(value, 1, 1)
                result += factors[level, 4] * turn(value, -1, 1)
                p = 2 * field + level
                result += base_force[p] + float(number) * step_force[p]
                target[p] = result
            return carry

        lax.fori_loop(0, STATES // 2, per_field, 0)

    substep(here, there, 1)

    @pl.when(is_nest)
    def _():
        substep(there, here, 2)
        substep(here, there, 3)

    out_ref[...] = there[:, :ROWS, :COLS]
    columns = iota((COLS, LANE), 1) * RATIO
    source = iota((COLS, LANE), 0)
    gather = ((source >= columns) & (source < columns + RATIO)).astype(jnp.float32)
    narrowed[...] = dot(out_ref[...].reshape(STATES * ROWS, COLS), gather)
    total = sum(narrowed[pl.ds(i, STATES * 8, stride=RATIO), :] for i in range(RATIO))
    means_ref[...] = total / (RATIO * RATIO)


def merge_kernel(offset_ref, first_ref, second_ref, third_ref, fourth_ref, block_ref, out_ref):
    tile = lax.axis_index("tile")
    section = lax.axis_index("section")
    offset = offset_ref[0]
    rest = offset % 8

    @pl.when(section > 0)
    def _():
        out_ref[...] = block_ref[...]

    @pl.when(section == 0)
    def _():
        nest_row = tile * ROWS + iota((ROWS, COLS), 0) - offset
        covered = (nest_row >= 0) & (nest_row < 64)
        for p in range(STATES):
            parts = [r[8 * p : 8 * p + 8] for r in (first_ref, second_ref, third_ref, fourth_ref)]
            moved = pltpu.roll(jnp.concatenate(parts, axis=0), rest + 24, 0)
            out_ref[p] = jnp.where(covered, moved[:ROWS], block_ref[p])


VMEM = pl.BlockSpec(memory_space=pltpu.VMEM)
SMEM = pl.BlockSpec(memory_space=pltpu.SMEM)


def shaped(*shape):
    return jax.ShapeDtypeStruct(shape, jnp.float32)


def in_rounds(edges, count):
    at = {}
    for source, target in edges:
        mine, theirs = ("from", source), ("to", target)
        a = next(c for c in range(count) if (mine, c) not in at)
        b = next(c for c in range(count) if (theirs, c) not in at)
        path = []
        node, color = theirs, a
        while (node, color) in at:
            node_next = at[(node, color)]
            path.append((node, node_next, color))
            node, color = node_next, (b if color == a else a)
        for one, two, color in path:
            del at[(one, color)], at[(two, color)]
        for one, two, color in path:
            swapped = b if color == a else a
            at[(one, swapped)] = two
            at[(two, swapped)] = one
        at[(mine, a)] = theirs
        at[(theirs, a)] = mine
    rounds = [[] for _ in range(count)]
    for (node, color), other in sorted(at.items()):
        if node[0] == "from":
            rounds[color].append((node[1], other[1]))
    return rounds


def rim_pairs(start):
    to_chips = [(0, 0), (1, 1), (0, 2), (1, 3), (2, 3), (2, 4), (1, 5), (3, 4), (2, 6), (3, 7)]
    sends = [(start + step, tile) for step, tile in to_chips]
    middle = [[(start, 0), (start + 1, 1), (start + 2, 6), (start + 3, 7)]]
    if start == 1:
        sends.append((0, 0))
        middle.append([(0, 0)])
    groups = []
    for section, inner in ((1, ((2, 1), (3, 2))), (3, ((1, 2), (2, 3)))):
        edges = [(device(a, 0), device(b, section)) for a, b in sends]
        edges += [(device(t, a), device(t, b)) for t in range(8) for a, b in inner]
        groups.append(in_rounds(edges, 3))
    middle = [[(device(a, 0), device(b, 2)) for a, b in pairs] for pairs in middle]
    return groups[0], middle, groups[1]


TOGETHER = ((1, 8), (2, 10), (3, 11), (4, 12), (5,), (6,), (7,), (9,))


def mean_pairs(distance):
    (group,) = [g for g in TOGETHER if distance in g]
    return [
        (device(3 * tile - step, 0), device(tile, 0))
        for step in group
        for tile in range(8)
        if 0 <= 3 * tile - step < 8
    ]


BOTH = ("tile", "section")


def on_device(state, courant, nest_offset):
    planes = state.reshape(STATES, ROWS, COLS)
    speeds = courant.reshape(4, ROWS, COLS)
    offset = nest_offset[0]
    payloads = pl.pallas_call(
        pack_kernel,
        out_shape=[shaped(SLOTS, 2 * LANE)] * 3,
        in_specs=[SMEM, VMEM, VMEM],
        out_specs=[VMEM] * 3,
        name="pack",
    )(nest_offset, planes, speeds)

    def send_rims(start, west, middle, east):
        groups = rim_pairs(start)
        west, middle, east = (
            [lax.ppermute(value, BOTH, pairs) for pairs in lists]
            for value, lists in zip((west, middle, east), groups)
        )
        return (*west, sum(middle), *east)

    received = lax.switch(
        (offset - 2) // ROWS - 1,
        [functools.partial(send_rims, start) for start in (1, 2, 3)],
        *payloads,
    )
    west, east, rims, to_pair, to_cross = pl.pallas_call(
        relay_kernel,
        out_shape=[
            shaped(ROWS, LANE),
            shaped(ROWS, LANE),
            shaped(RIMS, 2 * LANE),
            shaped(HALO + RIMS, COLS),
            shaped(HALO + ROWS, COLS),
        ],
        in_specs=[SMEM] + [VMEM] * 9,
        out_specs=[VMEM] * 5,
        name="relay",
    )(nest_offset, planes, speeds, *received)
    pair_map = [(device(t, s), device(t ^ 1, s)) for t in range(8) for s in range(4)]
    cross_map = [
        (device(a, s), device(b, s))
        for low in (1, 3, 5)
        for a, b in ((low, low + 1), (low + 1, low))
        for s in range(4)
    ]
    from_cross = lax.ppermute(to_cross, BOTH, cross_map)
    from_pair = lax.ppermute(to_pair, BOTH, pair_map)
    block, means = pl.pallas_call(
        main_kernel,
        out_shape=[shaped(STATES, ROWS, COLS), shaped(STATES * 8, LANE)],
        in_specs=[SMEM] + [VMEM] * 7,
        out_specs=[VMEM] * 2,
        scratch_shapes=[
            pltpu.VMEM((STATES, 32, 4 * LANE), jnp.float32),
            pltpu.VMEM((STATES, 32, 4 * LANE), jnp.float32),
            pltpu.VMEM((2, 6, 32, 4 * LANE), jnp.float32),
            pltpu.VMEM((STATES, 32, 4 * LANE), jnp.float32),
            pltpu.VMEM((STATES, 32, 4 * LANE), jnp.float32),
            pltpu.VMEM((STATES * ROWS, LANE), jnp.float32),
        ],
        compiler_params=pltpu.CompilerParams(vmem_limit_bytes=32 * 1024 * 1024),
        name="nest",
    )(nest_offset, planes, speeds, west, east, rims, from_pair, from_cross)
    columns = jnp.concatenate(
        [
            lax.ppermute(means, BOTH, [(device(t, s), device(t, 0)) for t in range(8)])
            for s in (1, 2, 3)
        ],
        axis=1,
    )

    def send_means(start, value):
        return tuple(lax.ppermute(value, BOTH, mean_pairs(start + 1 - j)) for j in range(4))

    blocks = lax.switch(
        offset // 8 - 3,
        [functools.partial(send_means, start) for start in range(3, 12)],
        columns,
    )
    merged = pl.pallas_call(
        merge_kernel,
        out_shape=shaped(STATES, ROWS, COLS),
        in_specs=[SMEM] + [VMEM] * 5,
        out_specs=VMEM,
        compiler_params=pltpu.CompilerParams(vmem_limit_bytes=32 * 1024 * 1024),
        name="merge",
    )(nest_offset, *blocks, block)
    return merged.reshape(state.shape)


def solution(mesh):
    small = mesh.shape["tile"] == 8 and mesh.shape["section"] == 4
    return jax.shard_map(
        on_device if small else general_on_device,
        mesh=mesh,
        in_specs=(P(None, None, "tile", "section"), P(None, None, "tile", "section"), P()),
        out_specs=P(None, None, "tile", "section"),
        check_vma=False,
    )
```

```python
import functools

import jax
import jax.numpy as jnp
from jax import lax
from jax.experimental import pallas as pl
from jax.experimental.pallas import tpu as pltpu
from jax.sharding import PartitionSpec as P

RATIO = 3
ZONE = 5


diffusion = 0.02
mixing = 0.05


def shifted(value, axis, steps):
    count = lax.axis_size(axis)
    leading, last = (max(0, -steps), min(count, count - steps))
    return lax.ppermute(value, axis, [(source, source + steps) for source in range(leading, last)])


def with_halo(block, sides, width):
    for axis, dim in sides:
        count = lax.axis_size(axis)
        forward = [(i, i + 1) for i in range(count - 1)]
        backward = [(target, source) for source, target in forward]
        low = lax.ppermute(
            lax.slice_in_dim(block, block.shape[dim] - width, None, axis=dim), axis, forward
        )
        high = lax.ppermute(lax.slice_in_dim(block, 0, width, axis=dim), axis, backward)
        block = jnp.concatenate([low, block, high], axis=dim)
    return block


def advance(values, courant, padded, low_row, high_row, low_col, high_col):
    row_count = values.shape[2]
    col_count = values.shape[3]
    row_index = lax.broadcasted_iota(jnp.int32, (1, 1, row_count, col_count), 2)
    column_index = lax.broadcasted_iota(jnp.int32, (1, 1, row_count, col_count), 3)
    south_side = jnp.where(low_row & (row_index == 0), values, padded[:, :, :-2, 1:-1])
    north_side = jnp.where(high_row & (row_index == row_count - 1), values, padded[:, :, 2:, 1:-1])
    west_side = jnp.where(low_col & (column_index == 0), values, padded[:, :, 1:-1, :-2])
    east_side = jnp.where(
        high_col & (column_index == col_count - 1), values, padded[:, :, 1:-1, 2:]
    )
    stacked = jnp.pad(values, ((0, 0), (1, 1), (0, 0), (0, 0)), mode="edge")
    level_below = stacked[:, :-2]
    level_above = stacked[:, 2:]
    speed_y = courant[0]
    speed_x = courant[1]
    transport = (
        jnp.maximum(speed_y, 0.0) * (values - south_side)
        + jnp.minimum(speed_y, 0.0) * (north_side - values)
        + jnp.maximum(speed_x, 0.0) * (values - west_side)
        + jnp.minimum(speed_x, 0.0) * (east_side - values)
    )
    spread = south_side + north_side + west_side + east_side - 4.0 * values
    column = level_below + level_above - 2.0 * values
    return values - transport + diffusion * spread + mixing * column


def send_rims(values, distance):
    return shifted(values, "section", distance)


def general_on_device(state, courant, nest_offset):
    fields, levels, row_count, col_count = state.shape
    tile_count = lax.axis_size("tile")
    section_count = lax.axis_size("section")
    parent_count = section_count // 4
    tile_index = lax.axis_index("tile")
    section = lax.axis_index("section")
    offset = nest_offset[0]
    total_rows = row_count * tile_count
    nest_height = total_rows // RATIO
    third_width = col_count // RATIO
    coarse_rows = row_count // RATIO
    parent_width = parent_count * col_count
    nest_width = section_count * col_count - parent_width
    is_parent = section < parent_count
    low_row = tile_index == 0
    high_row = tile_index == tile_count - 1
    low_col = (section == 0) | (section == parent_count)
    high_col = (section == parent_count - 1) | (section == section_count - 1)

    def step(values):
        padded = with_halo(values, (("tile", 2), ("section", 3)), 1)
        return advance(values, courant, padded, low_row, high_row, low_col, high_col)

    stepped = step(state)
    local_rows = tile_index * row_count + jnp.arange(row_count, dtype=jnp.int32)
    rim_coarse = jnp.array([0, 1, nest_height - 2, nest_height - 1], dtype=jnp.int32)
    wanted = offset + rim_coarse
    pick_rows = (wanted[:, None] == local_rows[None, :]).astype(jnp.float32)
    parent_flag = is_parent.astype(jnp.float32)
    both_states = jnp.stack([state, stepped]) * parent_flag
    rim_part = jnp.einsum(
        "jr,tflrc->tfljc", pick_rows, both_states, precision=lax.Precision.HIGHEST
    )
    edge_cols = jnp.array([0, 1, parent_width - 2, parent_width - 1], dtype=jnp.int32)
    global_cols = section * col_count + jnp.arange(col_count, dtype=jnp.int32)
    pick_edge = (global_cols[:, None] == edge_cols[None, :]).astype(jnp.float32)
    edge_local = jnp.einsum(
        "tflrc,ck->tflrk", both_states, pick_edge, precision=lax.Precision.HIGHEST
    )
    span_rows = offset + jnp.arange(nest_height, dtype=jnp.int32)
    pick_span = (span_rows[:, None] == local_rows[None, :]).astype(jnp.float32)
    edge_part = jnp.einsum(
        "nr,tflrk->tflnk", pick_span, edge_local, precision=lax.Precision.HIGHEST
    )
    packed = jnp.concatenate(
        [
            rim_part.reshape(2 * fields * levels, 4 * col_count),
            edge_part.reshape(2 * fields * levels, nest_height * 4),
        ],
        axis=1,
    )
    summed = lax.psum(packed, "tile")
    nest_index = jnp.maximum(section - parent_count, 0)
    source_parent = nest_index // RATIO
    received = jnp.zeros_like(summed)
    for distance in range(parent_count, 3 * parent_count + 1):
        arrived = send_rims(summed, distance)
        hit = jnp.logical_not(is_parent) & (section - distance == source_parent)
        received = jnp.where(hit, arrived, received)
    rim_rows = received[:, : 4 * col_count].reshape(2, fields, levels, 4, col_count)
    edges = received[:, 4 * col_count :].reshape(2, fields, levels, nest_height, 4)
    rim_strip = lax.dynamic_slice_in_dim(rim_rows, nest_index % RATIO * third_width, third_width, 4)
    rim_strip = jnp.repeat(rim_strip, RATIO, axis=4)
    row_choice = ((local_rows // RATIO)[:, None] == rim_coarse[None, :]).astype(jnp.float32)
    forcing_rows = jnp.einsum(
        "rj,tfljc->tflrc", row_choice, rim_strip, precision=lax.Precision.HIGHEST
    )
    nest_cols = nest_index * col_count + jnp.arange(col_count, dtype=jnp.int32)
    col_choice = (edge_cols[:, None] == (nest_cols // RATIO)[None, :]).astype(jnp.float32)
    coarse_choice = (
        (local_rows // RATIO)[:, None] == jnp.arange(nest_height, dtype=jnp.int32)[None, :]
    ).astype(jnp.float32)
    edge_rows = jnp.einsum("rn,tflnk->tflrk", coarse_choice, edges, precision=lax.Precision.HIGHEST)
    forcing_cols = jnp.einsum(
        "tflrk,kc->tflrc", edge_rows, col_choice, precision=lax.Precision.HIGHEST
    )
    row_depth = jnp.minimum(local_rows, total_rows - 1 - local_rows)
    col_depth = jnp.minimum(nest_cols, nest_width - 1 - nest_cols)
    row_zone = (row_depth < ZONE)[:, None]
    forcing = jnp.where(row_zone, forcing_rows, forcing_cols)
    depth = jnp.minimum(row_depth[:, None], col_depth[None, :])
    weight = jnp.maximum(ZONE - depth, 0).astype(jnp.float32) / ZONE

    def relax(values, substep):
        fraction = (substep + 1) / RATIO
        target = forcing[0] + fraction * (forcing[1] - forcing[0])
        return values + weight * (target - values)

    nest_field = relax(stepped, 0)
    for substep in range(1, RATIO):
        nest_field = relax(step(nest_field), substep)
    block_means = nest_field.reshape(fields, levels, coarse_rows, RATIO, third_width, RATIO).sum(
        axis=(3, 5)
    ) / (RATIO * RATIO)
    wanted_nest = local_rows - offset
    portion = lax.all_gather(block_means, "tile", axis=2, tiled=True)
    row_span = portion.shape[2]
    select = (wanted_nest[:, None] == jnp.arange(row_span, dtype=jnp.int32)[None, :]).astype(
        jnp.float32
    )
    gathered = jnp.einsum("rs,flsc->flrc", select, portion, precision=lax.Precision.HIGHEST)
    target_slot = jnp.where(is_parent, -1, (section - parent_count) // RATIO)
    slot_index = jnp.arange(section_count, dtype=jnp.int32)
    outbound = jnp.where(
        (slot_index == target_slot)[None, None, None, :, None], gathered[:, :, :, None, :], 0.0
    )
    outbound = outbound.reshape(fields, levels, row_count, section_count * third_width)
    received_means = lax.all_to_all(outbound, "section", split_axis=3, concat_axis=3, tiled=True)
    start_col = (parent_count + RATIO * jnp.minimum(section, parent_count - 1)) * third_width
    feedback = lax.dynamic_slice_in_dim(received_means, start_col, col_count, 3)
    covered = ((wanted_nest >= 0) & (wanted_nest < nest_height))[:, None]
    parent_final = jnp.where(covered, feedback, stepped)
    return jnp.where(is_parent, parent_final, nest_field)


ROWS = 24
COLS = 384
LANE = 128
STATES = 10
PLANES = 14
SLOTS = 4 * PLANES
HALO = SLOTS + 8
NEST_MARK = 1.0
PARENT_MARK = 2.0
RIMS = 3 * ROWS
EXACT = lax.Precision.HIGHEST


def device(tile, section):
    return tile * 4 + section


def third(value):
    return (value * 43) >> 7


def iota(shape, dim):
    return lax.broadcasted_iota(jnp.int32, shape, dim)


def dot(a, b):
    return jnp.dot(a, b, precision=EXACT, preferred_element_type=jnp.float32)


def turn(value, steps, dim):
    size = value.shape[dim]
    steps = steps % size
    return pltpu.roll(value, steps, dim) if steps else value


def plane_of(state_ref, courant_ref, p):
    return state_ref[p] if p < STATES else courant_ref[p - STATES]


def pack_kernel(offset_ref, state_ref, courant_ref, west_ref, middle_ref, east_ref):
    tile = lax.axis_index("tile")
    section = lax.axis_index("section")
    offset = offset_ref[0]
    first = tile * ROWS
    lane = iota((ROWS, LANE), 1)
    left = jnp.zeros((ROWS, LANE), jnp.float32)
    right = jnp.zeros((ROWS, LANE), jnp.float32)
    for p in range(PLANES):
        source = plane_of(state_ref, courant_ref, p)
        mine = (lane >= 3 * p) & (lane < 3 * p + 3)
        left = jnp.where(mine, turn(source[:, :LANE], 3 * p, 1), left)
        right = jnp.where(mine, turn(source[:, COLS - LANE :], 3 * p - (LANE - 3), 1), right)
    top = (first <= offset + 2) & (first + ROWS - 1 >= offset - 1)
    base = jnp.where(top, offset - 1, offset + 61) - first

    def chosen(start, count):
        slot = iota((4 * count, ROWS * count), 0)
        column = iota((4 * count, ROWS * count), 1)
        local = base + (slot & 3)
        hit = (local >= 0) & (local < ROWS) & (column == (slot >> 2) * ROWS + local)
        return hit.astype(jnp.float32)

    rows = jnp.concatenate(
        [
            dot(chosen(0, STATES), state_ref[...].reshape(STATES * ROWS, COLS)),
            dot(chosen(0, 4), courant_ref[...].reshape(4 * ROWS, COLS)),
        ],
        axis=0,
    )
    lane = iota((SLOTS, LANE), 1)
    mark = jnp.where(section == 0, PARENT_MARK + tile.astype(jnp.float32), NEST_MARK)
    blank = jnp.zeros((SLOTS, LANE), jnp.float32)
    outs = ((west_ref, left), (middle_ref, left), (east_ref, right))
    for s, (out_ref, edge) in enumerate(outs):
        before = rows[:, LANE * (s - 1) : LANE * s] if s > 0 else blank
        after = rows[:, LANE * (s + 1) : LANE * (s + 2)] if s < 2 else blank
        extra = turn(jnp.where(lane < 2, after, before), 44, 1)
        side = jnp.where(
            (lane >= 42) & (lane < 46), extra, jnp.where(lane == LANE - 1, mark, 0.0)
        )
        out_ref[:, :LANE] = rows[:, LANE * s : LANE * (s + 1)]
        out_ref[:ROWS, LANE:] = jnp.where(lane[:ROWS] < 42, edge, side[:ROWS])
        out_ref[ROWS:, LANE:] = side[ROWS:]


def first_source(offset, tile):
    return jnp.maximum((offset - 2) // ROWS, 1) - 1 + jnp.minimum(tile // 2, 2)


def relay_kernel(offset_ref, state_ref, courant_ref, *refs):
    to_west, middle, to_east = refs[:3], refs[3], refs[4:7]
    west_ref, east_ref, rims_ref, pair_ref, cross_ref = refs[7:]
    tile = lax.axis_index("tile")
    even = tile % 2 == 0
    source = first_source(offset_ref[0], tile).astype(jnp.float32) + PARENT_MARK
    lane = iota((ROWS, LANE), 1)

    def marked(sources, mark):
        total = jnp.zeros((ROWS, LANE), jnp.float32)
        for ref in sources:
            total += jnp.where(ref[:ROWS, 2 * LANE - 1 :] == mark, ref[:ROWS, LANE:], 0.0)
        return jnp.where(lane < 42, total, 0.0)

    east = marked(to_west, NEST_MARK)
    west = marked(to_east, NEST_MARK)
    west_ref[...] = west
    east_ref[...] = east
    rows = middle[...]
    for ref in to_west + to_east:
        value = ref[...]
        rows += jnp.where(value[:, 2 * LANE - 1 :] >= PARENT_MARK, value, 0.0)
    wide = iota((SLOTS, LANE), 1)
    rims_ref[:SLOTS, :LANE] = rows[:, :LANE]
    rims_ref[SLOTS:, :LANE] = jnp.zeros((RIMS - SLOTS, LANE), jnp.float32)
    extra = jnp.where((wide >= 42) & (wide < 46), rows[:, LANE:], 0.0)
    extra = jnp.concatenate([extra, jnp.zeros((RIMS - SLOTS, LANE), jnp.float32)], axis=0)
    edges = [marked(to_west + to_east, source + slot) for slot in range(3)]
    rims_ref[:, LANE:] = jnp.concatenate(edges, axis=0) + extra

    def put(rows, lanes, value):
        head, tail = value[:4], value[ROWS - 4 :]
        pair_ref[rows, lanes] = jnp.where(even, tail, head)
        cross_ref[rows, lanes] = jnp.where(even, head, tail)

    for p in range(PLANES):
        put(slice(4 * p, 4 * p + 4), slice(None), plane_of(state_ref, courant_ref, p))
    put(slice(SLOTS, SLOTS + 4), slice(0, LANE), west)
    put(slice(SLOTS, SLOTS + 4), slice(LANE, 2 * LANE), east)
    pair_ref[HALO:, : 2 * LANE] = rims_ref[...]
    cross_ref[HALO:, :LANE] = edges[0]


def flux(value, south, north, west, east, other, cy, cx):
    transport = (
        jnp.maximum(cy, 0.0) * (value - south)
        + jnp.minimum(cy, 0.0) * (north - value)
        + jnp.maximum(cx, 0.0) * (value - west)
        + jnp.minimum(cx, 0.0) * (east - value)
    )
    spread = south + north + west + east - 4.0 * value
    return diffusion * spread + mixing * (other - value) - transport


def main_kernel(
    offset_ref,
    state_ref,
    courant_ref,
    west_ref,
    east_ref,
    rims_ref,
    pair_ref,
    cross_ref,
    out_ref,
    means_ref,
    here,
    there,
    factors,
    base_force,
    step_force,
    narrowed,
):
    tile = lax.axis_index("tile")
    section = lax.axis_index("section")
    offset = offset_ref[0]
    even = tile % 2 == 0
    is_nest = section > 0
    full = (32, 4 * LANE)

    after = jnp.where(even, pair_ref[:HALO], cross_ref[:HALO])
    before = jnp.where(even, cross_ref[:HALO], pair_ref[:HALO])
    wests = jnp.concatenate(
        [west_ref[...], after[SLOTS : SLOTS + 4, :LANE], before[SLOTS : SLOTS + 4, :LANE]], axis=0
    )
    easts = jnp.concatenate(
        [
            east_ref[...],
            after[SLOTS : SLOTS + 4, LANE : 2 * LANE],
            before[SLOTS : SLOTS + 4, LANE : 2 * LANE],
        ],
        axis=0,
    )
    lane = iota((32, LANE), 1)

    def ring(p):
        tail = jnp.concatenate([after[4 * p : 4 * p + 4], before[4 * p : 4 * p + 4]], axis=0)
        cells = jnp.concatenate([plane_of(state_ref, courant_ref, p), tail], axis=0)
        outside = jnp.where(
            lane < 3,
            turn(easts, -3 * p, 1),
            jnp.where(lane >= LANE - 3, turn(wests, LANE - 3 - 3 * p, 1), 0.0),
        )
        return jnp.concatenate([cells, outside], axis=1)

    for p in range(STATES):
        here[p] = ring(p)

    row = iota(full, 0)
    column = iota(full, 1)
    near_row = jnp.where(row < 28, row, row - 32)
    near_column = jnp.where(column < 448, column, column - 512)
    grid_row = near_row + tile * ROWS
    grid_column = near_column + (section - 1) * COLS
    row_depth = jnp.minimum(grid_row, 8 * ROWS - 1 - grid_row)
    column_depth = jnp.minimum(grid_column, 3 * COLS - 1 - grid_column)
    depth = jnp.maximum(jnp.minimum(row_depth, column_depth), 0)
    weight = jnp.maximum(ZONE - depth, 0).astype(jnp.float32) / ZONE
    weight = jnp.where(is_nest, weight, 0.0)
    keep = 1.0 - weight
    no_south = row == jnp.where(tile == 0, 0, -1)
    no_north = row == jnp.where(tile == 7, ROWS - 1, -1)
    no_west = column == jnp.where(section < 2, 0, -1)
    no_east = column == jnp.where((section == 0) | (section == 3), COLS - 1, -1)
    for level in range(2):
        cy = ring(STATES + level)
        cx = ring(STATES + 2 + level)
        from_south = jnp.maximum(cy, 0.0) + diffusion
        from_north = diffusion - jnp.minimum(cy, 0.0)
        from_west = jnp.maximum(cx, 0.0) + diffusion
        from_east = diffusion - jnp.minimum(cx, 0.0)
        from_south = jnp.where(no_south, 0.0, from_south)
        from_north = jnp.where(no_north, 0.0, from_north)
        from_west = jnp.where(no_west, 0.0, from_west)
        from_east = jnp.where(no_east, 0.0, from_east)
        own = (1.0 - mixing) - (from_south + from_north + from_west + from_east)
        factors[level, 0] = own * keep
        factors[level, 1] = from_south * keep
        factors[level, 2] = from_north * keep
        factors[level, 3] = from_west * keep
        factors[level, 4] = from_east * keep
    factors[0, 5] = mixing * keep

    base_force[...] = jnp.zeros(base_force.shape, jnp.float32)
    step_force[...] = jnp.zeros(step_force.shape, jnp.float32)
    rims = rims_ref[...] + pair_ref[HALO:, : 2 * LANE]

    @pl.when((section == 1) | (section == 3))
    def _():
        on_left = section == 1
        before_six = jnp.where(tile == 6, cross_ref[HALO:, :LANE], 0.0)
        edges = jnp.concatenate([rims[:ROWS, LANE:] + before_six, rims[ROWS:, LANE:]], axis=0)
        source_tile = first_source(offset, tile)
        pick = iota((96, RIMS), 0)
        part = pick >> 5
        near = pick & 31
        near = jnp.where(near < 28, near, near - 32)
        coarse = offset + tile * 8 + third(near + 6) - 2 + part - 1 - source_tile * ROWS
        picked = dot((iota((96, RIMS), 1) == coarse).astype(jnp.float32), edges)
        south, value, north = picked[:32], picked[32:64], picked[64:]
        place = lane - 3 * third(lane)
        west = jnp.where(place == jnp.where(on_left, 0, -1), value, turn(value, 1, 1))
        east = jnp.where(place == jnp.where(on_left, -1, 2), value, turn(value, -1, 1))
        other = jnp.where((third(lane) & 1) == 0, turn(value, -3, 1), turn(value, 3, 1))
        cy = jnp.zeros((32, LANE), jnp.float32)
        cx = jnp.zeros((32, LANE), jnp.float32)
        for field in range(STATES // 2):
            mine = (lane >= 6 * field) & (lane < 6 * field + 6)
            cy = jnp.where(mine, turn(value, 6 * field - 3 * STATES, 1), cy)
            cx = jnp.where(mine, turn(value, 6 * field - 3 * STATES - 6, 1), cx)
        change = flux(value, south, north, west, east, other, cy, cx) / RATIO
        out = iota((LANE, STATES * LANE), 1)
        spot = out & (LANE - 1)
        wanted = 3 * (out >> 7) + jnp.where(on_left, third(spot), third(spot - 119))
        start = jnp.where(on_left, 0, LANE - 6)
        valid = (spot >= start) & (spot < start + 6)
        spread = (valid & (iota((LANE, STATES * LANE), 0) == wanted)).astype(jnp.float32)
        forced = dot(jnp.concatenate([value, change], axis=0), spread)

        def place_side(lanes):
            for p in range(STATES):
                block = forced[:, p * LANE : (p + 1) * LANE]
                base_force[p, :, lanes] = weight[:, lanes] * block[:32]
                step_force[p, :, lanes] = weight[:, lanes] * block[32:]

        @pl.when(on_left)
        def _():
            place_side(slice(0, LANE))

        @pl.when(jnp.logical_not(on_left))
        def _():
            place_side(slice(2 * LANE, 3 * LANE))

    @pl.when(is_nest & ((tile == 0) | (tile == 7)))
    def _():
        rows = rims[:SLOTS]
        wide = iota((8, 2 * LANE), 1)
        narrow = iota((SLOTS, LANE), 1)
        outside = turn(rows[:, LANE:], 84, 1)
        outside = jnp.where((narrow < 2) | (narrow >= LANE - 2), outside, 0.0)
        rows = jnp.concatenate([rows[:, :LANE], outside], axis=1)
        cy = rows[4 * STATES : 4 * STATES + 8]
        cx = rows[4 * STATES + 8 :]
        changes = []
        for field in range(STATES // 2):
            value = rows[8 * field : 8 * field + 8]
            west = jnp.where(wide == jnp.where(section == 1, 0, -1), value, turn(value, 1, 1))
            east = jnp.where(wide == jnp.where(section == 3, LANE - 1, -1), value, turn(value, -1, 1))
            changes.append(
                flux(
                    value,
                    turn(value, 1, 0),
                    turn(value, -1, 0),
                    west,
                    east,
                    turn(value, 4, 0),
                    cy,
                    cx,
                )
                / RATIO
            )
        both = jnp.concatenate([rows[: 4 * STATES]] + changes, axis=0)
        target = iota((2 * LANE, 4 * LANE), 1)
        target = jnp.where(target < 448, target, target - 512)
        coarse = (((target + 66) * 171) >> 9) - 22
        spread = (iota((2 * LANE, 4 * LANE), 0) == (coarse & (2 * LANE - 1))).astype(jnp.float32)
        forced = dot(both, spread)
        eight = iota((8, 4 * LANE), 0)

        def place_rows(rows, split):
            zone = jnp.where(split == 3, eight < ZONE, eight >= 8 - ZONE)
            for p in range(STATES):
                for ref, start in ((base_force, 0), (step_force, 4 * STATES)):
                    spot = start + 4 * p
                    value = jnp.where(eight < split, forced[spot + 1 : spot + 2], forced[spot + 2 : spot + 3])
                    ref[p, rows, :] = jnp.where(zone, weight[rows] * value, ref[p, rows, :])

        @pl.when(tile == 0)
        def _():
            place_rows(slice(0, 8), 3)

        @pl.when(tile == 7)
        def _():
            place_rows(slice(16, 24), 5)

    def substep(source, target, number):
        def per_field(field, carry):
            values = [source[2 * field + level] for level in range(2)]
            for level in range(2):
                value = values[level]
                result = factors[level, 0] * value + factors[0, 5] * values[1 - level]
                result += factors[level, 1] * turn(value, 1, 0)
                result += factors[level, 2] * turn(value, -1, 0)
                result += factors[level, 3] * turn(value, 1, 1)
                result += factors[level, 4] * turn(value, -1, 1)
                p = 2 * field + level
                result += base_force[p] + float(number) * step_force[p]
                target[p] = result
            return carry

        lax.fori_loop(0, STATES // 2, per_field, 0)

    substep(here, there, 1)

    @pl.when(is_nest)
    def _():
        substep(there, here, 2)
        substep(here, there, 3)

    out_ref[...] = there[:, :ROWS, :COLS]
    columns = iota((COLS, LANE), 1) * RATIO
    source = iota((COLS, LANE), 0)
    gather = ((source >= columns) & (source < columns + RATIO)).astype(jnp.float32)
    narrowed[...] = dot(out_ref[...].reshape(STATES * ROWS, COLS), gather)
    total = sum(narrowed[pl.ds(i, STATES * 8, stride=RATIO), :] for i in range(RATIO))
    means_ref[...] = total / (RATIO * RATIO)


def merge_kernel(offset_ref, first_ref, second_ref, third_ref, fourth_ref, block_ref, out_ref):
    tile = lax.axis_index("tile")
    section = lax.axis_index("section")
    offset = offset_ref[0]
    rest = offset % 8

    @pl.when(section > 0)
    def _():
        out_ref[...] = block_ref[...]

    @pl.when(section == 0)
    def _():
        nest_row = tile * ROWS + iota((ROWS, COLS), 0) - offset
        covered = (nest_row >= 0) & (nest_row < 64)
        for p in range(STATES):
            parts = [r[8 * p : 8 * p + 8] for r in (first_ref, second_ref, third_ref, fourth_ref)]
            moved = pltpu.roll(jnp.concatenate(parts, axis=0), rest + 24, 0)
            out_ref[p] = jnp.where(covered, moved[:ROWS], block_ref[p])


VMEM = pl.BlockSpec(memory_space=pltpu.VMEM)
SMEM = pl.BlockSpec(memory_space=pltpu.SMEM)


def shaped(*shape):
    return jax.ShapeDtypeStruct(shape, jnp.float32)


def in_rounds(edges, count):
    at = {}
    for source, target in edges:
        mine, theirs = ("from", source), ("to", target)
        a = next(c for c in range(count) if (mine, c) not in at)
        b = next(c for c in range(count) if (theirs, c) not in at)
        path = []
        node, color = theirs, a
        while (node, color) in at:
            node_next = at[(node, color)]
            path.append((node, node_next, color))
            node, color = node_next, (b if color == a else a)
        for one, two, color in path:
            del at[(one, color)], at[(two, color)]
        for one, two, color in path:
            swapped = b if color == a else a
            at[(one, swapped)] = two
            at[(two, swapped)] = one
        at[(mine, a)] = theirs
        at[(theirs, a)] = mine
    rounds = [[] for _ in range(count)]
    for (node, color), other in sorted(at.items()):
        if node[0] == "from":
            rounds[color].append((node[1], other[1]))
    return rounds


def rim_pairs(start):
    to_chips = [(0, 0), (1, 1), (0, 2), (1, 3), (2, 3), (2, 4), (1, 5), (3, 4), (2, 6), (3, 7)]
    sends = [(start + step, tile) for step, tile in to_chips]
    middle = [[(start, 0), (start + 1, 1), (start + 2, 6), (start + 3, 7)]]
    if start == 1:
        sends.append((0, 0))
        middle.append([(0, 0)])
    groups = []
    for section, inner in ((1, ((2, 1), (3, 2))), (3, ((1, 2), (2, 3)))):
        edges = [(device(a, 0), device(b, section)) for a, b in sends]
        edges += [(device(t, a), device(t, b)) for t in range(8) for a, b in inner]
        groups.append(in_rounds(edges, 3))
    middle = [[(device(a, 0), device(b, 2)) for a, b in pairs] for pairs in middle]
    return groups[0], middle, groups[1]


TOGETHER = ((1, 8), (2, 10), (3, 11), (4, 12), (5,), (6,), (7,), (9,))


def mean_pairs(distance):
    (group,) = [g for g in TOGETHER if distance in g]
    return [
        (device(3 * tile - step, 0), device(tile, 0))
        for step in group
        for tile in range(8)
        if 0 <= 3 * tile - step < 8
    ]


BOTH = ("tile", "section")


def on_device(state, courant, nest_offset):
    planes = state.reshape(STATES, ROWS, COLS)
    speeds = courant.reshape(4, ROWS, COLS)
    offset = nest_offset[0]
    payloads = pl.pallas_call(
        pack_kernel,
        out_shape=[shaped(SLOTS, 2 * LANE)] * 3,
        in_specs=[SMEM, VMEM, VMEM],
        out_specs=[VMEM] * 3,
        name="pack",
    )(nest_offset, planes, speeds)

    def send_rims(start, nest_offset, planes, speeds, west, middle, east):
        groups = rim_pairs(start)
        west, middle, east = (
            [lax.ppermute(value, BOTH, pairs) for pairs in lists]
            for value, lists in zip((west, middle, east), groups)
        )
        return pl.pallas_call(
            relay_kernel,
            out_shape=[
                shaped(ROWS, LANE),
                shaped(ROWS, LANE),
                shaped(RIMS, 2 * LANE),
                shaped(HALO + RIMS, COLS),
                shaped(HALO + ROWS, COLS),
            ],
            in_specs=[SMEM] + [VMEM] * 9,
            out_specs=[VMEM] * 5,
            name="relay",
        )(nest_offset, planes, speeds, *west, sum(middle), *east)

    west, east, rims, to_pair, to_cross = lax.switch(
        (offset - 2) // ROWS - 1,
        [functools.partial(send_rims, start) for start in (1, 2, 3)],
        nest_offset,
        planes,
        speeds,
        *payloads,
    )
    pair_map = [(device(t, s), device(t ^ 1, s)) for t in range(8) for s in range(4)]
    cross_map = [
        (device(a, s), device(b, s))
        for low in (1, 3, 5)
        for a, b in ((low, low + 1), (low + 1, low))
        for s in range(4)
    ]
    from_cross = lax.ppermute(to_cross, BOTH, cross_map)
    from_pair = lax.ppermute(to_pair, BOTH, pair_map)
    block, means = pl.pallas_call(
        main_kernel,
        out_shape=[shaped(STATES, ROWS, COLS), shaped(STATES * 8, LANE)],
        in_specs=[SMEM] + [VMEM] * 7,
        out_specs=[VMEM] * 2,
        scratch_shapes=[
            pltpu.VMEM((STATES, 32, 4 * LANE), jnp.float32),
            pltpu.VMEM((STATES, 32, 4 * LANE), jnp.float32),
            pltpu.VMEM((2, 6, 32, 4 * LANE), jnp.float32),
            pltpu.VMEM((STATES, 32, 4 * LANE), jnp.float32),
            pltpu.VMEM((STATES, 32, 4 * LANE), jnp.float32),
            pltpu.VMEM((STATES * ROWS, LANE), jnp.float32),
        ],
        compiler_params=pltpu.CompilerParams(vmem_limit_bytes=32 * 1024 * 1024),
        name="nest",
    )(nest_offset, planes, speeds, west, east, rims, from_pair, from_cross)
    columns = jnp.concatenate(
        [
            lax.ppermute(means, BOTH, [(device(t, s), device(t, 0)) for t in range(8)])
            for s in (1, 2, 3)
        ],
        axis=1,
    )

    def send_means(start, nest_offset, value, block):
        blocks = [lax.ppermute(value, BOTH, mean_pairs(start + 1 - j)) for j in range(4)]
        return pl.pallas_call(
            merge_kernel,
            out_shape=shaped(STATES, ROWS, COLS),
            in_specs=[SMEM] + [VMEM] * 5,
            out_specs=VMEM,
            compiler_params=pltpu.CompilerParams(vmem_limit_bytes=32 * 1024 * 1024),
            name="merge",
        )(nest_offset, *blocks, block)

    merged = lax.switch(
        offset // 8 - 3,
        [functools.partial(send_means, start) for start in range(3, 12)],
        nest_offset,
        columns,
        block,
    )
    return merged.reshape(state.shape)


def solution(mesh):
    small = mesh.shape["tile"] == 8 and mesh.shape["section"] == 4
    return jax.shard_map(
        on_device if small else general_on_device,
        mesh=mesh,
        in_specs=(P(None, None, "tile", "section"), P(None, None, "tile", "section"), P()),
        out_specs=P(None, None, "tile", "section"),
        check_vma=False,
    )
```

```python
import functools

import jax
import jax.numpy as jnp
from jax import lax
from jax.experimental import pallas as pl
from jax.experimental.pallas import tpu as pltpu
from jax.sharding import PartitionSpec as P

RATIO = 3
ZONE = 5


diffusion = 0.02
mixing = 0.05


def shifted(value, axis, steps):
    count = lax.axis_size(axis)
    leading, last = (max(0, -steps), min(count, count - steps))
    return lax.ppermute(value, axis, [(source, source + steps) for source in range(leading, last)])


def with_halo(block, sides, width):
    for axis, dim in sides:
        count = lax.axis_size(axis)
        forward = [(i, i + 1) for i in range(count - 1)]
        backward = [(target, source) for source, target in forward]
        low = lax.ppermute(
            lax.slice_in_dim(block, block.shape[dim] - width, None, axis=dim), axis, forward
        )
        high = lax.ppermute(lax.slice_in_dim(block, 0, width, axis=dim), axis, backward)
        block = jnp.concatenate([low, block, high], axis=dim)
    return block


def advance(values, courant, padded, low_row, high_row, low_col, high_col):
    row_count = values.shape[2]
    col_count = values.shape[3]
    row_index = lax.broadcasted_iota(jnp.int32, (1, 1, row_count, col_count), 2)
    column_index = lax.broadcasted_iota(jnp.int32, (1, 1, row_count, col_count), 3)
    south_side = jnp.where(low_row & (row_index == 0), values, padded[:, :, :-2, 1:-1])
    north_side = jnp.where(high_row & (row_index == row_count - 1), values, padded[:, :, 2:, 1:-1])
    west_side = jnp.where(low_col & (column_index == 0), values, padded[:, :, 1:-1, :-2])
    east_side = jnp.where(
        high_col & (column_index == col_count - 1), values, padded[:, :, 1:-1, 2:]
    )
    stacked = jnp.pad(values, ((0, 0), (1, 1), (0, 0), (0, 0)), mode="edge")
    level_below = stacked[:, :-2]
    level_above = stacked[:, 2:]
    speed_y = courant[0]
    speed_x = courant[1]
    transport = (
        jnp.maximum(speed_y, 0.0) * (values - south_side)
        + jnp.minimum(speed_y, 0.0) * (north_side - values)
        + jnp.maximum(speed_x, 0.0) * (values - west_side)
        + jnp.minimum(speed_x, 0.0) * (east_side - values)
    )
    spread = south_side + north_side + west_side + east_side - 4.0 * values
    column = level_below + level_above - 2.0 * values
    return values - transport + diffusion * spread + mixing * column


def send_rims(values, distance):
    return shifted(values, "section", distance)


def general_on_device(state, courant, nest_offset):
    fields, levels, row_count, col_count = state.shape
    tile_count = lax.axis_size("tile")
    section_count = lax.axis_size("section")
    parent_count = section_count // 4
    tile_index = lax.axis_index("tile")
    section = lax.axis_index("section")
    offset = nest_offset[0]
    total_rows = row_count * tile_count
    nest_height = total_rows // RATIO
    third_width = col_count // RATIO
    coarse_rows = row_count // RATIO
    parent_width = parent_count * col_count
    nest_width = section_count * col_count - parent_width
    is_parent = section < parent_count
    low_row = tile_index == 0
    high_row = tile_index == tile_count - 1
    low_col = (section == 0) | (section == parent_count)
    high_col = (section == parent_count - 1) | (section == section_count - 1)

    def step(values):
        padded = with_halo(values, (("tile", 2), ("section", 3)), 1)
        return advance(values, courant, padded, low_row, high_row, low_col, high_col)

    stepped = step(state)
    local_rows = tile_index * row_count + jnp.arange(row_count, dtype=jnp.int32)
    rim_coarse = jnp.array([0, 1, nest_height - 2, nest_height - 1], dtype=jnp.int32)
    wanted = offset + rim_coarse
    pick_rows = (wanted[:, None] == local_rows[None, :]).astype(jnp.float32)
    parent_flag = is_parent.astype(jnp.float32)
    both_states = jnp.stack([state, stepped]) * parent_flag
    rim_part = jnp.einsum(
        "jr,tflrc->tfljc", pick_rows, both_states, precision=lax.Precision.HIGHEST
    )
    edge_cols = jnp.array([0, 1, parent_width - 2, parent_width - 1], dtype=jnp.int32)
    global_cols = section * col_count + jnp.arange(col_count, dtype=jnp.int32)
    pick_edge = (global_cols[:, None] == edge_cols[None, :]).astype(jnp.float32)
    edge_local = jnp.einsum(
        "tflrc,ck->tflrk", both_states, pick_edge, precision=lax.Precision.HIGHEST
    )
    span_rows = offset + jnp.arange(nest_height, dtype=jnp.int32)
    pick_span = (span_rows[:, None] == local_rows[None, :]).astype(jnp.float32)
    edge_part = jnp.einsum(
        "nr,tflrk->tflnk", pick_span, edge_local, precision=lax.Precision.HIGHEST
    )
    packed = jnp.concatenate(
        [
            rim_part.reshape(2 * fields * levels, 4 * col_count),
            edge_part.reshape(2 * fields * levels, nest_height * 4),
        ],
        axis=1,
    )
    summed = lax.psum(packed, "tile")
    nest_index = jnp.maximum(section - parent_count, 0)
    source_parent = nest_index // RATIO
    received = jnp.zeros_like(summed)
    for distance in range(parent_count, 3 * parent_count + 1):
        arrived = send_rims(summed, distance)
        hit = jnp.logical_not(is_parent) & (section - distance == source_parent)
        received = jnp.where(hit, arrived, received)
    rim_rows = received[:, : 4 * col_count].reshape(2, fields, levels, 4, col_count)
    edges = received[:, 4 * col_count :].reshape(2, fields, levels, nest_height, 4)
    rim_strip = lax.dynamic_slice_in_dim(rim_rows, nest_index % RATIO * third_width, third_width, 4)
    rim_strip = jnp.repeat(rim_strip, RATIO, axis=4)
    row_choice = ((local_rows // RATIO)[:, None] == rim_coarse[None, :]).astype(jnp.float32)
    forcing_rows = jnp.einsum(
        "rj,tfljc->tflrc", row_choice, rim_strip, precision=lax.Precision.HIGHEST
    )
    nest_cols = nest_index * col_count + jnp.arange(col_count, dtype=jnp.int32)
    col_choice = (edge_cols[:, None] == (nest_cols // RATIO)[None, :]).astype(jnp.float32)
    coarse_choice = (
        (local_rows // RATIO)[:, None] == jnp.arange(nest_height, dtype=jnp.int32)[None, :]
    ).astype(jnp.float32)
    edge_rows = jnp.einsum("rn,tflnk->tflrk", coarse_choice, edges, precision=lax.Precision.HIGHEST)
    forcing_cols = jnp.einsum(
        "tflrk,kc->tflrc", edge_rows, col_choice, precision=lax.Precision.HIGHEST
    )
    row_depth = jnp.minimum(local_rows, total_rows - 1 - local_rows)
    col_depth = jnp.minimum(nest_cols, nest_width - 1 - nest_cols)
    row_zone = (row_depth < ZONE)[:, None]
    forcing = jnp.where(row_zone, forcing_rows, forcing_cols)
    depth = jnp.minimum(row_depth[:, None], col_depth[None, :])
    weight = jnp.maximum(ZONE - depth, 0).astype(jnp.float32) / ZONE

    def relax(values, substep):
        fraction = (substep + 1) / RATIO
        target = forcing[0] + fraction * (forcing[1] - forcing[0])
        return values + weight * (target - values)

    nest_field = relax(stepped, 0)
    for substep in range(1, RATIO):
        nest_field = relax(step(nest_field), substep)
    block_means = nest_field.reshape(fields, levels, coarse_rows, RATIO, third_width, RATIO).sum(
        axis=(3, 5)
    ) / (RATIO * RATIO)
    wanted_nest = local_rows - offset
    portion = lax.all_gather(block_means, "tile", axis=2, tiled=True)
    row_span = portion.shape[2]
    select = (wanted_nest[:, None] == jnp.arange(row_span, dtype=jnp.int32)[None, :]).astype(
        jnp.float32
    )
    gathered = jnp.einsum("rs,flsc->flrc", select, portion, precision=lax.Precision.HIGHEST)
    target_slot = jnp.where(is_parent, -1, (section - parent_count) // RATIO)
    slot_index = jnp.arange(section_count, dtype=jnp.int32)
    outbound = jnp.where(
        (slot_index == target_slot)[None, None, None, :, None], gathered[:, :, :, None, :], 0.0
    )
    outbound = outbound.reshape(fields, levels, row_count, section_count * third_width)
    received_means = lax.all_to_all(outbound, "section", split_axis=3, concat_axis=3, tiled=True)
    start_col = (parent_count + RATIO * jnp.minimum(section, parent_count - 1)) * third_width
    feedback = lax.dynamic_slice_in_dim(received_means, start_col, col_count, 3)
    covered = ((wanted_nest >= 0) & (wanted_nest < nest_height))[:, None]
    parent_final = jnp.where(covered, feedback, stepped)
    return jnp.where(is_parent, parent_final, nest_field)


ROWS = 24
COLS = 384
LANE = 128
STATES = 10
PLANES = 14
SLOTS = 4 * PLANES
HALO = SLOTS + 8
NEST_MARK = 1.0
PARENT_MARK = 2.0
RIMS = 3 * ROWS
EXACT = lax.Precision.HIGHEST


def device(tile, section):
    return tile * 4 + section


def third(value):
    return (value * 43) >> 7


def iota(shape, dim):
    return lax.broadcasted_iota(jnp.int32, shape, dim)


def dot(a, b):
    return jnp.dot(a, b, precision=EXACT, preferred_element_type=jnp.float32)


def turn(value, steps, dim):
    size = value.shape[dim]
    steps = steps % size
    return pltpu.roll(value, steps, dim) if steps else value


def plane_of(state_ref, courant_ref, p):
    return state_ref[p] if p < STATES else courant_ref[p - STATES]


def pack_kernel(offset_ref, state_ref, courant_ref, west_ref, middle_ref, east_ref):
    tile = lax.axis_index("tile")
    section = lax.axis_index("section")
    offset = offset_ref[0]
    first = tile * ROWS
    lane = iota((ROWS, LANE), 1)
    left = jnp.zeros((ROWS, LANE), jnp.float32)
    right = jnp.zeros((ROWS, LANE), jnp.float32)
    for p in range(PLANES):
        source = plane_of(state_ref, courant_ref, p)
        mine = (lane >= 3 * p) & (lane < 3 * p + 3)
        left = jnp.where(mine, turn(source[:, :LANE], 3 * p, 1), left)
        right = jnp.where(mine, turn(source[:, COLS - LANE :], 3 * p - (LANE - 3), 1), right)
    top = (first <= offset + 2) & (first + ROWS - 1 >= offset - 1)
    base = jnp.where(top, offset - 1, offset + 61) - first

    def chosen(start, count):
        slot = iota((4 * count, ROWS * count), 0)
        column = iota((4 * count, ROWS * count), 1)
        local = base + (slot & 3)
        hit = (local >= 0) & (local < ROWS) & (column == (slot >> 2) * ROWS + local)
        return hit.astype(jnp.float32)

    rows = jnp.concatenate(
        [
            dot(chosen(0, STATES), state_ref[...].reshape(STATES * ROWS, COLS)),
            dot(chosen(0, 4), courant_ref[...].reshape(4 * ROWS, COLS)),
        ],
        axis=0,
    )
    lane = iota((SLOTS, LANE), 1)
    mark = jnp.where(section == 0, PARENT_MARK + tile.astype(jnp.float32), NEST_MARK)
    blank = jnp.zeros((SLOTS, LANE), jnp.float32)
    outs = ((west_ref, left), (middle_ref, left), (east_ref, right))
    for s, (out_ref, edge) in enumerate(outs):
        before = rows[:, LANE * (s - 1) : LANE * s] if s > 0 else blank
        after = rows[:, LANE * (s + 1) : LANE * (s + 2)] if s < 2 else blank
        extra = turn(jnp.where(lane < 2, after, before), 44, 1)
        side = jnp.where(
            (lane >= 42) & (lane < 46), extra, jnp.where(lane == LANE - 1, mark, 0.0)
        )
        out_ref[:, :LANE] = rows[:, LANE * s : LANE * (s + 1)]
        out_ref[:ROWS, LANE:] = jnp.where(lane[:ROWS] < 42, edge, side[:ROWS])
        out_ref[ROWS:, LANE:] = side[ROWS:]


def first_source(offset, tile):
    return jnp.maximum((offset - 2) // ROWS, 1) - 1 + jnp.minimum(tile // 2, 2)


def relay_kernel(offset_ref, state_ref, courant_ref, *refs):
    to_east = refs[0:3]
    middle = refs[3]
    to_west = refs[4:7]
    west_ref, east_ref, rims_ref, pair_ref, cross_ref = refs[7:]
    tile = lax.axis_index("tile")
    even = tile % 2 == 0
    source = first_source(offset_ref[0], tile).astype(jnp.float32) + PARENT_MARK
    lane = iota((ROWS, LANE), 1)

    def marked(sources, mark):
        total = jnp.zeros((ROWS, LANE), jnp.float32)
        for ref in sources:
            total += jnp.where(ref[:ROWS, 2 * LANE - 1 :] == mark, ref[:ROWS, LANE:], 0.0)
        return jnp.where(lane < 42, total, 0.0)

    east = marked(to_west, NEST_MARK)
    west = marked(to_east, NEST_MARK)
    west_ref[...] = west
    east_ref[...] = east
    rows = middle[...]
    for ref in to_west + to_east:
        value = ref[...]
        rows += jnp.where(value[:, 2 * LANE - 1 :] >= PARENT_MARK, value, 0.0)
    wide = iota((SLOTS, LANE), 1)
    rims_ref[:SLOTS, :LANE] = rows[:, :LANE]
    rims_ref[SLOTS:, :LANE] = jnp.zeros((RIMS - SLOTS, LANE), jnp.float32)
    extra = jnp.where((wide >= 42) & (wide < 46), rows[:, LANE:], 0.0)
    extra = jnp.concatenate([extra, jnp.zeros((RIMS - SLOTS, LANE), jnp.float32)], axis=0)
    edges = [marked(to_west + to_east, source + slot) for slot in range(3)]
    rims_ref[:, LANE:] = jnp.concatenate(edges, axis=0) + extra

    def put(rows, lanes, value):
        head, tail = value[:4], value[ROWS - 4 :]
        pair_ref[rows, lanes] = jnp.where(even, tail, head)
        cross_ref[rows, lanes] = jnp.where(even, head, tail)

    for p in range(PLANES):
        put(slice(4 * p, 4 * p + 4), slice(None), plane_of(state_ref, courant_ref, p))
    put(slice(SLOTS, SLOTS + 4), slice(0, LANE), west)
    put(slice(SLOTS, SLOTS + 4), slice(LANE, 2 * LANE), east)
    pair_ref[HALO:, : 2 * LANE] = rims_ref[...]
    cross_ref[HALO:, :LANE] = edges[0]


def flux(value, south, north, west, east, other, cy, cx):
    transport = (
        jnp.maximum(cy, 0.0) * (value - south)
        + jnp.minimum(cy, 0.0) * (north - value)
        + jnp.maximum(cx, 0.0) * (value - west)
        + jnp.minimum(cx, 0.0) * (east - value)
    )
    spread = south + north + west + east - 4.0 * value
    return diffusion * spread + mixing * (other - value) - transport


def main_kernel(
    offset_ref,
    state_ref,
    courant_ref,
    west_ref,
    east_ref,
    rims_ref,
    pair_ref,
    cross_ref,
    out_ref,
    means_ref,
    here,
    there,
    factors,
    base_force,
    step_force,
    narrowed,
):
    tile = lax.axis_index("tile")
    section = lax.axis_index("section")
    offset = offset_ref[0]
    even = tile % 2 == 0
    is_nest = section > 0
    full = (32, 4 * LANE)

    after = jnp.where(even, pair_ref[:HALO], cross_ref[:HALO])
    before = jnp.where(even, cross_ref[:HALO], pair_ref[:HALO])
    wests = jnp.concatenate(
        [west_ref[...], after[SLOTS : SLOTS + 4, :LANE], before[SLOTS : SLOTS + 4, :LANE]], axis=0
    )
    easts = jnp.concatenate(
        [
            east_ref[...],
            after[SLOTS : SLOTS + 4, LANE : 2 * LANE],
            before[SLOTS : SLOTS + 4, LANE : 2 * LANE],
        ],
        axis=0,
    )
    lane = iota((32, LANE), 1)

    def ring(p):
        tail = jnp.concatenate([after[4 * p : 4 * p + 4], before[4 * p : 4 * p + 4]], axis=0)
        cells = jnp.concatenate([plane_of(state_ref, courant_ref, p), tail], axis=0)
        outside = jnp.where(
            lane < 3,
            turn(easts, -3 * p, 1),
            jnp.where(lane >= LANE - 3, turn(wests, LANE - 3 - 3 * p, 1), 0.0),
        )
        return jnp.concatenate([cells, outside], axis=1)

    for p in range(STATES):
        here[p] = ring(p)

    row = iota(full, 0)
    column = iota(full, 1)
    near_row = jnp.where(row < 28, row, row - 32)
    near_column = jnp.where(column < 448, column, column - 512)
    grid_row = near_row + tile * ROWS
    grid_column = near_column + (section - 1) * COLS
    row_depth = jnp.minimum(grid_row, 8 * ROWS - 1 - grid_row)
    column_depth = jnp.minimum(grid_column, 3 * COLS - 1 - grid_column)
    depth = jnp.maximum(jnp.minimum(row_depth, column_depth), 0)
    weight = jnp.maximum(ZONE - depth, 0).astype(jnp.float32) / ZONE
    weight = jnp.where(is_nest, weight, 0.0)
    keep = 1.0 - weight
    no_south = row == jnp.where(tile == 0, 0, -1)
    no_north = row == jnp.where(tile == 7, ROWS - 1, -1)
    no_west = column == jnp.where(section < 2, 0, -1)
    no_east = column == jnp.where((section == 0) | (section == 3), COLS - 1, -1)
    for level in range(2):
        cy = ring(STATES + level)
        cx = ring(STATES + 2 + level)
        from_south = jnp.maximum(cy, 0.0) + diffusion
        from_north = diffusion - jnp.minimum(cy, 0.0)
        from_west = jnp.maximum(cx, 0.0) + diffusion
        from_east = diffusion - jnp.minimum(cx, 0.0)
        from_south = jnp.where(no_south, 0.0, from_south)
        from_north = jnp.where(no_north, 0.0, from_north)
        from_west = jnp.where(no_west, 0.0, from_west)
        from_east = jnp.where(no_east, 0.0, from_east)
        own = (1.0 - mixing) - (from_south + from_north + from_west + from_east)
        factors[level, 0] = own * keep
        factors[level, 1] = from_south * keep
        factors[level, 2] = from_north * keep
        factors[level, 3] = from_west * keep
        factors[level, 4] = from_east * keep
    factors[0, 5] = mixing * keep

    base_force[...] = jnp.zeros(base_force.shape, jnp.float32)
    step_force[...] = jnp.zeros(step_force.shape, jnp.float32)
    rims = rims_ref[...] + pair_ref[HALO:, : 2 * LANE]

    @pl.when((section == 1) | (section == 3))
    def _():
        on_left = section == 1
        before_six = jnp.where(tile == 6, cross_ref[HALO:, :LANE], 0.0)
        edges = jnp.concatenate([rims[:ROWS, LANE:] + before_six, rims[ROWS:, LANE:]], axis=0)
        source_tile = first_source(offset, tile)
        pick = iota((96, RIMS), 0)
        part = pick >> 5
        near = pick & 31
        near = jnp.where(near < 28, near, near - 32)
        coarse = offset + tile * 8 + third(near + 6) - 2 + part - 1 - source_tile * ROWS
        picked = dot((iota((96, RIMS), 1) == coarse).astype(jnp.float32), edges)
        south, value, north = picked[:32], picked[32:64], picked[64:]
        place = lane - 3 * third(lane)
        west = jnp.where(place == jnp.where(on_left, 0, -1), value, turn(value, 1, 1))
        east = jnp.where(place == jnp.where(on_left, -1, 2), value, turn(value, -1, 1))
        other = jnp.where((third(lane) & 1) == 0, turn(value, -3, 1), turn(value, 3, 1))
        cy = jnp.zeros((32, LANE), jnp.float32)
        cx = jnp.zeros((32, LANE), jnp.float32)
        for field in range(STATES // 2):
            mine = (lane >= 6 * field) & (lane < 6 * field + 6)
            cy = jnp.where(mine, turn(value, 6 * field - 3 * STATES, 1), cy)
            cx = jnp.where(mine, turn(value, 6 * field - 3 * STATES - 6, 1), cx)
        change = flux(value, south, north, west, east, other, cy, cx) / RATIO
        out = iota((LANE, STATES * LANE), 1)
        spot = out & (LANE - 1)
        wanted = 3 * (out >> 7) + jnp.where(on_left, third(spot), third(spot - 119))
        start = jnp.where(on_left, 0, LANE - 6)
        valid = (spot >= start) & (spot < start + 6)
        spread = (valid & (iota((LANE, STATES * LANE), 0) == wanted)).astype(jnp.float32)
        forced = dot(jnp.concatenate([value, change], axis=0), spread)

        def place_side(lanes):
            for p in range(STATES):
                block = forced[:, p * LANE : (p + 1) * LANE]
                base_force[p, :, lanes] = weight[:, lanes] * block[:32]
                step_force[p, :, lanes] = weight[:, lanes] * block[32:]

        @pl.when(on_left)
        def _():
            place_side(slice(0, LANE))

        @pl.when(jnp.logical_not(on_left))
        def _():
            place_side(slice(2 * LANE, 3 * LANE))

    @pl.when(is_nest & ((tile == 0) | (tile == 7)))
    def _():
        rows = rims[:SLOTS]
        wide = iota((8, 2 * LANE), 1)
        narrow = iota((SLOTS, LANE), 1)
        outside = turn(rows[:, LANE:], 84, 1)
        outside = jnp.where((narrow < 2) | (narrow >= LANE - 2), outside, 0.0)
        rows = jnp.concatenate([rows[:, :LANE], outside], axis=1)
        cy = rows[4 * STATES : 4 * STATES + 8]
        cx = rows[4 * STATES + 8 :]
        changes = []
        for field in range(STATES // 2):
            value = rows[8 * field : 8 * field + 8]
            west = jnp.where(wide == jnp.where(section == 1, 0, -1), value, turn(value, 1, 1))
            east = jnp.where(wide == jnp.where(section == 3, LANE - 1, -1), value, turn(value, -1, 1))
            changes.append(
                flux(
                    value,
                    turn(value, 1, 0),
                    turn(value, -1, 0),
                    west,
                    east,
                    turn(value, 4, 0),
                    cy,
                    cx,
                )
                / RATIO
            )
        both = jnp.concatenate([rows[: 4 * STATES]] + changes, axis=0)
        target = iota((2 * LANE, 4 * LANE), 1)
        target = jnp.where(target < 448, target, target - 512)
        coarse = (((target + 66) * 171) >> 9) - 22
        spread = (iota((2 * LANE, 4 * LANE), 0) == (coarse & (2 * LANE - 1))).astype(jnp.float32)
        forced = dot(both, spread)
        eight = iota((8, 4 * LANE), 0)

        def place_rows(rows, split):
            zone = jnp.where(split == 3, eight < ZONE, eight >= 8 - ZONE)
            for p in range(STATES):
                for ref, start in ((base_force, 0), (step_force, 4 * STATES)):
                    spot = start + 4 * p
                    value = jnp.where(eight < split, forced[spot + 1 : spot + 2], forced[spot + 2 : spot + 3])
                    ref[p, rows, :] = jnp.where(zone, weight[rows] * value, ref[p, rows, :])

        @pl.when(tile == 0)
        def _():
            place_rows(slice(0, 8), 3)

        @pl.when(tile == 7)
        def _():
            place_rows(slice(16, 24), 5)

    def substep(source, target, number):
        def per_field(field, carry):
            values = [source[2 * field + level] for level in range(2)]
            for level in range(2):
                value = values[level]
                result = factors[level, 0] * value + factors[0, 5] * values[1 - level]
                result += factors[level, 1] * turn(value, 1, 0)
                result += factors[level, 2] * turn(value, -1, 0)
                result += factors[level, 3] * turn(value, 1, 1)
                result += factors[level, 4] * turn(value, -1, 1)
                p = 2 * field + level
                result += base_force[p] + float(number) * step_force[p]
                target[p] = result
            return carry

        lax.fori_loop(0, STATES // 2, per_field, 0)

    substep(here, there, 1)

    @pl.when(is_nest)
    def _():
        substep(there, here, 2)
        substep(here, there, 3)

    out_ref[...] = there[:, :ROWS, :COLS]
    columns = iota((COLS, LANE), 1) * RATIO
    source = iota((COLS, LANE), 0)
    gather = ((source >= columns) & (source < columns + RATIO)).astype(jnp.float32)
    narrowed[...] = dot(out_ref[...].reshape(STATES * ROWS, COLS), gather)
    total = sum(narrowed[pl.ds(i, STATES * 8, stride=RATIO), :] for i in range(RATIO))
    means_ref[...] = total / (RATIO * RATIO)


def merge_kernel(offset_ref, *refs):
    *block_refs, stepped_ref, out_ref, near = refs
    tile = lax.axis_index("tile")
    section = lax.axis_index("section")
    offset = offset_ref[0]
    rest = offset % 8

    @pl.when(section > 0)
    def _():
        out_ref[...] = stepped_ref[...]

    @pl.when(section == 0)
    def _():
        for step in range(4):
            source = 3 * tile - offset // 8 - 1 + step
            inside = (source >= 0) & (source < 8)
            for way, block_ref in enumerate(block_refs):

                @pl.when(inside & (source == (tile ^ way)))
                def _():
                    near[step] = block_ref[...]

        nest_row = tile * ROWS + iota((ROWS, COLS), 0) - offset
        covered = (nest_row >= 0) & (nest_row < 64)
        for p in range(STATES):
            parts = [near[step, 8 * p : 8 * p + 8] for step in range(4)]
            moved = pltpu.roll(jnp.concatenate(parts, axis=0), rest + 24, 0)
            out_ref[p] = jnp.where(covered, moved[:ROWS], stepped_ref[p])


VMEM = pl.BlockSpec(memory_space=pltpu.VMEM)
SMEM = pl.BlockSpec(memory_space=pltpu.SMEM)


def shaped(*shape):
    return jax.ShapeDtypeStruct(shape, jnp.float32)


def in_rounds(edges, count):
    at = {}
    for source, target in edges:
        mine, theirs = ("from", source), ("to", target)
        a = next(c for c in range(count) if (mine, c) not in at)
        b = next(c for c in range(count) if (theirs, c) not in at)
        path = []
        node, color = theirs, a
        while (node, color) in at:
            node_next = at[(node, color)]
            path.append((node, node_next, color))
            node, color = node_next, (b if color == a else a)
        for one, two, color in path:
            del at[(one, color)], at[(two, color)]
        for one, two, color in path:
            swapped = b if color == a else a
            at[(one, swapped)] = two
            at[(two, swapped)] = one
        at[(mine, a)] = theirs
        at[(theirs, a)] = mine
    rounds = [[] for _ in range(count)]
    for (node, color), other in sorted(at.items()):
        if node[0] == "from":
            rounds[color].append((node[1], other[1]))
    return rounds


def rim_pairs(start):
    to_chips = [(0, 0), (1, 1), (0, 2), (1, 3), (2, 3), (2, 4), (1, 5), (3, 4), (2, 6), (3, 7)]
    sends = [(start + step, tile) for step, tile in to_chips]
    middle = [[(start, 0), (start + 1, 1), (start + 2, 6), (start + 3, 7)]]
    if start == 1:
        sends.append((0, 0))
        middle.append([(0, 0)])
    groups = []
    for section, inner in ((1, ((2, 1), (3, 2))), (3, ((1, 2), (2, 3)))):
        edges = [(device(a, 0), device(b, section)) for a, b in sends]
        edges += [(device(t, a), device(t, b)) for t in range(8) for a, b in inner]
        groups.append(in_rounds(edges, 3)[::-1])
    middle = [[(device(a, 0), device(b, 2)) for a, b in pairs] for pairs in middle]
    return groups[0], middle, groups[1]


TOGETHER = ((1, 8), (2, 10), (3, 11), (4, 12), (5,), (6,), (7,), (9,))


def mean_pairs(distance):
    (group,) = [g for g in TOGETHER if distance in g]
    return [
        (device(3 * tile - step, 0), device(tile, 0))
        for step in group
        for tile in range(8)
        if 0 <= 3 * tile - step < 8
    ]


BOTH = ("tile", "section")


def on_device(state, courant, nest_offset):
    planes = state.reshape(STATES, ROWS, COLS)
    speeds = courant.reshape(4, ROWS, COLS)
    offset = nest_offset[0]
    payloads = pl.pallas_call(
        pack_kernel,
        out_shape=[shaped(SLOTS, 2 * LANE)] * 3,
        in_specs=[SMEM, VMEM, VMEM],
        out_specs=[VMEM] * 3,
        name="pack",
    )(nest_offset, planes, speeds)

    def send_rims(start, nest_offset, planes, speeds, west, middle, east):
        groups = rim_pairs(start)
        west, middle, east = (
            [lax.ppermute(value, BOTH, pairs) for pairs in lists]
            for value, lists in zip((west, middle, east), groups)
        )
        return pl.pallas_call(
            relay_kernel,
            out_shape=[
                shaped(ROWS, LANE),
                shaped(ROWS, LANE),
                shaped(RIMS, 2 * LANE),
                shaped(HALO + RIMS, COLS),
                shaped(HALO + ROWS, COLS),
            ],
            in_specs=[SMEM] + [VMEM] * 9,
            out_specs=[VMEM] * 5,
            name="relay",
        )(nest_offset, planes, speeds, *east, sum(middle), *west)

    west, east, rims, to_pair, to_cross = lax.switch(
        (offset - 2) // ROWS - 1,
        [functools.partial(send_rims, start) for start in (1, 2, 3)],
        nest_offset,
        planes,
        speeds,
        *payloads,
    )
    pair_map = [(device(t, s), device(t ^ 1, s)) for t in range(8) for s in range(4)]
    cross_map = [
        (device(a, s), device(b, s))
        for low in (1, 3, 5)
        for a, b in ((low, low + 1), (low + 1, low))
        for s in range(4)
    ]
    from_cross = lax.ppermute(to_cross, BOTH, cross_map)
    from_pair = lax.ppermute(to_pair, BOTH, pair_map)
    block, means = pl.pallas_call(
        main_kernel,
        out_shape=[shaped(STATES, ROWS, COLS), shaped(STATES * 8, LANE)],
        in_specs=[SMEM] + [VMEM] * 7,
        out_specs=[VMEM] * 2,
        scratch_shapes=[
            pltpu.VMEM((STATES, 32, 4 * LANE), jnp.float32),
            pltpu.VMEM((STATES, 32, 4 * LANE), jnp.float32),
            pltpu.VMEM((2, 6, 32, 4 * LANE), jnp.float32),
            pltpu.VMEM((STATES, 32, 4 * LANE), jnp.float32),
            pltpu.VMEM((STATES, 32, 4 * LANE), jnp.float32),
            pltpu.VMEM((STATES * ROWS, LANE), jnp.float32),
        ],
        compiler_params=pltpu.CompilerParams(vmem_limit_bytes=32 * 1024 * 1024),
        name="nest",
    )(nest_offset, planes, speeds, west, east, rims, from_pair, from_cross)
    columns = jnp.concatenate(
        [
            lax.ppermute(means, BOTH, [(device(t, s), device(t, 0)) for t in range(8)])
            for s in (1, 2, 3)
        ],
        axis=1,
    )

    def across(value, way):
        pairs = [(device(t, s), device(t ^ way, s)) for t in range(8) for s in range(4)]
        return lax.ppermute(value, BOTH, pairs)

    blocks = {0: columns}
    for way in (7, 3, 4, 1):
        blocks[way] = across(columns, way)
    for way in (7, 3, 4):
        blocks[way ^ 1] = across(blocks[way], 1)
    merged = pl.pallas_call(
        merge_kernel,
        out_shape=shaped(STATES, ROWS, COLS),
        in_specs=[SMEM] + [VMEM] * 9,
        out_specs=VMEM,
        scratch_shapes=[pltpu.VMEM((4, STATES * 8, COLS), jnp.float32)],
        compiler_params=pltpu.CompilerParams(vmem_limit_bytes=32 * 1024 * 1024),
        name="merge",
    )(nest_offset, *[blocks[way] for way in range(8)], block)
    return merged.reshape(state.shape)


def solution(mesh):
    small = mesh.shape["tile"] == 8 and mesh.shape["section"] == 4
    return jax.shard_map(
        on_device if small else general_on_device,
        mesh=mesh,
        in_specs=(P(None, None, "tile", "section"), P(None, None, "tile", "section"), P()),
        out_specs=P(None, None, "tile", "section"),
        check_vma=False,
    )
```

```python
import functools

import jax
import jax.numpy as jnp
from jax import lax
from jax.experimental import pallas as pl
from jax.experimental.pallas import tpu as pltpu
from jax.sharding import PartitionSpec as P

RATIO = 3
ZONE = 5


diffusion = 0.02
mixing = 0.05


def shifted(value, axis, steps):
    count = lax.axis_size(axis)
    leading, last = (max(0, -steps), min(count, count - steps))
    return lax.ppermute(value, axis, [(source, source + steps) for source in range(leading, last)])


def with_halo(block, sides, width):
    for axis, dim in sides:
        count = lax.axis_size(axis)
        forward = [(i, i + 1) for i in range(count - 1)]
        backward = [(target, source) for source, target in forward]
        low = lax.ppermute(
            lax.slice_in_dim(block, block.shape[dim] - width, None, axis=dim), axis, forward
        )
        high = lax.ppermute(lax.slice_in_dim(block, 0, width, axis=dim), axis, backward)
        block = jnp.concatenate([low, block, high], axis=dim)
    return block


def advance(values, courant, padded, low_row, high_row, low_col, high_col):
    row_count = values.shape[2]
    col_count = values.shape[3]
    row_index = lax.broadcasted_iota(jnp.int32, (1, 1, row_count, col_count), 2)
    column_index = lax.broadcasted_iota(jnp.int32, (1, 1, row_count, col_count), 3)
    south_side = jnp.where(low_row & (row_index == 0), values, padded[:, :, :-2, 1:-1])
    north_side = jnp.where(high_row & (row_index == row_count - 1), values, padded[:, :, 2:, 1:-1])
    west_side = jnp.where(low_col & (column_index == 0), values, padded[:, :, 1:-1, :-2])
    east_side = jnp.where(
        high_col & (column_index == col_count - 1), values, padded[:, :, 1:-1, 2:]
    )
    stacked = jnp.pad(values, ((0, 0), (1, 1), (0, 0), (0, 0)), mode="edge")
    level_below = stacked[:, :-2]
    level_above = stacked[:, 2:]
    speed_y = courant[0]
    speed_x = courant[1]
    transport = (
        jnp.maximum(speed_y, 0.0) * (values - south_side)
        + jnp.minimum(speed_y, 0.0) * (north_side - values)
        + jnp.maximum(speed_x, 0.0) * (values - west_side)
        + jnp.minimum(speed_x, 0.0) * (east_side - values)
    )
    spread = south_side + north_side + west_side + east_side - 4.0 * values
    column = level_below + level_above - 2.0 * values
    return values - transport + diffusion * spread + mixing * column


def send_rims(values, distance):
    return shifted(values, "section", distance)


def general_on_device(state, courant, nest_offset):
    fields, levels, row_count, col_count = state.shape
    tile_count = lax.axis_size("tile")
    section_count = lax.axis_size("section")
    parent_count = section_count // 4
    tile_index = lax.axis_index("tile")
    section = lax.axis_index("section")
    offset = nest_offset[0]
    total_rows = row_count * tile_count
    nest_height = total_rows // RATIO
    third_width = col_count // RATIO
    coarse_rows = row_count // RATIO
    parent_width = parent_count * col_count
    nest_width = section_count * col_count - parent_width
    is_parent = section < parent_count
    low_row = tile_index == 0
    high_row = tile_index == tile_count - 1
    low_col = (section == 0) | (section == parent_count)
    high_col = (section == parent_count - 1) | (section == section_count - 1)

    def step(values):
        padded = with_halo(values, (("tile", 2), ("section", 3)), 1)
        return advance(values, courant, padded, low_row, high_row, low_col, high_col)

    stepped = step(state)
    local_rows = tile_index * row_count + jnp.arange(row_count, dtype=jnp.int32)
    rim_coarse = jnp.array([0, 1, nest_height - 2, nest_height - 1], dtype=jnp.int32)
    wanted = offset + rim_coarse
    pick_rows = (wanted[:, None] == local_rows[None, :]).astype(jnp.float32)
    parent_flag = is_parent.astype(jnp.float32)
    both_states = jnp.stack([state, stepped]) * parent_flag
    rim_part = jnp.einsum(
        "jr,tflrc->tfljc", pick_rows, both_states, precision=lax.Precision.HIGHEST
    )
    edge_cols = jnp.array([0, 1, parent_width - 2, parent_width - 1], dtype=jnp.int32)
    global_cols = section * col_count + jnp.arange(col_count, dtype=jnp.int32)
    pick_edge = (global_cols[:, None] == edge_cols[None, :]).astype(jnp.float32)
    edge_local = jnp.einsum(
        "tflrc,ck->tflrk", both_states, pick_edge, precision=lax.Precision.HIGHEST
    )
    span_rows = offset + jnp.arange(nest_height, dtype=jnp.int32)
    pick_span = (span_rows[:, None] == local_rows[None, :]).astype(jnp.float32)
    edge_part = jnp.einsum(
        "nr,tflrk->tflnk", pick_span, edge_local, precision=lax.Precision.HIGHEST
    )
    packed = jnp.concatenate(
        [
            rim_part.reshape(2 * fields * levels, 4 * col_count),
            edge_part.reshape(2 * fields * levels, nest_height * 4),
        ],
        axis=1,
    )
    summed = lax.psum(packed, "tile")
    nest_index = jnp.maximum(section - parent_count, 0)
    source_parent = nest_index // RATIO
    received = jnp.zeros_like(summed)
    for distance in range(parent_count, 3 * parent_count + 1):
        arrived = send_rims(summed, distance)
        hit = jnp.logical_not(is_parent) & (section - distance == source_parent)
        received = jnp.where(hit, arrived, received)
    rim_rows = received[:, : 4 * col_count].reshape(2, fields, levels, 4, col_count)
    edges = received[:, 4 * col_count :].reshape(2, fields, levels, nest_height, 4)
    rim_strip = lax.dynamic_slice_in_dim(rim_rows, nest_index % RATIO * third_width, third_width, 4)
    rim_strip = jnp.repeat(rim_strip, RATIO, axis=4)
    row_choice = ((local_rows // RATIO)[:, None] == rim_coarse[None, :]).astype(jnp.float32)
    forcing_rows = jnp.einsum(
        "rj,tfljc->tflrc", row_choice, rim_strip, precision=lax.Precision.HIGHEST
    )
    nest_cols = nest_index * col_count + jnp.arange(col_count, dtype=jnp.int32)
    col_choice = (edge_cols[:, None] == (nest_cols // RATIO)[None, :]).astype(jnp.float32)
    coarse_choice = (
        (local_rows // RATIO)[:, None] == jnp.arange(nest_height, dtype=jnp.int32)[None, :]
    ).astype(jnp.float32)
    edge_rows = jnp.einsum("rn,tflnk->tflrk", coarse_choice, edges, precision=lax.Precision.HIGHEST)
    forcing_cols = jnp.einsum(
        "tflrk,kc->tflrc", edge_rows, col_choice, precision=lax.Precision.HIGHEST
    )
    row_depth = jnp.minimum(local_rows, total_rows - 1 - local_rows)
    col_depth = jnp.minimum(nest_cols, nest_width - 1 - nest_cols)
    row_zone = (row_depth < ZONE)[:, None]
    forcing = jnp.where(row_zone, forcing_rows, forcing_cols)
    depth = jnp.minimum(row_depth[:, None], col_depth[None, :])
    weight = jnp.maximum(ZONE - depth, 0).astype(jnp.float32) / ZONE

    def relax(values, substep):
        fraction = (substep + 1) / RATIO
        target = forcing[0] + fraction * (forcing[1] - forcing[0])
        return values + weight * (target - values)

    nest_field = relax(stepped, 0)
    for substep in range(1, RATIO):
        nest_field = relax(step(nest_field), substep)
    block_means = nest_field.reshape(fields, levels, coarse_rows, RATIO, third_width, RATIO).sum(
        axis=(3, 5)
    ) / (RATIO * RATIO)
    wanted_nest = local_rows - offset
    portion = lax.all_gather(block_means, "tile", axis=2, tiled=True)
    row_span = portion.shape[2]
    select = (wanted_nest[:, None] == jnp.arange(row_span, dtype=jnp.int32)[None, :]).astype(
        jnp.float32
    )
    gathered = jnp.einsum("rs,flsc->flrc", select, portion, precision=lax.Precision.HIGHEST)
    target_slot = jnp.where(is_parent, -1, (section - parent_count) // RATIO)
    slot_index = jnp.arange(section_count, dtype=jnp.int32)
    outbound = jnp.where(
        (slot_index == target_slot)[None, None, None, :, None], gathered[:, :, :, None, :], 0.0
    )
    outbound = outbound.reshape(fields, levels, row_count, section_count * third_width)
    received_means = lax.all_to_all(outbound, "section", split_axis=3, concat_axis=3, tiled=True)
    start_col = (parent_count + RATIO * jnp.minimum(section, parent_count - 1)) * third_width
    feedback = lax.dynamic_slice_in_dim(received_means, start_col, col_count, 3)
    covered = ((wanted_nest >= 0) & (wanted_nest < nest_height))[:, None]
    parent_final = jnp.where(covered, feedback, stepped)
    return jnp.where(is_parent, parent_final, nest_field)


ROWS = 24
COLS = 384
LANE = 128
STATES = 10
PLANES = 14
SLOTS = 4 * PLANES
HALO = SLOTS + 8
RIMS = 3 * ROWS
EXACT = lax.Precision.HIGHEST


def device(tile, section):
    return tile * 4 + section


def device_mark(tile, section):
    return (device(tile, section) + 1).astype(jnp.float32)


def third(value):
    return (value * 43) >> 7


def iota(shape, dim):
    return lax.broadcasted_iota(jnp.int32, shape, dim)


def dot(a, b):
    return jnp.dot(a, b, precision=EXACT, preferred_element_type=jnp.float32)


def turn(value, steps, dim):
    size = value.shape[dim]
    steps = steps % size
    return pltpu.roll(value, steps, dim) if steps else value


def plane_of(state_ref, courant_ref, p):
    return state_ref[p] if p < STATES else courant_ref[p - STATES]


def pack_kernel(offset_ref, state_ref, courant_ref, west_ref, middle_ref, east_ref):
    tile = lax.axis_index("tile")
    section = lax.axis_index("section")
    offset = offset_ref[0]
    first = tile * ROWS
    lane = iota((ROWS, LANE), 1)
    left = jnp.zeros((ROWS, LANE), jnp.float32)
    right = jnp.zeros((ROWS, LANE), jnp.float32)
    for p in range(PLANES):
        source = plane_of(state_ref, courant_ref, p)
        mine = (lane >= 3 * p) & (lane < 3 * p + 3)
        left = jnp.where(mine, turn(source[:, :LANE], 3 * p, 1), left)
        right = jnp.where(mine, turn(source[:, COLS - LANE :], 3 * p - (LANE - 3), 1), right)
    top = (first <= offset + 2) & (first + ROWS - 1 >= offset - 1)
    base = jnp.where(top, offset - 1, offset + 61) - first

    def chosen(start, count):
        slot = iota((4 * count, ROWS * count), 0)
        column = iota((4 * count, ROWS * count), 1)
        local = base + (slot & 3)
        hit = (local >= 0) & (local < ROWS) & (column == (slot >> 2) * ROWS + local)
        return hit.astype(jnp.float32)

    rows = jnp.concatenate(
        [
            dot(chosen(0, STATES), state_ref[...].reshape(STATES * ROWS, COLS)),
            dot(chosen(0, 4), courant_ref[...].reshape(4 * ROWS, COLS)),
        ],
        axis=0,
    )
    lane = iota((SLOTS, LANE), 1)
    mark = device_mark(tile, section)
    blank = jnp.zeros((SLOTS, LANE), jnp.float32)
    outs = ((west_ref, left), (middle_ref, left), (east_ref, right))
    for s, (out_ref, edge) in enumerate(outs):
        before = rows[:, LANE * (s - 1) : LANE * s] if s > 0 else blank
        after = rows[:, LANE * (s + 1) : LANE * (s + 2)] if s < 2 else blank
        extra = turn(jnp.where(lane < 2, after, before), 44, 1)
        side = jnp.where(
            (lane >= 42) & (lane < 46), extra, jnp.where(lane == LANE - 1, mark, 0.0)
        )
        out_ref[:, :LANE] = rows[:, LANE * s : LANE * (s + 1)]
        out_ref[:ROWS, LANE:] = jnp.where(lane[:ROWS] < 42, edge, side[:ROWS])
        out_ref[ROWS:, LANE:] = side[ROWS:]


def first_source(offset, tile):
    return jnp.maximum((offset - 2) // ROWS, 1) - 1 + jnp.minimum(tile // 2, 2)


def relay_kernel(middles, offset_ref, state_ref, courant_ref, *refs):
    to_east, middle, to_west = refs[:3], refs[3 : 3 + middles], refs[3 + middles : 6 + middles]
    west_ref, east_ref, rims_ref, pair_ref, cross_ref = refs[6 + middles :]
    tile = lax.axis_index("tile")
    section = lax.axis_index("section")
    even = tile % 2 == 0
    lane = iota((ROWS, LANE), 1)
    first = first_source(offset_ref[0], tile)
    sources = [device_mark(first + slot, 0) for slot in range(3)]

    def marked(refs, mark):
        total = jnp.zeros((ROWS, LANE), jnp.float32)
        for ref in refs:
            total += jnp.where(ref[:ROWS, 2 * LANE - 1 :] == mark, ref[:ROWS, LANE:], 0.0)
        return jnp.where(lane < 42, total, 0.0)

    has_east = (section == 1) | (section == 2)
    has_west = (section == 2) | (section == 3)
    east = marked(to_west, jnp.where(has_east, device_mark(tile, section + 1), 0.0))
    west = marked(to_east, jnp.where(has_west, device_mark(tile, section - 1), 0.0))
    west_ref[...] = west
    east_ref[...] = east
    rows = jnp.zeros((SLOTS, 2 * LANE), jnp.float32)
    edges = [jnp.zeros((ROWS, LANE), jnp.float32)] * 3
    for refs_in, target in ((to_west, 1), (middle, 2), (to_east, 3)):
        marks = [jnp.where(section == target, mark, 0.0) for mark in sources]
        for ref in refs_in:
            value = ref[...]
            mark = value[:, 2 * LANE - 1 :]
            for source in marks:
                rows += jnp.where(mark == source, value, 0.0)
        if target != 2:
            edges = [edge + marked(refs_in, mark) for edge, mark in zip(edges, marks)]
    wide = iota((SLOTS, LANE), 1)
    rims_ref[:SLOTS, :LANE] = rows[:, :LANE]
    rims_ref[SLOTS:, :LANE] = jnp.zeros((RIMS - SLOTS, LANE), jnp.float32)
    extra = jnp.where((wide >= 42) & (wide < 46), rows[:, LANE:], 0.0)
    extra = jnp.concatenate([extra, jnp.zeros((RIMS - SLOTS, LANE), jnp.float32)], axis=0)
    rims_ref[:, LANE:] = jnp.concatenate(edges, axis=0) + extra

    def put(rows, lanes, value):
        head, tail = value[:4], value[ROWS - 4 :]
        pair_ref[rows, lanes] = jnp.where(even, tail, head)
        cross_ref[rows, lanes] = jnp.where(even, head, tail)

    for p in range(PLANES):
        put(slice(4 * p, 4 * p + 4), slice(None), plane_of(state_ref, courant_ref, p))
    put(slice(SLOTS, SLOTS + 4), slice(0, LANE), west)
    put(slice(SLOTS, SLOTS + 4), slice(LANE, 2 * LANE), east)
    pair_ref[HALO:, : 2 * LANE] = rims_ref[...]
    cross_ref[HALO:, :LANE] = edges[0]


def flux(value, south, north, west, east, other, cy, cx):
    transport = (
        jnp.maximum(cy, 0.0) * (value - south)
        + jnp.minimum(cy, 0.0) * (north - value)
        + jnp.maximum(cx, 0.0) * (value - west)
        + jnp.minimum(cx, 0.0) * (east - value)
    )
    spread = south + north + west + east - 4.0 * value
    return diffusion * spread + mixing * (other - value) - transport


def main_kernel(
    offset_ref,
    state_ref,
    courant_ref,
    west_ref,
    east_ref,
    rims_ref,
    pair_ref,
    cross_ref,
    out_ref,
    means_ref,
    here,
    there,
    factors,
    base_force,
    step_force,
    narrowed,
):
    tile = lax.axis_index("tile")
    section = lax.axis_index("section")
    offset = offset_ref[0]
    even = tile % 2 == 0
    is_nest = section > 0
    full = (32, 4 * LANE)

    after = jnp.where(even, pair_ref[:HALO], cross_ref[:HALO])
    before = jnp.where(even, cross_ref[:HALO], pair_ref[:HALO])
    wests = jnp.concatenate(
        [west_ref[...], after[SLOTS : SLOTS + 4, :LANE], before[SLOTS : SLOTS + 4, :LANE]], axis=0
    )
    easts = jnp.concatenate(
        [
            east_ref[...],
            after[SLOTS : SLOTS + 4, LANE : 2 * LANE],
            before[SLOTS : SLOTS + 4, LANE : 2 * LANE],
        ],
        axis=0,
    )
    lane = iota((32, LANE), 1)

    def ring(p):
        tail = jnp.concatenate([after[4 * p : 4 * p + 4], before[4 * p : 4 * p + 4]], axis=0)
        cells = jnp.concatenate([plane_of(state_ref, courant_ref, p), tail], axis=0)
        outside = jnp.where(
            lane < 3,
            turn(easts, -3 * p, 1),
            jnp.where(lane >= LANE - 3, turn(wests, LANE - 3 - 3 * p, 1), 0.0),
        )
        return jnp.concatenate([cells, outside], axis=1)

    for p in range(STATES):
        here[p] = ring(p)

    row = iota(full, 0)
    column = iota(full, 1)
    near_row = jnp.where(row < 28, row, row - 32)
    near_column = jnp.where(column < 448, column, column - 512)
    grid_row = near_row + tile * ROWS
    grid_column = near_column + (section - 1) * COLS
    row_depth = jnp.minimum(grid_row, 8 * ROWS - 1 - grid_row)
    column_depth = jnp.minimum(grid_column, 3 * COLS - 1 - grid_column)
    depth = jnp.maximum(jnp.minimum(row_depth, column_depth), 0)
    weight = jnp.maximum(ZONE - depth, 0).astype(jnp.float32) / ZONE
    weight = jnp.where(is_nest, weight, 0.0)
    keep = 1.0 - weight
    no_south = row == jnp.where(tile == 0, 0, -1)
    no_north = row == jnp.where(tile == 7, ROWS - 1, -1)
    no_west = column == jnp.where(section < 2, 0, -1)
    no_east = column == jnp.where((section == 0) | (section == 3), COLS - 1, -1)
    for level in range(2):
        cy = ring(STATES + level)
        cx = ring(STATES + 2 + level)
        from_south = jnp.maximum(cy, 0.0) + diffusion
        from_north = diffusion - jnp.minimum(cy, 0.0)
        from_west = jnp.maximum(cx, 0.0) + diffusion
        from_east = diffusion - jnp.minimum(cx, 0.0)
        from_south = jnp.where(no_south, 0.0, from_south)
        from_north = jnp.where(no_north, 0.0, from_north)
        from_west = jnp.where(no_west, 0.0, from_west)
        from_east = jnp.where(no_east, 0.0, from_east)
        own = (1.0 - mixing) - (from_south + from_north + from_west + from_east)
        factors[level, 0] = own * keep
        factors[level, 1] = from_south * keep
        factors[level, 2] = from_north * keep
        factors[level, 3] = from_west * keep
        factors[level, 4] = from_east * keep
    factors[0, 5] = mixing * keep

    base_force[...] = jnp.zeros(base_force.shape, jnp.float32)
    step_force[...] = jnp.zeros(step_force.shape, jnp.float32)
    rims = rims_ref[...] + pair_ref[HALO:, : 2 * LANE]

    @pl.when((section == 1) | (section == 3))
    def _():
        on_left = section == 1
        before_six = jnp.where(tile == 6, cross_ref[HALO:, :LANE], 0.0)
        edges = jnp.concatenate([rims[:ROWS, LANE:] + before_six, rims[ROWS:, LANE:]], axis=0)
        source_tile = first_source(offset, tile)
        pick = iota((96, RIMS), 0)
        part = pick >> 5
        near = pick & 31
        near = jnp.where(near < 28, near, near - 32)
        coarse = offset + tile * 8 + third(near + 6) - 2 + part - 1 - source_tile * ROWS
        picked = dot((iota((96, RIMS), 1) == coarse).astype(jnp.float32), edges)
        south, value, north = picked[:32], picked[32:64], picked[64:]
        place = lane - 3 * third(lane)
        west = jnp.where(place == jnp.where(on_left, 0, -1), value, turn(value, 1, 1))
        east = jnp.where(place == jnp.where(on_left, -1, 2), value, turn(value, -1, 1))
        other = jnp.where((third(lane) & 1) == 0, turn(value, -3, 1), turn(value, 3, 1))
        cy = jnp.zeros((32, LANE), jnp.float32)
        cx = jnp.zeros((32, LANE), jnp.float32)
        for field in range(STATES // 2):
            mine = (lane >= 6 * field) & (lane < 6 * field + 6)
            cy = jnp.where(mine, turn(value, 6 * field - 3 * STATES, 1), cy)
            cx = jnp.where(mine, turn(value, 6 * field - 3 * STATES - 6, 1), cx)
        change = flux(value, south, north, west, east, other, cy, cx) / RATIO
        out = iota((LANE, STATES * LANE), 1)
        spot = out & (LANE - 1)
        wanted = 3 * (out >> 7) + jnp.where(on_left, third(spot), third(spot - 119))
        start = jnp.where(on_left, 0, LANE - 6)
        valid = (spot >= start) & (spot < start + 6)
        spread = (valid & (iota((LANE, STATES * LANE), 0) == wanted)).astype(jnp.float32)
        forced = dot(jnp.concatenate([value, change], axis=0), spread)

        def place_side(lanes):
            for p in range(STATES):
                block = forced[:, p * LANE : (p + 1) * LANE]
                base_force[p, :, lanes] = weight[:, lanes] * block[:32]
                step_force[p, :, lanes] = weight[:, lanes] * block[32:]

        @pl.when(on_left)
        def _():
            place_side(slice(0, LANE))

        @pl.when(jnp.logical_not(on_left))
        def _():
            place_side(slice(2 * LANE, 3 * LANE))

    @pl.when(is_nest & ((tile == 0) | (tile == 7)))
    def _():
        rows = rims[:SLOTS]
        wide = iota((8, 2 * LANE), 1)
        narrow = iota((SLOTS, LANE), 1)
        outside = turn(rows[:, LANE:], 84, 1)
        outside = jnp.where((narrow < 2) | (narrow >= LANE - 2), outside, 0.0)
        rows = jnp.concatenate([rows[:, :LANE], outside], axis=1)
        cy = rows[4 * STATES : 4 * STATES + 8]
        cx = rows[4 * STATES + 8 :]
        changes = []
        for field in range(STATES // 2):
            value = rows[8 * field : 8 * field + 8]
            west = jnp.where(wide == jnp.where(section == 1, 0, -1), value, turn(value, 1, 1))
            east = jnp.where(wide == jnp.where(section == 3, LANE - 1, -1), value, turn(value, -1, 1))
            changes.append(
                flux(
                    value,
                    turn(value, 1, 0),
                    turn(value, -1, 0),
                    west,
                    east,
                    turn(value, 4, 0),
                    cy,
                    cx,
                )
                / RATIO
            )
        both = jnp.concatenate([rows[: 4 * STATES]] + changes, axis=0)
        target = iota((2 * LANE, 4 * LANE), 1)
        target = jnp.where(target < 448, target, target - 512)
        coarse = (((target + 66) * 171) >> 9) - 22
        spread = (iota((2 * LANE, 4 * LANE), 0) == (coarse & (2 * LANE - 1))).astype(jnp.float32)
        forced = dot(both, spread)
        eight = iota((8, 4 * LANE), 0)

        def place_rows(rows, split):
            zone = jnp.where(split == 3, eight < ZONE, eight >= 8 - ZONE)
            for p in range(STATES):
                for ref, start in ((base_force, 0), (step_force, 4 * STATES)):
                    spot = start + 4 * p
                    value = jnp.where(eight < split, forced[spot + 1 : spot + 2], forced[spot + 2 : spot + 3])
                    ref[p, rows, :] = jnp.where(zone, weight[rows] * value, ref[p, rows, :])

        @pl.when(tile == 0)
        def _():
            place_rows(slice(0, 8), 3)

        @pl.when(tile == 7)
        def _():
            place_rows(slice(16, 24), 5)

    def substep(source, target, number):
        def per_field(field, carry):
            values = [source[2 * field + level] for level in range(2)]
            for level in range(2):
                value = values[level]
                result = factors[level, 0] * value + factors[0, 5] * values[1 - level]
                result += factors[level, 1] * turn(value, 1, 0)
                result += factors[level, 2] * turn(value, -1, 0)
                result += factors[level, 3] * turn(value, 1, 1)
                result += factors[level, 4] * turn(value, -1, 1)
                p = 2 * field + level
                result += base_force[p] + float(number) * step_force[p]
                target[p] = result
            return carry

        lax.fori_loop(0, STATES // 2, per_field, 0)

    substep(here, there, 1)

    @pl.when(is_nest)
    def _():
        substep(there, here, 2)
        substep(here, there, 3)

    out_ref[...] = there[:, :ROWS, :COLS]
    columns = iota((COLS, LANE), 1) * RATIO
    source = iota((COLS, LANE), 0)
    gather = ((source >= columns) & (source < columns + RATIO)).astype(jnp.float32)
    narrowed[...] = dot(out_ref[...].reshape(STATES * ROWS, COLS), gather)
    total = sum(narrowed[pl.ds(i, STATES * 8, stride=RATIO), :] for i in range(RATIO))
    means_ref[...] = total / (RATIO * RATIO)


def merge_kernel(offset_ref, *refs):
    *block_refs, stepped_ref, out_ref, near = refs
    tile = lax.axis_index("tile")
    section = lax.axis_index("section")
    offset = offset_ref[0]
    rest = offset % 8

    @pl.when(section > 0)
    def _():
        out_ref[...] = stepped_ref[...]

    @pl.when(section == 0)
    def _():
        for step in range(4):
            source = 3 * tile - offset // 8 - 1 + step
            inside = (source >= 0) & (source < 8)
            for way, block_ref in enumerate(block_refs):

                @pl.when(inside & (source == (tile ^ way)))
                def _():
                    near[step] = block_ref[...]

        nest_row = tile * ROWS + iota((ROWS, COLS), 0) - offset
        covered = (nest_row >= 0) & (nest_row < 64)
        for p in range(STATES):
            parts = [near[step, 8 * p : 8 * p + 8] for step in range(4)]
            moved = pltpu.roll(jnp.concatenate(parts, axis=0), rest + 24, 0)
            out_ref[p] = jnp.where(covered, moved[:ROWS], stepped_ref[p])


VMEM = pl.BlockSpec(memory_space=pltpu.VMEM)
SMEM = pl.BlockSpec(memory_space=pltpu.SMEM)


def shaped(*shape):
    return jax.ShapeDtypeStruct(shape, jnp.float32)


def in_rounds(edges, count):
    at = {}
    for source, target in edges:
        mine, theirs = ("from", source), ("to", target)
        a = next(c for c in range(count) if (mine, c) not in at)
        b = next(c for c in range(count) if (theirs, c) not in at)
        path = []
        node, color = theirs, a
        while (node, color) in at:
            node_next = at[(node, color)]
            path.append((node, node_next, color))
            node, color = node_next, (b if color == a else a)
        for one, two, color in path:
            del at[(one, color)], at[(two, color)]
        for one, two, color in path:
            swapped = b if color == a else a
            at[(one, swapped)] = two
            at[(two, swapped)] = one
        at[(mine, a)] = theirs
        at[(theirs, a)] = mine
    rounds = [[] for _ in range(count)]
    for (node, color), other in sorted(at.items()):
        if node[0] == "from":
            rounds[color].append((node[1], other[1]))
    return rounds


def hops(one, two):
    (t, s), (u, r) = divmod(one, 4), divmod(two, 4)
    links = abs((t >> 2) - (u >> 2)) + abs(((t >> 1) & 1) - ((u >> 1) & 1)) + abs(s - r)
    return links or 0.3


def completed(pairs, valid):
    senders = [d for d in range(32) if d not in {a for a, _ in pairs}]
    takers = [d for d in range(32) if d not in {b for _, b in pairs}]

    def cost(a, b):
        from_parent = a % 4 == 0 and b % 4 > 0
        return 1e3 if a == b or from_parent or (a, b) in valid else hops(a, b) ** 2

    n = len(senders)
    row_price, column_price = [0.0] * (n + 1), [0.0] * (n + 1)
    owner = [0] * (n + 1)
    for i in range(1, n + 1):
        owner[0] = i
        column = 0
        least, before, used = [1e9] * (n + 1), [0] * (n + 1), [False] * (n + 1)
        while True:
            used[column] = True
            row, step, best = owner[column], 1e9, 0
            for j in range(1, n + 1):
                if not used[j]:
                    gap = cost(senders[row - 1], takers[j - 1]) - row_price[row] - column_price[j]
                    if gap < least[j]:
                        least[j], before[j] = gap, column
                    if least[j] < step:
                        step, best = least[j], j
            for j in range(n + 1):
                if used[j]:
                    row_price[owner[j]] += step
                    column_price[j] -= step
                else:
                    least[j] -= step
            column = best
            if owner[column] == 0:
                break
        while column:
            owner[column], column = owner[before[column]], before[column]
    return pairs + [(senders[owner[j] - 1], takers[j - 1]) for j in range(1, n + 1)]


def rim_pairs(start):
    to_chips = [(0, 0), (1, 1), (0, 2), (1, 3), (2, 3), (2, 4), (1, 5), (3, 4), (2, 6), (3, 7)]
    sends = [(start + step, tile) for step, tile in to_chips]
    middle = [[(start, 0), (start + 1, 1), (start + 2, 6), (start + 3, 7)]]
    if start == 1:
        sends.append((0, 0))
        middle.append([(0, 0)])
    groups = []
    for section, inner in ((1, ((2, 1), (3, 2))), (3, ((1, 2), (2, 3)))):
        edges = [(device(a, 0), device(b, section)) for a, b in sends]
        edges += [(device(t, a), device(t, b)) for t in range(8) for a, b in inner]
        rounds = in_rounds(edges, 3)[::-1]
        groups.append([completed(pairs, edges) for pairs in rounds])
    middle = [[(device(a, 0), device(b, 2)) for a, b in pairs] for pairs in middle]
    middle = [completed(pairs, []) for pairs in middle]
    return groups[0], middle, groups[1]


BOTH = ("tile", "section")


def on_device(state, courant, nest_offset):
    planes = state.reshape(STATES, ROWS, COLS)
    speeds = courant.reshape(4, ROWS, COLS)
    offset = nest_offset[0]
    payloads = pl.pallas_call(
        pack_kernel,
        out_shape=[shaped(SLOTS, 2 * LANE)] * 3,
        in_specs=[SMEM, VMEM, VMEM],
        out_specs=[VMEM] * 3,
        name="pack",
    )(nest_offset, planes, speeds)

    def send_rims(start, nest_offset, planes, speeds, west, middle, east):
        groups = rim_pairs(start)
        west, middle, east = (
            [lax.ppermute(value, BOTH, pairs) for pairs in lists]
            for value, lists in zip((west, middle, east), groups)
        )
        return pl.pallas_call(
            functools.partial(relay_kernel, len(middle)),
            out_shape=[
                shaped(ROWS, LANE),
                shaped(ROWS, LANE),
                shaped(RIMS, 2 * LANE),
                shaped(HALO + RIMS, COLS),
                shaped(HALO + ROWS, COLS),
            ],
            in_specs=[SMEM] + [VMEM] * (8 + len(middle)),
            out_specs=[VMEM] * 5,
            name="relay",
        )(nest_offset, planes, speeds, *east, *middle, *west)

    west, east, rims, to_pair, to_cross = lax.switch(
        (offset - 2) // ROWS - 1,
        [functools.partial(send_rims, start) for start in (1, 2, 3)],
        nest_offset,
        planes,
        speeds,
        *payloads,
    )
    pair_map = [(device(t, s), device(t ^ 1, s)) for t in range(8) for s in range(4)]
    cross_map = [
        (device(a, s), device(b, s))
        for low in (1, 3, 5, 7)
        for a, b in ((low, (low + 1) % 8), ((low + 1) % 8, low))
        for s in range(4)
    ]
    from_cross = lax.ppermute(to_cross, BOTH, cross_map)
    from_pair = lax.ppermute(to_pair, BOTH, pair_map)
    block, means = pl.pallas_call(
        main_kernel,
        out_shape=[shaped(STATES, ROWS, COLS), shaped(STATES * 8, LANE)],
        in_specs=[SMEM] + [VMEM] * 7,
        out_specs=[VMEM] * 2,
        scratch_shapes=[
            pltpu.VMEM((STATES, 32, 4 * LANE), jnp.float32),
            pltpu.VMEM((STATES, 32, 4 * LANE), jnp.float32),
            pltpu.VMEM((2, 6, 32, 4 * LANE), jnp.float32),
            pltpu.VMEM((STATES, 32, 4 * LANE), jnp.float32),
            pltpu.VMEM((STATES, 32, 4 * LANE), jnp.float32),
            pltpu.VMEM((STATES * ROWS, LANE), jnp.float32),
        ],
        compiler_params=pltpu.CompilerParams(vmem_limit_bytes=32 * 1024 * 1024),
        name="nest",
    )(nest_offset, planes, speeds, west, east, rims, from_pair, from_cross)
    columns = jnp.concatenate(
        [
            lax.ppermute(means, BOTH, [(device(t, s), device(t, 0)) for t in range(8)])
            for s in (1, 2, 3)
        ],
        axis=1,
    )

    def across(value, way):
        pairs = [(device(t, s), device(t ^ way, s)) for t in range(8) for s in range(4)]
        return lax.ppermute(value, BOTH, pairs)

    blocks = {0: columns}
    for way in (7, 3, 4, 1):
        blocks[way] = across(columns, way)
    for way in (7, 3, 4):
        blocks[way ^ 1] = across(blocks[way], 1)
    merged = pl.pallas_call(
        merge_kernel,
        out_shape=shaped(STATES, ROWS, COLS),
        in_specs=[SMEM] + [VMEM] * 9,
        out_specs=VMEM,
        scratch_shapes=[pltpu.VMEM((4, STATES * 8, COLS), jnp.float32)],
        compiler_params=pltpu.CompilerParams(vmem_limit_bytes=32 * 1024 * 1024),
        name="merge",
    )(nest_offset, *[blocks[way] for way in range(8)], block)
    return merged.reshape(state.shape)


def solution(mesh):
    small = mesh.shape["tile"] == 8 and mesh.shape["section"] == 4
    return jax.shard_map(
        on_device if small else general_on_device,
        mesh=mesh,
        in_specs=(P(None, None, "tile", "section"), P(None, None, "tile", "section"), P()),
        out_specs=P(None, None, "tile", "section"),
        check_vma=False,
    )
```

```python
import functools

import jax
import jax.numpy as jnp
from jax import lax
from jax.experimental import pallas as pl
from jax.experimental.pallas import tpu as pltpu
from jax.sharding import PartitionSpec as P

RATIO = 3
ZONE = 5


diffusion = 0.02
mixing = 0.05


def shifted(value, axis, steps):
    count = lax.axis_size(axis)
    leading, last = (max(0, -steps), min(count, count - steps))
    return lax.ppermute(value, axis, [(source, source + steps) for source in range(leading, last)])


def with_halo(block, sides, width):
    for axis, dim in sides:
        count = lax.axis_size(axis)
        forward = [(i, i + 1) for i in range(count - 1)]
        backward = [(target, source) for source, target in forward]
        low = lax.ppermute(
            lax.slice_in_dim(block, block.shape[dim] - width, None, axis=dim), axis, forward
        )
        high = lax.ppermute(lax.slice_in_dim(block, 0, width, axis=dim), axis, backward)
        block = jnp.concatenate([low, block, high], axis=dim)
    return block


def advance(values, courant, padded, low_row, high_row, low_col, high_col):
    row_count = values.shape[2]
    col_count = values.shape[3]
    row_index = lax.broadcasted_iota(jnp.int32, (1, 1, row_count, col_count), 2)
    column_index = lax.broadcasted_iota(jnp.int32, (1, 1, row_count, col_count), 3)
    south_side = jnp.where(low_row & (row_index == 0), values, padded[:, :, :-2, 1:-1])
    north_side = jnp.where(high_row & (row_index == row_count - 1), values, padded[:, :, 2:, 1:-1])
    west_side = jnp.where(low_col & (column_index == 0), values, padded[:, :, 1:-1, :-2])
    east_side = jnp.where(
        high_col & (column_index == col_count - 1), values, padded[:, :, 1:-1, 2:]
    )
    stacked = jnp.pad(values, ((0, 0), (1, 1), (0, 0), (0, 0)), mode="edge")
    level_below = stacked[:, :-2]
    level_above = stacked[:, 2:]
    speed_y = courant[0]
    speed_x = courant[1]
    transport = (
        jnp.maximum(speed_y, 0.0) * (values - south_side)
        + jnp.minimum(speed_y, 0.0) * (north_side - values)
        + jnp.maximum(speed_x, 0.0) * (values - west_side)
        + jnp.minimum(speed_x, 0.0) * (east_side - values)
    )
    spread = south_side + north_side + west_side + east_side - 4.0 * values
    column = level_below + level_above - 2.0 * values
    return values - transport + diffusion * spread + mixing * column


def send_rims(values, distance):
    return shifted(values, "section", distance)


def general_on_device(state, courant, nest_offset):
    fields, levels, row_count, col_count = state.shape
    tile_count = lax.axis_size("tile")
    section_count = lax.axis_size("section")
    parent_count = section_count // 4
    tile_index = lax.axis_index("tile")
    section = lax.axis_index("section")
    offset = nest_offset[0]
    total_rows = row_count * tile_count
    nest_height = total_rows // RATIO
    third_width = col_count // RATIO
    coarse_rows = row_count // RATIO
    parent_width = parent_count * col_count
    nest_width = section_count * col_count - parent_width
    is_parent = section < parent_count
    low_row = tile_index == 0
    high_row = tile_index == tile_count - 1
    low_col = (section == 0) | (section == parent_count)
    high_col = (section == parent_count - 1) | (section == section_count - 1)

    def step(values):
        padded = with_halo(values, (("tile", 2), ("section", 3)), 1)
        return advance(values, courant, padded, low_row, high_row, low_col, high_col)

    stepped = step(state)
    local_rows = tile_index * row_count + jnp.arange(row_count, dtype=jnp.int32)
    rim_coarse = jnp.array([0, 1, nest_height - 2, nest_height - 1], dtype=jnp.int32)
    wanted = offset + rim_coarse
    pick_rows = (wanted[:, None] == local_rows[None, :]).astype(jnp.float32)
    parent_flag = is_parent.astype(jnp.float32)
    both_states = jnp.stack([state, stepped]) * parent_flag
    rim_part = jnp.einsum(
        "jr,tflrc->tfljc", pick_rows, both_states, precision=lax.Precision.HIGHEST
    )
    edge_cols = jnp.array([0, 1, parent_width - 2, parent_width - 1], dtype=jnp.int32)
    global_cols = section * col_count + jnp.arange(col_count, dtype=jnp.int32)
    pick_edge = (global_cols[:, None] == edge_cols[None, :]).astype(jnp.float32)
    edge_local = jnp.einsum(
        "tflrc,ck->tflrk", both_states, pick_edge, precision=lax.Precision.HIGHEST
    )
    span_rows = offset + jnp.arange(nest_height, dtype=jnp.int32)
    pick_span = (span_rows[:, None] == local_rows[None, :]).astype(jnp.float32)
    edge_part = jnp.einsum(
        "nr,tflrk->tflnk", pick_span, edge_local, precision=lax.Precision.HIGHEST
    )
    packed = jnp.concatenate(
        [
            rim_part.reshape(2 * fields * levels, 4 * col_count),
            edge_part.reshape(2 * fields * levels, nest_height * 4),
        ],
        axis=1,
    )
    summed = lax.psum(packed, "tile")
    nest_index = jnp.maximum(section - parent_count, 0)
    source_parent = nest_index // RATIO
    received = jnp.zeros_like(summed)
    for distance in range(parent_count, 3 * parent_count + 1):
        arrived = send_rims(summed, distance)
        hit = jnp.logical_not(is_parent) & (section - distance == source_parent)
        received = jnp.where(hit, arrived, received)
    rim_rows = received[:, : 4 * col_count].reshape(2, fields, levels, 4, col_count)
    edges = received[:, 4 * col_count :].reshape(2, fields, levels, nest_height, 4)
    rim_strip = lax.dynamic_slice_in_dim(rim_rows, nest_index % RATIO * third_width, third_width, 4)
    rim_strip = jnp.repeat(rim_strip, RATIO, axis=4)
    row_choice = ((local_rows // RATIO)[:, None] == rim_coarse[None, :]).astype(jnp.float32)
    forcing_rows = jnp.einsum(
        "rj,tfljc->tflrc", row_choice, rim_strip, precision=lax.Precision.HIGHEST
    )
    nest_cols = nest_index * col_count + jnp.arange(col_count, dtype=jnp.int32)
    col_choice = (edge_cols[:, None] == (nest_cols // RATIO)[None, :]).astype(jnp.float32)
    coarse_choice = (
        (local_rows // RATIO)[:, None] == jnp.arange(nest_height, dtype=jnp.int32)[None, :]
    ).astype(jnp.float32)
    edge_rows = jnp.einsum("rn,tflnk->tflrk", coarse_choice, edges, precision=lax.Precision.HIGHEST)
    forcing_cols = jnp.einsum(
        "tflrk,kc->tflrc", edge_rows, col_choice, precision=lax.Precision.HIGHEST
    )
    row_depth = jnp.minimum(local_rows, total_rows - 1 - local_rows)
    col_depth = jnp.minimum(nest_cols, nest_width - 1 - nest_cols)
    row_zone = (row_depth < ZONE)[:, None]
    forcing = jnp.where(row_zone, forcing_rows, forcing_cols)
    depth = jnp.minimum(row_depth[:, None], col_depth[None, :])
    weight = jnp.maximum(ZONE - depth, 0).astype(jnp.float32) / ZONE

    def relax(values, substep):
        fraction = (substep + 1) / RATIO
        target = forcing[0] + fraction * (forcing[1] - forcing[0])
        return values + weight * (target - values)

    nest_field = relax(stepped, 0)
    for substep in range(1, RATIO):
        nest_field = relax(step(nest_field), substep)
    block_means = nest_field.reshape(fields, levels, coarse_rows, RATIO, third_width, RATIO).sum(
        axis=(3, 5)
    ) / (RATIO * RATIO)
    wanted_nest = local_rows - offset
    portion = lax.all_gather(block_means, "tile", axis=2, tiled=True)
    row_span = portion.shape[2]
    select = (wanted_nest[:, None] == jnp.arange(row_span, dtype=jnp.int32)[None, :]).astype(
        jnp.float32
    )
    gathered = jnp.einsum("rs,flsc->flrc", select, portion, precision=lax.Precision.HIGHEST)
    target_slot = jnp.where(is_parent, -1, (section - parent_count) // RATIO)
    slot_index = jnp.arange(section_count, dtype=jnp.int32)
    outbound = jnp.where(
        (slot_index == target_slot)[None, None, None, :, None], gathered[:, :, :, None, :], 0.0
    )
    outbound = outbound.reshape(fields, levels, row_count, section_count * third_width)
    received_means = lax.all_to_all(outbound, "section", split_axis=3, concat_axis=3, tiled=True)
    start_col = (parent_count + RATIO * jnp.minimum(section, parent_count - 1)) * third_width
    feedback = lax.dynamic_slice_in_dim(received_means, start_col, col_count, 3)
    covered = ((wanted_nest >= 0) & (wanted_nest < nest_height))[:, None]
    parent_final = jnp.where(covered, feedback, stepped)
    return jnp.where(is_parent, parent_final, nest_field)


ROWS = 24
COLS = 384
LANE = 128
STATES = 10
PLANES = 14
SLOTS = 4 * PLANES
HALO = SLOTS + 8
RIMS = 3 * ROWS


def device(tile, section):
    return tile * 4 + section


def device_mark(tile, section):
    return (device(tile, section) + 1).astype(jnp.float32)


def third(value):
    return (value * 43) >> 7


def iota(shape, dim):
    return lax.broadcasted_iota(jnp.int32, shape, dim)


def parts(value):
    high = value.astype(jnp.bfloat16)
    rest = value - high.astype(jnp.float32)
    middle = rest.astype(jnp.bfloat16)
    return high, middle, (rest - middle.astype(jnp.float32)).astype(jnp.bfloat16)


def product(a, b):
    return jnp.dot(a, b, preferred_element_type=jnp.float32)


def choose(ones, value):
    return sum(product(ones.astype(jnp.bfloat16), part) for part in parts(value))


def turn(value, steps, dim):
    size = value.shape[dim]
    steps = steps % size
    return pltpu.roll(value, steps, dim) if steps else value


def plane_of(state_ref, courant_ref, p):
    return state_ref[p] if p < STATES else courant_ref[p - STATES]


def pack_kernel(
    offset_ref, state_ref, courant_ref, west_ref, middle_ref, east_ref, pair_ref, cross_ref
):
    tile = lax.axis_index("tile")
    section = lax.axis_index("section")
    offset = offset_ref[0]
    first = tile * ROWS
    lane = iota((ROWS, LANE), 1)
    left = jnp.zeros((ROWS, LANE), jnp.float32)
    right = jnp.zeros((ROWS, LANE), jnp.float32)
    for p in range(PLANES):
        source = plane_of(state_ref, courant_ref, p)
        mine = (lane >= 3 * p) & (lane < 3 * p + 3)
        left = jnp.where(mine, turn(source[:, :LANE], 3 * p, 1), left)
        right = jnp.where(mine, turn(source[:, COLS - LANE :], 3 * p - (LANE - 3), 1), right)
    top = (first <= offset + 2) & (first + ROWS - 1 >= offset - 1)
    base = jnp.where(top, offset - 1, offset + 61) - first

    def chosen(count):
        slot = iota((4 * count, ROWS * count), 0)
        column = iota((4 * count, ROWS * count), 1)
        local = base + (slot & 3)
        hit = (local >= 0) & (local < ROWS) & (column == (slot >> 2) * ROWS + local)
        return hit.astype(jnp.float32)

    rows = jnp.concatenate(
        [
            choose(chosen(STATES), state_ref[...].reshape(STATES * ROWS, COLS)),
            choose(chosen(4), courant_ref[...].reshape(4 * ROWS, COLS)),
        ],
        axis=0,
    )
    lane = iota((SLOTS, LANE), 1)
    mark = device_mark(tile, section)
    blank = jnp.zeros((SLOTS, LANE), jnp.float32)
    outs = ((west_ref, left), (middle_ref, left), (east_ref, right))
    for s, (out_ref, edge) in enumerate(outs):
        before = rows[:, LANE * (s - 1) : LANE * s] if s > 0 else blank
        after = rows[:, LANE * (s + 1) : LANE * (s + 2)] if s < 2 else blank
        extra = turn(jnp.where(lane < 2, after, before), 44, 1)
        side = jnp.where(
            (lane >= 42) & (lane < 46), extra, jnp.where(lane == LANE - 1, mark, 0.0)
        )
        out_ref[:, :LANE] = rows[:, LANE * s : LANE * (s + 1)]
        out_ref[:ROWS, LANE:] = jnp.where(lane[:ROWS] < 42, edge, side[:ROWS])
        out_ref[ROWS:, LANE:] = side[ROWS:]


    even = tile % 2 == 0
    for p in range(PLANES):
        source = plane_of(state_ref, courant_ref, p)
        head, tail = source[:4], source[ROWS - 4 :]
        pair_ref[4 * p : 4 * p + 4] = jnp.where(even, tail, head)
        cross_ref[4 * p : 4 * p + 4] = jnp.where(even, head, tail)


def first_source(start, tile):
    return start - 1 + jnp.minimum(tile // 2, 2)


def relay_kernel(start, middles, _, __, *refs):
    to_east, middle, to_west = refs[:3], refs[3 : 3 + middles], refs[3 + middles : 6 + middles]
    west_ref, east_ref, rims_ref, pair_ref, cross_ref = refs[6 + middles :]
    tile = lax.axis_index("tile")
    section = lax.axis_index("section")
    even = tile % 2 == 0
    lane = iota((ROWS, LANE), 1)
    first = first_source(start, tile)
    sources = [device_mark(first + slot, 0) for slot in range(3)]

    has_east = (section == 1) | (section == 2)
    has_west = (section == 2) | (section == 3)
    east_mark = jnp.where(has_east, device_mark(tile, section + 1), 0.0)
    west_mark = jnp.where(has_west, device_mark(tile, section - 1), 0.0)
    nothing = jnp.zeros((ROWS, LANE), jnp.float32)
    east = west = nothing
    edges = [nothing] * 3
    center = side = jnp.zeros((SLOTS, LANE), jnp.float32)
    targets = [3] * 3 + [2] * middles + [1] * 3
    for ref, target in zip(to_east + middle + to_west, targets):
        tail = ref[:, LANE:]
        mark = jnp.broadcast_to(tail[:, LANE - 1 :], (SLOTS, LANE))
        marks = [jnp.where(section == target, source, 0.0) for source in sources]
        hits = [mark == source for source in marks]
        hit = hits[0] | hits[1] | hits[2]
        center = jnp.where(hit, center + ref[:, :LANE], center)
        side = jnp.where(hit, side + tail, side)
        if target != 2:
            cells = tail[:ROWS]
            edges = [jnp.where(one[:ROWS], cells, edge) for one, edge in zip(hits, edges)]
        if target == 1:
            east = jnp.where(mark[:ROWS] == east_mark, cells, east)
        if target == 3:
            west = jnp.where(mark[:ROWS] == west_mark, cells, west)
    east, west, *edges = [jnp.where(lane < 42, value, 0.0) for value in (east, west, *edges)]
    west_ref[...] = west
    east_ref[...] = east
    wide = iota((SLOTS, LANE), 1)
    rims_ref[:SLOTS, :LANE] = center
    rims_ref[SLOTS:, :LANE] = jnp.zeros((RIMS - SLOTS, LANE), jnp.float32)
    extra = jnp.where((wide >= 42) & (wide < 46), side, 0.0)
    extra = jnp.concatenate([extra, jnp.zeros((RIMS - SLOTS, LANE), jnp.float32)], axis=0)
    rims_ref[:, LANE:] = jnp.concatenate(edges, axis=0) + extra

    for lanes, value in ((slice(0, LANE), west), (slice(LANE, 2 * LANE), east)):
        head, tail = value[:4], value[ROWS - 4 :]
        pair_ref[SLOTS : SLOTS + 4, lanes] = jnp.where(even, tail, head)
        cross_ref[SLOTS : SLOTS + 4, lanes] = jnp.where(even, head, tail)
    pair_ref[HALO:, : 2 * LANE] = rims_ref[...]
    cross_ref[HALO:, :LANE] = edges[0]


def flux(value, south, north, west, east, other, cy, cx):
    transport = (
        jnp.maximum(cy, 0.0) * (value - south)
        + jnp.minimum(cy, 0.0) * (north - value)
        + jnp.maximum(cx, 0.0) * (value - west)
        + jnp.minimum(cx, 0.0) * (east - value)
    )
    spread = south + north + west + east - 4.0 * value
    return diffusion * spread + mixing * (other - value) - transport


def main_kernel(
    offset_ref,
    state_ref,
    courant_ref,
    west_ref,
    east_ref,
    rims_ref,
    pair_ref,
    cross_ref,
    out_ref,
    means_ref,
    here,
    there,
    factors,
    column_force,
    row_force,
    narrowed,
):
    tile = lax.axis_index("tile")
    section = lax.axis_index("section")
    offset = offset_ref[0]
    even = tile % 2 == 0
    is_nest = section > 0
    full = (32, 4 * LANE)

    after = jnp.where(even, pair_ref[:HALO], cross_ref[:HALO])
    before = jnp.where(even, cross_ref[:HALO], pair_ref[:HALO])
    wests = jnp.concatenate(
        [west_ref[...], after[SLOTS : SLOTS + 4, :LANE], before[SLOTS : SLOTS + 4, :LANE]], axis=0
    )
    easts = jnp.concatenate(
        [
            east_ref[...],
            after[SLOTS : SLOTS + 4, LANE : 2 * LANE],
            before[SLOTS : SLOTS + 4, LANE : 2 * LANE],
        ],
        axis=0,
    )
    lane = iota((32, LANE), 1)

    def ring(p):
        tail = jnp.concatenate([after[4 * p : 4 * p + 4], before[4 * p : 4 * p + 4]], axis=0)
        cells = jnp.concatenate([plane_of(state_ref, courant_ref, p), tail], axis=0)
        outside = jnp.where(
            lane < 3,
            turn(easts, -3 * p, 1),
            jnp.where(lane >= LANE - 3, turn(wests, LANE - 3 - 3 * p, 1), 0.0),
        )
        return jnp.concatenate([cells, outside], axis=1)

    for p in range(STATES):
        here[p] = ring(p)

    row = iota(full, 0)
    column = iota(full, 1)
    near_row = jnp.where(row < 28, row, row - 32)
    near_column = jnp.where(column < 448, column, column - 512)
    grid_row = near_row + tile * ROWS
    grid_column = near_column + (section - 1) * COLS
    row_depth = jnp.minimum(grid_row, 8 * ROWS - 1 - grid_row)
    column_depth = jnp.minimum(grid_column, 3 * COLS - 1 - grid_column)
    depth = jnp.maximum(jnp.minimum(row_depth, column_depth), 0)
    weight = jnp.maximum(ZONE - depth, 0).astype(jnp.float32) / ZONE
    weight = jnp.where(is_nest, weight, 0.0)
    keep = 1.0 - weight
    no_south = row == jnp.where(tile == 0, 0, -1)
    no_north = row == jnp.where(tile == 7, ROWS - 1, -1)
    no_west = column == jnp.where(section < 2, 0, -1)
    no_east = column == jnp.where((section == 0) | (section == 3), COLS - 1, -1)
    for level in range(2):
        cy = ring(STATES + level)
        cx = ring(STATES + 2 + level)
        from_south = jnp.maximum(cy, 0.0) + diffusion
        from_north = diffusion - jnp.minimum(cy, 0.0)
        from_west = jnp.maximum(cx, 0.0) + diffusion
        from_east = diffusion - jnp.minimum(cx, 0.0)
        from_south = jnp.where(no_south, 0.0, from_south)
        from_north = jnp.where(no_north, 0.0, from_north)
        from_west = jnp.where(no_west, 0.0, from_west)
        from_east = jnp.where(no_east, 0.0, from_east)
        own = (1.0 - mixing) - (from_south + from_north + from_west + from_east)
        factors[level, 0] = own * keep
        factors[level, 1] = from_south * keep
        factors[level, 2] = from_north * keep
        factors[level, 3] = from_west * keep
        factors[level, 4] = from_east * keep
    factors[0, 5] = mixing * keep

    rims = rims_ref[...] + pair_ref[HALO:, : 2 * LANE]
    on_left = section == 1
    on_right = section == 3
    at_first = is_nest & (tile == 0)
    at_last = is_nest & (tile == 7)

    @pl.when(on_left | on_right)
    def _():
        before_six = jnp.where(tile == 6, cross_ref[HALO:, :LANE], 0.0)
        edges = jnp.concatenate([rims[:ROWS, LANE:] + before_six, rims[ROWS:, LANE:]], axis=0)
        start = offset + tile * 8 - 2 - first_source(jnp.maximum((offset - 2) // ROWS, 1), tile) * ROWS
        value = pltpu.roll(edges, RIMS - start, 0)[:16]
        short = iota((16, LANE), 1)
        place = short - 3 * third(short)
        west = jnp.where(place == jnp.where(on_left, 0, -1), value, turn(value, 1, 1))
        east = jnp.where(place == jnp.where(on_left, -1, 2), value, turn(value, -1, 1))
        other = jnp.where((third(short) & 1) == 0, turn(value, -3, 1), turn(value, 3, 1))
        cy = jnp.zeros((16, LANE), jnp.float32)
        cx = jnp.zeros((16, LANE), jnp.float32)
        for field in range(STATES // 2):
            mine = (short >= 6 * field) & (short < 6 * field + 6)
            cy = jnp.where(mine, turn(value, 6 * field - 3 * STATES, 1), cy)
            cx = jnp.where(mine, turn(value, 6 * field - 3 * STATES - 6, 1), cx)
        change = (
            flux(value, turn(value, 1, 0), turn(value, -1, 0), west, east, other, cy, cx) / RATIO
        )
        eight = iota((8, LANE), 0)

        def tall(narrow):
            tiles = []
            for block in range(4):
                rows = [8 * block + i for i in range(8)]
                under = [(i if i < 28 else i - 32) // RATIO + 2 for i in rows]
                tile_rows = jnp.broadcast_to(narrow[under[0] : under[0] + 1], (8, LANE))
                for i in range(1, 8):
                    if under[i] != under[i - 1]:
                        tile_rows = jnp.where(eight >= i, narrow[under[i] : under[i] + 1], tile_rows)
                tiles.append(tile_rows)
            return jnp.concatenate(tiles, axis=0)

        wide_value, wide_change = tall(value), tall(change)

        def place_side(lanes, first, split):
            free = row_depth[:, lanes] >= ZONE
            share = jnp.where(free, weight[:, lanes], 0.0)
            for p in range(STATES):
                for kind, source in enumerate((wide_value, wide_change)):
                    at = 3 * p + first
                    near, far = source[:, at : at + 1], source[:, at + 1 : at + 2]
                    column_force[kind, p] = share * jnp.where(lane < split, near, far)

        @pl.when(on_left)
        def _():
            place_side(slice(0, LANE), 0, 3)

        @pl.when(on_right)
        def _():
            place_side(slice(2 * LANE, 3 * LANE), 1, LANE - 3)

    @pl.when(at_first | at_last)
    def _():
        wide = iota((8, 2 * LANE), 1)
        short = iota((8, LANE), 1)
        eight = iota((8, 4 * LANE), 0)
        outside = turn(rims[:SLOTS, LANE:], 84, 1)
        rows = jnp.concatenate([rims[:SLOTS, :LANE], outside], axis=1)
        cy = rows[4 * STATES : 4 * STATES + 8]
        cx = rows[4 * STATES + 8 :]
        under = [((short + LANE * i) * 171) >> 9 for i in range(3)]

        def stretch(value):
            inside = [
                jnp.take_along_axis(value[:, :LANE], i, axis=1, mode="promise_in_bounds")
                for i in under
            ]
            after_last = value[:, LANE : LANE + 1]
            before_first = value[:, 2 * LANE - 1 :]
            beside = jnp.where(
                short < 3, after_last, jnp.where(short >= LANE - 3, before_first, 0.0)
            )
            return jnp.concatenate(inside + [beside], axis=1)

        forces = []
        for field in range(STATES // 2):
            value = rows[8 * field : 8 * field + 8]
            west = jnp.where(wide == jnp.where(section == 1, 0, -1), value, turn(value, 1, 1))
            east = jnp.where(
                wide == jnp.where(section == 3, LANE - 1, -1), value, turn(value, -1, 1)
            )
            south, north, other = turn(value, 1, 0), turn(value, -1, 0), turn(value, 4, 0)
            change = flux(value, south, north, west, east, other, cy, cx) / RATIO
            forces.append((stretch(value), stretch(change)))

        def place_rows(rows, split):
            share = jnp.where(row_depth[rows] < ZONE, weight[rows], 0.0)
            for p in range(STATES):
                at = 4 * (p % 2)
                for kind in range(2):
                    source = forces[p // 2][kind]
                    near, far = source[at + 1 : at + 2], source[at + 2 : at + 3]
                    row_force[kind, p] = share * jnp.where(eight < split, near, far)

        @pl.when(at_first)
        def _():
            place_rows(slice(0, 8), 3)

        @pl.when(at_last)
        def _():
            place_rows(slice(16, 24), 5)

    def substep(source, target, number, rows, lanes):
        def per_field(field, carry):
            values = [source[2 * field + level] for level in range(2)]
            for level in range(2):
                value = values[level]
                factor = [factors[level, i, rows, lanes] for i in range(5)]
                result = factor[0] * value[rows, lanes]
                result += factors[0, 5, rows, lanes] * values[1 - level][rows, lanes]
                result += factor[1] * turn(value, 1, 0)[rows, lanes]
                result += factor[2] * turn(value, -1, 0)[rows, lanes]
                result += factor[3] * turn(value, 1, 1)[rows, lanes]
                result += factor[4] * turn(value, -1, 1)[rows, lanes]
                target[2 * field + level] = result
            return carry

        lax.fori_loop(0, STATES // 2, per_field, 0)

        def push(force, rows, lanes, part):
            def per_plane(p, carry):
                amount = force[0, p][part] + float(number) * force[1, p][part]
                target[p, rows, lanes] = target[p, rows, lanes] + amount
                return carry

            lax.fori_loop(0, STATES, per_plane, 0, unroll=2)

        for where, section_lanes in ((on_left, slice(0, LANE)), (on_right, slice(2 * LANE, COLS))):

            @pl.when(where)
            def _():
                push(column_force, rows, section_lanes, (rows, slice(None)))

        for where, tile_rows in ((at_first, slice(0, 8)), (at_last, slice(16, 24))):

            @pl.when(where)
            def _():
                push(row_force, tile_rows, lanes, (slice(None), lanes))

    @pl.when(is_nest)
    def _():
        substep(here, there, 1, slice(0, 32), slice(0, 4 * LANE))
        substep(there, here, 2, slice(0, 32), slice(0, 4 * LANE))

    substep(here, out_ref, 3, slice(0, ROWS), slice(0, COLS))

    @pl.when(is_nest)
    def _():
        columns = iota((COLS, LANE), 1) * RATIO
        source = iota((COLS, LANE), 0)
        gather = ((source >= columns) & (source < columns + RATIO)).astype(jnp.bfloat16)
        cells = out_ref[...].reshape(STATES * ROWS, COLS)
        narrowed[...] = sum(product(part, gather) for part in parts(cells))
        total = sum(narrowed[pl.ds(i, STATES * 8, stride=RATIO), :] for i in range(RATIO))
        means_ref[...] = total / (RATIO * RATIO)


def merge_kernel(offset_ref, *refs):
    *block_refs, stepped_ref, out_ref, near = refs
    tile = lax.axis_index("tile")
    section = lax.axis_index("section")
    offset = offset_ref[0]
    rest = offset % 8

    @pl.when(section > 0)
    def _():
        out_ref[...] = stepped_ref[...]

    @pl.when(section == 0)
    def _():
        for step in range(4):
            source = 3 * tile - offset // 8 - 1 + step
            inside = (source >= 0) & (source < 8)
            for way, block_ref in enumerate(block_refs):

                @pl.when(inside & (source == (tile ^ way)))
                def _():
                    near[step] = block_ref[...]

        nest_row = tile * ROWS + iota((ROWS, COLS), 0) - offset
        covered = (nest_row >= 0) & (nest_row < 64)
        for p in range(STATES):
            parts = [near[step, 8 * p : 8 * p + 8] for step in range(4)]
            moved = pltpu.roll(jnp.concatenate(parts, axis=0), rest + 24, 0)
            out_ref[p] = jnp.where(covered, moved[:ROWS], stepped_ref[p])


VMEM = pl.BlockSpec(memory_space=pltpu.VMEM)
SMEM = pl.BlockSpec(memory_space=pltpu.SMEM)


def shaped(*shape):
    return jax.ShapeDtypeStruct(shape, jnp.float32)


def in_rounds(edges, count):
    at = {}
    for source, target in edges:
        mine, theirs = ("from", source), ("to", target)
        a = next(c for c in range(count) if (mine, c) not in at)
        b = next(c for c in range(count) if (theirs, c) not in at)
        path = []
        node, color = theirs, a
        while (node, color) in at:
            node_next = at[(node, color)]
            path.append((node, node_next, color))
            node, color = node_next, (b if color == a else a)
        for one, two, color in path:
            del at[(one, color)], at[(two, color)]
        for one, two, color in path:
            swapped = b if color == a else a
            at[(one, swapped)] = two
            at[(two, swapped)] = one
        at[(mine, a)] = theirs
        at[(theirs, a)] = mine
    rounds = [[] for _ in range(count)]
    for (node, color), other in sorted(at.items()):
        if node[0] == "from":
            rounds[color].append((node[1], other[1]))
    return rounds


def hops(one, two):
    (t, s), (u, r) = divmod(one, 4), divmod(two, 4)
    links = abs((t >> 2) - (u >> 2)) + abs(((t >> 1) & 1) - ((u >> 1) & 1)) + abs(s - r)
    return links or 0.3


def completed(pairs, valid):
    senders = [d for d in range(32) if d not in {a for a, _ in pairs}]
    takers = [d for d in range(32) if d not in {b for _, b in pairs}]

    def cost(a, b):
        from_parent = a % 4 == 0 and b % 4 > 0
        return 1e3 if a == b or from_parent or (a, b) in valid else hops(a, b) ** 2

    n = len(senders)
    row_price, column_price = [0.0] * (n + 1), [0.0] * (n + 1)
    owner = [0] * (n + 1)
    for i in range(1, n + 1):
        owner[0] = i
        column = 0
        least, before, used = [1e9] * (n + 1), [0] * (n + 1), [False] * (n + 1)
        while True:
            used[column] = True
            row, step, best = owner[column], 1e9, 0
            for j in range(1, n + 1):
                if not used[j]:
                    gap = cost(senders[row - 1], takers[j - 1]) - row_price[row] - column_price[j]
                    if gap < least[j]:
                        least[j], before[j] = gap, column
                    if least[j] < step:
                        step, best = least[j], j
            for j in range(n + 1):
                if used[j]:
                    row_price[owner[j]] += step
                    column_price[j] -= step
                else:
                    least[j] -= step
            column = best
            if owner[column] == 0:
                break
        while column:
            owner[column], column = owner[before[column]], before[column]
    return pairs + [(senders[owner[j] - 1], takers[j - 1]) for j in range(1, n + 1)]


def rim_pairs(start):
    to_chips = [(0, 0), (1, 1), (0, 2), (1, 3), (2, 3), (2, 4), (1, 5), (3, 4), (2, 6), (3, 7)]
    sends = [(start + step, tile) for step, tile in to_chips]
    middle = [[(start, 0), (start + 1, 1), (start + 2, 6), (start + 3, 7)]]
    if start == 1:
        sends.append((0, 0))
        middle.append([(0, 0)])
    groups = []
    for section, inner in ((1, ((2, 1), (3, 2))), (3, ((1, 2), (2, 3)))):
        edges = [(device(a, 0), device(b, section)) for a, b in sends]
        edges += [(device(t, a), device(t, b)) for t in range(8) for a, b in inner]
        rounds = in_rounds(edges, 3)[::-1]
        groups.append([completed(pairs, edges) for pairs in rounds])
    middle = [[(device(a, 0), device(b, 2)) for a, b in pairs] for pairs in middle]
    middle = [completed(pairs, []) for pairs in middle]
    return groups[0], middle, groups[1]


BOTH = ("tile", "section")


def on_device(state, courant, nest_offset):
    planes = state.reshape(STATES, ROWS, COLS)
    speeds = courant.reshape(4, ROWS, COLS)
    offset = nest_offset[0]
    *payloads, to_pair, to_cross = pl.pallas_call(
        pack_kernel,
        out_shape=[shaped(SLOTS, 2 * LANE)] * 3
        + [shaped(HALO + RIMS, COLS), shaped(HALO + ROWS, COLS)],
        in_specs=[SMEM, VMEM, VMEM],
        out_specs=[VMEM] * 5,
        name="pack",
    )(nest_offset, planes, speeds)

    def send_rims(start, to_pair, to_cross, west, middle, east):
        groups = rim_pairs(start)
        west, middle, east = (
            [lax.ppermute(value, BOTH, pairs) for pairs in lists]
            for value, lists in zip((west, middle, east), groups)
        )
        return pl.pallas_call(
            functools.partial(relay_kernel, start, len(middle)),
            out_shape=[
                shaped(ROWS, LANE),
                shaped(ROWS, LANE),
                shaped(RIMS, 2 * LANE),
                shaped(HALO + RIMS, COLS),
                shaped(HALO + ROWS, COLS),
            ],
            in_specs=[VMEM] * (8 + len(middle)),
            out_specs=[VMEM] * 5,
            input_output_aliases={0: 3, 1: 4},
            name="relay",
        )(to_pair, to_cross, *east, *middle, *west)

    west, east, rims, to_pair, to_cross = lax.switch(
        (offset - 2) // ROWS - 1,
        [functools.partial(send_rims, start) for start in (1, 2, 3)],
        to_pair,
        to_cross,
        *payloads,
    )
    pair_map = [(device(t, s), device(t ^ 1, s)) for t in range(8) for s in range(4)]
    cross_map = [
        (device(a, s), device(b, s))
        for low in (1, 3, 5, 7)
        for a, b in ((low, (low + 1) % 8), ((low + 1) % 8, low))
        for s in range(4)
    ]
    from_cross = lax.ppermute(to_cross, BOTH, cross_map)
    from_pair = lax.ppermute(to_pair, BOTH, pair_map)
    block, means = pl.pallas_call(
        main_kernel,
        out_shape=[shaped(STATES, ROWS, COLS), shaped(STATES * 8, LANE)],
        in_specs=[SMEM] + [VMEM] * 7,
        out_specs=[VMEM] * 2,
        scratch_shapes=[
            pltpu.VMEM((STATES, 32, 4 * LANE), jnp.float32),
            pltpu.VMEM((STATES, 32, 4 * LANE), jnp.float32),
            pltpu.VMEM((2, 6, 32, 4 * LANE), jnp.float32),
            pltpu.VMEM((2, STATES, 32, LANE), jnp.float32),
            pltpu.VMEM((2, STATES, 8, 4 * LANE), jnp.float32),
            pltpu.VMEM((STATES * ROWS, LANE), jnp.float32),
        ],
        compiler_params=pltpu.CompilerParams(vmem_limit_bytes=32 * 1024 * 1024),
        name="nest",
    )(nest_offset, planes, speeds, west, east, rims, from_pair, from_cross)
    def gather_from(s):
        pairs = [(device(t, s), device(t, 0)) for t in range(8)]
        if s == 2:
            pairs = completed(pairs, [])
        return lax.ppermute(means, BOTH, pairs)

    got = {s: gather_from(s) for s in (1, 2, 3)}
    columns = jnp.concatenate([got[s] for s in (1, 2, 3)], axis=1)

    def across(value, way):
        pairs = [(device(t, s), device(t ^ way, s)) for t in range(8) for s in range(4)]
        return lax.ppermute(value, BOTH, pairs)

    blocks = {0: columns}
    for way in (7, 3, 4, 1):
        blocks[way] = across(columns, way)
    for way in (7, 3, 4):
        blocks[way ^ 1] = across(blocks[way], 1)
    merged = pl.pallas_call(
        merge_kernel,
        out_shape=shaped(STATES, ROWS, COLS),
        in_specs=[SMEM] + [VMEM] * 9,
        out_specs=VMEM,
        scratch_shapes=[pltpu.VMEM((4, STATES * 8, COLS), jnp.float32)],
        compiler_params=pltpu.CompilerParams(vmem_limit_bytes=32 * 1024 * 1024),
        name="merge",
    )(nest_offset, *[blocks[way] for way in range(8)], block)
    return merged.reshape(state.shape)


def solution(mesh):
    small = mesh.shape["tile"] == 8 and mesh.shape["section"] == 4
    return jax.shard_map(
        on_device if small else general_on_device,
        mesh=mesh,
        in_specs=(P(None, None, "tile", "section"), P(None, None, "tile", "section"), P()),
        out_specs=P(None, None, "tile", "section"),
        check_vma=False,
    )
```

```python
import functools

import jax
import jax.numpy as jnp
from jax import lax
from jax.experimental import pallas as pl
from jax.experimental.pallas import tpu as pltpu
from jax.sharding import PartitionSpec as P

RATIO = 3
ZONE = 5


diffusion = 0.02
mixing = 0.05


def shifted(value, axis, steps):
    count = lax.axis_size(axis)
    leading, last = (max(0, -steps), min(count, count - steps))
    return lax.ppermute(value, axis, [(source, source + steps) for source in range(leading, last)])


def with_halo(block, sides, width):
    for axis, dim in sides:
        count = lax.axis_size(axis)
        forward = [(i, i + 1) for i in range(count - 1)]
        backward = [(target, source) for source, target in forward]
        low = lax.ppermute(
            lax.slice_in_dim(block, block.shape[dim] - width, None, axis=dim), axis, forward
        )
        high = lax.ppermute(lax.slice_in_dim(block, 0, width, axis=dim), axis, backward)
        block = jnp.concatenate([low, block, high], axis=dim)
    return block


def advance(values, courant, padded, low_row, high_row, low_col, high_col):
    row_count = values.shape[2]
    col_count = values.shape[3]
    row_index = lax.broadcasted_iota(jnp.int32, (1, 1, row_count, col_count), 2)
    column_index = lax.broadcasted_iota(jnp.int32, (1, 1, row_count, col_count), 3)
    south_side = jnp.where(low_row & (row_index == 0), values, padded[:, :, :-2, 1:-1])
    north_side = jnp.where(high_row & (row_index == row_count - 1), values, padded[:, :, 2:, 1:-1])
    west_side = jnp.where(low_col & (column_index == 0), values, padded[:, :, 1:-1, :-2])
    east_side = jnp.where(
        high_col & (column_index == col_count - 1), values, padded[:, :, 1:-1, 2:]
    )
    stacked = jnp.pad(values, ((0, 0), (1, 1), (0, 0), (0, 0)), mode="edge")
    level_below = stacked[:, :-2]
    level_above = stacked[:, 2:]
    speed_y = courant[0]
    speed_x = courant[1]
    transport = (
        jnp.maximum(speed_y, 0.0) * (values - south_side)
        + jnp.minimum(speed_y, 0.0) * (north_side - values)
        + jnp.maximum(speed_x, 0.0) * (values - west_side)
        + jnp.minimum(speed_x, 0.0) * (east_side - values)
    )
    spread = south_side + north_side + west_side + east_side - 4.0 * values
    column = level_below + level_above - 2.0 * values
    return values - transport + diffusion * spread + mixing * column


def send_rims(values, distance):
    return shifted(values, "section", distance)


def general_on_device(state, courant, nest_offset):
    fields, levels, row_count, col_count = state.shape
    tile_count = lax.axis_size("tile")
    section_count = lax.axis_size("section")
    parent_count = section_count // 4
    tile_index = lax.axis_index("tile")
    section = lax.axis_index("section")
    offset = nest_offset[0]
    total_rows = row_count * tile_count
    nest_height = total_rows // RATIO
    third_width = col_count // RATIO
    coarse_rows = row_count // RATIO
    parent_width = parent_count * col_count
    nest_width = section_count * col_count - parent_width
    is_parent = section < parent_count
    low_row = tile_index == 0
    high_row = tile_index == tile_count - 1
    low_col = (section == 0) | (section == parent_count)
    high_col = (section == parent_count - 1) | (section == section_count - 1)

    def step(values):
        padded = with_halo(values, (("tile", 2), ("section", 3)), 1)
        return advance(values, courant, padded, low_row, high_row, low_col, high_col)

    stepped = step(state)
    local_rows = tile_index * row_count + jnp.arange(row_count, dtype=jnp.int32)
    rim_coarse = jnp.array([0, 1, nest_height - 2, nest_height - 1], dtype=jnp.int32)
    wanted = offset + rim_coarse
    pick_rows = (wanted[:, None] == local_rows[None, :]).astype(jnp.float32)
    parent_flag = is_parent.astype(jnp.float32)
    both_states = jnp.stack([state, stepped]) * parent_flag
    rim_part = jnp.einsum(
        "jr,tflrc->tfljc", pick_rows, both_states, precision=lax.Precision.HIGHEST
    )
    edge_cols = jnp.array([0, 1, parent_width - 2, parent_width - 1], dtype=jnp.int32)
    global_cols = section * col_count + jnp.arange(col_count, dtype=jnp.int32)
    pick_edge = (global_cols[:, None] == edge_cols[None, :]).astype(jnp.float32)
    edge_local = jnp.einsum(
        "tflrc,ck->tflrk", both_states, pick_edge, precision=lax.Precision.HIGHEST
    )
    span_rows = offset + jnp.arange(nest_height, dtype=jnp.int32)
    pick_span = (span_rows[:, None] == local_rows[None, :]).astype(jnp.float32)
    edge_part = jnp.einsum(
        "nr,tflrk->tflnk", pick_span, edge_local, precision=lax.Precision.HIGHEST
    )
    packed = jnp.concatenate(
        [
            rim_part.reshape(2 * fields * levels, 4 * col_count),
            edge_part.reshape(2 * fields * levels, nest_height * 4),
        ],
        axis=1,
    )
    summed = lax.psum(packed, "tile")
    nest_index = jnp.maximum(section - parent_count, 0)
    source_parent = nest_index // RATIO
    received = jnp.zeros_like(summed)
    for distance in range(parent_count, 3 * parent_count + 1):
        arrived = send_rims(summed, distance)
        hit = jnp.logical_not(is_parent) & (section - distance == source_parent)
        received = jnp.where(hit, arrived, received)
    rim_rows = received[:, : 4 * col_count].reshape(2, fields, levels, 4, col_count)
    edges = received[:, 4 * col_count :].reshape(2, fields, levels, nest_height, 4)
    rim_strip = lax.dynamic_slice_in_dim(rim_rows, nest_index % RATIO * third_width, third_width, 4)
    rim_strip = jnp.repeat(rim_strip, RATIO, axis=4)
    row_choice = ((local_rows // RATIO)[:, None] == rim_coarse[None, :]).astype(jnp.float32)
    forcing_rows = jnp.einsum(
        "rj,tfljc->tflrc", row_choice, rim_strip, precision=lax.Precision.HIGHEST
    )
    nest_cols = nest_index * col_count + jnp.arange(col_count, dtype=jnp.int32)
    col_choice = (edge_cols[:, None] == (nest_cols // RATIO)[None, :]).astype(jnp.float32)
    coarse_choice = (
        (local_rows // RATIO)[:, None] == jnp.arange(nest_height, dtype=jnp.int32)[None, :]
    ).astype(jnp.float32)
    edge_rows = jnp.einsum("rn,tflnk->tflrk", coarse_choice, edges, precision=lax.Precision.HIGHEST)
    forcing_cols = jnp.einsum(
        "tflrk,kc->tflrc", edge_rows, col_choice, precision=lax.Precision.HIGHEST
    )
    row_depth = jnp.minimum(local_rows, total_rows - 1 - local_rows)
    col_depth = jnp.minimum(nest_cols, nest_width - 1 - nest_cols)
    row_zone = (row_depth < ZONE)[:, None]
    forcing = jnp.where(row_zone, forcing_rows, forcing_cols)
    depth = jnp.minimum(row_depth[:, None], col_depth[None, :])
    weight = jnp.maximum(ZONE - depth, 0).astype(jnp.float32) / ZONE

    def relax(values, substep):
        fraction = (substep + 1) / RATIO
        target = forcing[0] + fraction * (forcing[1] - forcing[0])
        return values + weight * (target - values)

    nest_field = relax(stepped, 0)
    for substep in range(1, RATIO):
        nest_field = relax(step(nest_field), substep)
    block_means = nest_field.reshape(fields, levels, coarse_rows, RATIO, third_width, RATIO).sum(
        axis=(3, 5)
    ) / (RATIO * RATIO)
    wanted_nest = local_rows - offset
    portion = lax.all_gather(block_means, "tile", axis=2, tiled=True)
    row_span = portion.shape[2]
    select = (wanted_nest[:, None] == jnp.arange(row_span, dtype=jnp.int32)[None, :]).astype(
        jnp.float32
    )
    gathered = jnp.einsum("rs,flsc->flrc", select, portion, precision=lax.Precision.HIGHEST)
    target_slot = jnp.where(is_parent, -1, (section - parent_count) // RATIO)
    slot_index = jnp.arange(section_count, dtype=jnp.int32)
    outbound = jnp.where(
        (slot_index == target_slot)[None, None, None, :, None], gathered[:, :, :, None, :], 0.0
    )
    outbound = outbound.reshape(fields, levels, row_count, section_count * third_width)
    received_means = lax.all_to_all(outbound, "section", split_axis=3, concat_axis=3, tiled=True)
    start_col = (parent_count + RATIO * jnp.minimum(section, parent_count - 1)) * third_width
    feedback = lax.dynamic_slice_in_dim(received_means, start_col, col_count, 3)
    covered = ((wanted_nest >= 0) & (wanted_nest < nest_height))[:, None]
    parent_final = jnp.where(covered, feedback, stepped)
    return jnp.where(is_parent, parent_final, nest_field)


ROWS = 24
COLS = 384
LANE = 128
STATES = 10
PLANES = 14
SLOTS = 4 * PLANES
HALO = SLOTS + 8
RIMS = 3 * ROWS


def device(tile, section):
    return tile * 4 + section


def device_mark(tile, section):
    return (device(tile, section) + 1).astype(jnp.float32)


def third(value):
    return (value * 43) >> 7


def iota(shape, dim):
    return lax.broadcasted_iota(jnp.int32, shape, dim)


def parts(value):
    high = value.astype(jnp.bfloat16)
    rest = value - high.astype(jnp.float32)
    middle = rest.astype(jnp.bfloat16)
    return high, middle, (rest - middle.astype(jnp.float32)).astype(jnp.bfloat16)


def product(a, b):
    return jnp.dot(a, b, preferred_element_type=jnp.float32)


def choose(ones, value):
    return sum(product(ones.astype(jnp.bfloat16), part) for part in parts(value))


def turn(value, steps, dim):
    size = value.shape[dim]
    steps = steps % size
    return pltpu.roll(value, steps, dim) if steps else value


def plane_of(state_ref, courant_ref, p):
    return state_ref[p] if p < STATES else courant_ref[p - STATES]


def pack_kernel(
    offset_ref, state_ref, courant_ref, west_ref, middle_ref, east_ref, pair_ref, cross_ref
):
    tile = lax.axis_index("tile")
    section = lax.axis_index("section")
    offset = offset_ref[0]
    first = tile * ROWS
    lane = iota((ROWS, LANE), 1)
    left = jnp.zeros((ROWS, LANE), jnp.float32)
    right = jnp.zeros((ROWS, LANE), jnp.float32)
    for p in range(PLANES):
        source = plane_of(state_ref, courant_ref, p)
        mine = (lane >= 3 * p) & (lane < 3 * p + 3)
        left = jnp.where(mine, turn(source[:, :LANE], 3 * p, 1), left)
        right = jnp.where(mine, turn(source[:, COLS - LANE :], 3 * p - (LANE - 3), 1), right)
    top = (first <= offset + 2) & (first + ROWS - 1 >= offset - 1)
    base = jnp.where(top, offset - 1, offset + 61) - first

    def chosen(count):
        slot = iota((4 * count, ROWS * count), 0)
        column = iota((4 * count, ROWS * count), 1)
        local = base + (slot & 3)
        hit = (local >= 0) & (local < ROWS) & (column == (slot >> 2) * ROWS + local)
        return hit.astype(jnp.float32)

    rows = jnp.concatenate(
        [
            choose(chosen(STATES), state_ref[...].reshape(STATES * ROWS, COLS)),
            choose(chosen(4), courant_ref[...].reshape(4 * ROWS, COLS)),
        ],
        axis=0,
    )
    lane = iota((SLOTS, LANE), 1)
    mark = device_mark(tile, section)
    blank = jnp.zeros((SLOTS, LANE), jnp.float32)
    both = jnp.where(iota((ROWS, LANE), 1) < 42, left, turn(right, 64, 1))
    outs = ((west_ref, left), (middle_ref, both), (east_ref, right))
    for s, (out_ref, edge) in enumerate(outs):
        before = rows[:, LANE * (s - 1) : LANE * s] if s > 0 else blank
        after = rows[:, LANE * (s + 1) : LANE * (s + 2)] if s < 2 else blank
        extra = turn(jnp.where(lane < 2, after, before), 44, 1)
        side = jnp.where(
            (lane >= 42) & (lane < 46), extra, jnp.where(lane == LANE - 1, mark, 0.0)
        )
        out_ref[:, :LANE] = rows[:, LANE * s : LANE * (s + 1)]
        free = (lane[:ROWS] >= 42) & (lane[:ROWS] < 64) | (lane[:ROWS] == LANE - 1)
        out_ref[:ROWS, LANE:] = jnp.where(free, side[:ROWS], edge)
        out_ref[ROWS:, LANE:] = side[ROWS:]


    even = tile % 2 == 0
    for p in range(PLANES):
        source = plane_of(state_ref, courant_ref, p)
        head, tail = source[:4], source[ROWS - 4 :]
        pair_ref[4 * p : 4 * p + 4] = jnp.where(even, tail, head)
        cross_ref[4 * p : 4 * p + 4] = jnp.where(even, head, tail)


def first_source(start, tile):
    return start - 1 + jnp.minimum(tile // 2, 2)


def across_chips(tile):
    return jnp.where(tile % 2 == 0, tile - 1, tile + 1)


def relay_kernel(start, middles, to_pair_ref, from_cross_ref, *refs):
    to_east, middle, to_west = refs[:3], refs[3 : 3 + middles], refs[3 + middles : 6 + middles]
    west_ref, east_ref, rims_ref, pair_ref, cross_ref = refs[6 + middles :]
    pair_ref[:SLOTS] = to_pair_ref[...]
    pair_ref[SLOTS + 4 : HALO] = jnp.zeros((HALO - SLOTS - 4, COLS), jnp.float32)
    cross_ref[...] = from_cross_ref[...]
    tile = lax.axis_index("tile")
    section = lax.axis_index("section")
    even = tile % 2 == 0
    lane = iota((ROWS, LANE), 1)
    first = first_source(start, tile)
    sources = [device_mark(first + slot, 0) for slot in range(3)]
    has_east = (section == 1) | (section == 2)
    has_west = (section == 2) | (section == 3)
    corner = across_chips(tile)
    east_mark = jnp.where(has_east, device_mark(tile, section + 1), 0.0)
    west_mark = jnp.where(has_west, device_mark(tile, section - 1), 0.0)
    far_east_mark = jnp.where(has_east, device_mark(corner, section + 1), 0.0)
    far_west_mark = jnp.where(has_west, device_mark(corner, section - 1), 0.0)
    nothing = jnp.zeros((ROWS, LANE), jnp.float32)
    east = west = far_east = far_west = nothing
    edges = [nothing] * 3
    center = side = jnp.zeros((SLOTS, LANE), jnp.float32)
    targets = [3] * 3 + [2] * middles + [1] * 3
    for ref, target in zip(to_east + middle + to_west, targets):
        tail = ref[:, LANE:]
        mark = jnp.broadcast_to(tail[:, LANE - 1 :], (SLOTS, LANE))
        marks = [jnp.where(section == target, source, 0.0) for source in sources]
        hit = (mark == marks[0]) | (mark == marks[1]) | (mark == marks[2])
        center = jnp.where(hit, center + ref[:, :LANE], center)
        side = jnp.where(hit, side + tail, side)
        mark, cells = mark[:ROWS], tail[:ROWS]
        if target == 2:
            marks = [jnp.where(section == 2, 0.0, source) for source in sources]
            cells = jnp.where(section == 3, turn(cells, -64, 1), cells)
        edges = [jnp.where(mark == one, cells, edge) for one, edge in zip(marks, edges)]
        if target < 3:
            east = jnp.where(mark == east_mark, cells, east)
            far_east = jnp.where(mark == far_east_mark, cells, far_east)
        if target > 1:
            west = jnp.where(mark == west_mark, cells, west)
            far_west = jnp.where(mark == far_west_mark, cells, far_west)
    edges = [jnp.where(lane < 42, value, 0.0) for value in edges]
    for lanes, out_ref, value, far in (
        (slice(0, LANE), west_ref, west, far_west),
        (slice(LANE, 2 * LANE), east_ref, east, far_east),
    ):
        out_ref[:ROWS] = value
        out_ref[ROWS : ROWS + 4] = jnp.where(even, far[ROWS - 4 :], far[:4])
        out_ref[ROWS + 4 :] = jnp.zeros((4, LANE), jnp.float32)
        pair_ref[SLOTS : SLOTS + 4, lanes] = jnp.where(even, value[ROWS - 4 :], value[:4])
    wide = iota((SLOTS, LANE), 1)
    rims_ref[:SLOTS, :LANE] = center
    rims_ref[SLOTS:, :LANE] = jnp.zeros((RIMS - SLOTS, LANE), jnp.float32)
    extra = jnp.where((wide >= 42) & (wide < 46), side, 0.0)
    extra = jnp.concatenate([extra, jnp.zeros((RIMS - SLOTS, LANE), jnp.float32)], axis=0)
    rims_ref[:, LANE:] = jnp.concatenate(edges, axis=0) + extra
    pair_ref[HALO:, : 2 * LANE] = rims_ref[...]


def flux(value, south, north, west, east, other, cy, cx):
    transport = (
        jnp.maximum(cy, 0.0) * (value - south)
        + jnp.minimum(cy, 0.0) * (north - value)
        + jnp.maximum(cx, 0.0) * (value - west)
        + jnp.minimum(cx, 0.0) * (east - value)
    )
    spread = south + north + west + east - 4.0 * value
    return diffusion * spread + mixing * (other - value) - transport


def main_kernel(
    offset_ref,
    state_ref,
    courant_ref,
    west_ref,
    east_ref,
    rims_ref,
    pair_ref,
    cross_ref,
    out_ref,
    means_ref,
    here,
    there,
    factors,
    column_force,
    row_force,
    narrowed,
):
    tile = lax.axis_index("tile")
    section = lax.axis_index("section")
    offset = offset_ref[0]
    even = tile % 2 == 0
    is_nest = section > 0
    full = (32, 4 * LANE)

    after = jnp.where(even, pair_ref[:SLOTS], cross_ref[...])
    before = jnp.where(even, cross_ref[...], pair_ref[:SLOTS])

    def beside(ref, lanes):
        inside, outside = pair_ref[SLOTS : SLOTS + 4, lanes], ref[ROWS : ROWS + 4]
        last = [jnp.where(even, inside, outside), jnp.where(even, outside, inside)]
        return jnp.concatenate([ref[:ROWS]] + last, axis=0)

    wests = beside(west_ref, slice(0, LANE))
    easts = beside(east_ref, slice(LANE, 2 * LANE))
    lane = iota((32, LANE), 1)

    def ring(p):
        tail = jnp.concatenate([after[4 * p : 4 * p + 4], before[4 * p : 4 * p + 4]], axis=0)
        cells = jnp.concatenate([plane_of(state_ref, courant_ref, p), tail], axis=0)
        outside = jnp.where(
            lane < 3,
            turn(easts, -3 * p, 1),
            jnp.where(lane >= LANE - 3, turn(wests, LANE - 3 - 3 * p, 1), 0.0),
        )
        return jnp.concatenate([cells, outside], axis=1)

    for p in range(STATES):
        here[p] = ring(p)

    row = iota(full, 0)
    column = iota(full, 1)
    near_row = jnp.where(row < 28, row, row - 32)
    near_column = jnp.where(column < 448, column, column - 512)
    grid_row = near_row + tile * ROWS
    grid_column = near_column + (section - 1) * COLS
    row_depth = jnp.minimum(grid_row, 8 * ROWS - 1 - grid_row)
    column_depth = jnp.minimum(grid_column, 3 * COLS - 1 - grid_column)
    depth = jnp.maximum(jnp.minimum(row_depth, column_depth), 0)
    weight = jnp.maximum(ZONE - depth, 0).astype(jnp.float32) / ZONE
    weight = jnp.where(is_nest, weight, 0.0)
    keep = 1.0 - weight
    no_south = row == jnp.where(tile == 0, 0, -1)
    no_north = row == jnp.where(tile == 7, ROWS - 1, -1)
    no_west = column == jnp.where(section < 2, 0, -1)
    no_east = column == jnp.where((section == 0) | (section == 3), COLS - 1, -1)
    for level in range(2):
        cy = ring(STATES + level)
        cx = ring(STATES + 2 + level)
        from_south = jnp.maximum(cy, 0.0) + diffusion
        from_north = diffusion - jnp.minimum(cy, 0.0)
        from_west = jnp.maximum(cx, 0.0) + diffusion
        from_east = diffusion - jnp.minimum(cx, 0.0)
        from_south = jnp.where(no_south, 0.0, from_south)
        from_north = jnp.where(no_north, 0.0, from_north)
        from_west = jnp.where(no_west, 0.0, from_west)
        from_east = jnp.where(no_east, 0.0, from_east)
        own = (1.0 - mixing) - (from_south + from_north + from_west + from_east)
        factors[level, 0] = own * keep
        factors[level, 1] = from_south * keep
        factors[level, 2] = from_north * keep
        factors[level, 3] = from_west * keep
        factors[level, 4] = from_east * keep
    factors[0, 5] = mixing * keep

    rims = rims_ref[...] + pair_ref[HALO:, : 2 * LANE]
    on_left = section == 1
    on_right = section == 3
    at_first = is_nest & (tile == 0)
    at_last = is_nest & (tile == 7)

    @pl.when(on_left | on_right)
    def _():
        edges = rims[:, LANE:]
        start = offset + tile * 8 - 2 - first_source(jnp.maximum((offset - 2) // ROWS, 1), tile) * ROWS
        value = pltpu.roll(edges, RIMS - start, 0)[:16]
        short = iota((16, LANE), 1)
        place = short - 3 * third(short)
        west = jnp.where(place == jnp.where(on_left, 0, -1), value, turn(value, 1, 1))
        east = jnp.where(place == jnp.where(on_left, -1, 2), value, turn(value, -1, 1))
        other = jnp.where((third(short) & 1) == 0, turn(value, -3, 1), turn(value, 3, 1))
        cy = jnp.zeros((16, LANE), jnp.float32)
        cx = jnp.zeros((16, LANE), jnp.float32)
        for field in range(STATES // 2):
            mine = (short >= 6 * field) & (short < 6 * field + 6)
            cy = jnp.where(mine, turn(value, 6 * field - 3 * STATES, 1), cy)
            cx = jnp.where(mine, turn(value, 6 * field - 3 * STATES - 6, 1), cx)
        change = (
            flux(value, turn(value, 1, 0), turn(value, -1, 0), west, east, other, cy, cx) / RATIO
        )
        eight = iota((8, LANE), 0)

        def tall(narrow):
            tiles = []
            for block in range(4):
                rows = [8 * block + i for i in range(8)]
                under = [(i if i < 28 else i - 32) // RATIO + 2 for i in rows]
                tile_rows = jnp.broadcast_to(narrow[under[0] : under[0] + 1], (8, LANE))
                for i in range(1, 8):
                    if under[i] != under[i - 1]:
                        tile_rows = jnp.where(eight >= i, narrow[under[i] : under[i] + 1], tile_rows)
                tiles.append(tile_rows)
            return jnp.concatenate(tiles, axis=0)

        wide_value, wide_change = tall(value), tall(change)

        def place_side(lanes, first, split):
            free = row_depth[:, lanes] >= ZONE
            share = jnp.where(free, weight[:, lanes], 0.0)
            for p in range(STATES):
                for kind, source in enumerate((wide_value, wide_change)):
                    at = 3 * p + first
                    near, far = source[:, at : at + 1], source[:, at + 1 : at + 2]
                    column_force[kind, p] = share * jnp.where(lane < split, near, far)

        @pl.when(on_left)
        def _():
            place_side(slice(0, LANE), 0, 3)

        @pl.when(on_right)
        def _():
            place_side(slice(2 * LANE, 3 * LANE), 1, LANE - 3)

    @pl.when(at_first | at_last)
    def _():
        wide = iota((8, 2 * LANE), 1)
        short = iota((8, LANE), 1)
        eight = iota((8, 4 * LANE), 0)
        outside = turn(rims[:SLOTS, LANE:], 84, 1)
        rows = jnp.concatenate([rims[:SLOTS, :LANE], outside], axis=1)
        cy = rows[4 * STATES : 4 * STATES + 8]
        cx = rows[4 * STATES + 8 :]
        under = [((short + LANE * i) * 171) >> 9 for i in range(3)]

        def stretch(value):
            inside = [
                jnp.take_along_axis(value[:, :LANE], i, axis=1, mode="promise_in_bounds")
                for i in under
            ]
            after_last = value[:, LANE : LANE + 1]
            before_first = value[:, 2 * LANE - 1 :]
            beside = jnp.where(
                short < 3, after_last, jnp.where(short >= LANE - 3, before_first, 0.0)
            )
            return jnp.concatenate(inside + [beside], axis=1)

        forces = []
        for field in range(STATES // 2):
            value = rows[8 * field : 8 * field + 8]
            west = jnp.where(wide == jnp.where(section == 1, 0, -1), value, turn(value, 1, 1))
            east = jnp.where(
                wide == jnp.where(section == 3, LANE - 1, -1), value, turn(value, -1, 1)
            )
            south, north, other = turn(value, 1, 0), turn(value, -1, 0), turn(value, 4, 0)
            change = flux(value, south, north, west, east, other, cy, cx) / RATIO
            forces.append((stretch(value), stretch(change)))

        def place_rows(rows, split):
            share = jnp.where(row_depth[rows] < ZONE, weight[rows], 0.0)
            for p in range(STATES):
                at = 4 * (p % 2)
                for kind in range(2):
                    source = forces[p // 2][kind]
                    near, far = source[at + 1 : at + 2], source[at + 2 : at + 3]
                    row_force[kind, p] = share * jnp.where(eight < split, near, far)

        @pl.when(at_first)
        def _():
            place_rows(slice(0, 8), 3)

        @pl.when(at_last)
        def _():
            place_rows(slice(16, 24), 5)

    def substep(source, target, number, rows, lanes):
        def per_field(field, carry):
            values = [source[2 * field + level] for level in range(2)]
            for level in range(2):
                value = values[level]
                factor = [factors[level, i, rows, lanes] for i in range(5)]
                result = factor[0] * value[rows, lanes]
                result += factors[0, 5, rows, lanes] * values[1 - level][rows, lanes]
                result += factor[1] * turn(value, 1, 0)[rows, lanes]
                result += factor[2] * turn(value, -1, 0)[rows, lanes]
                result += factor[3] * turn(value, 1, 1)[rows, lanes]
                result += factor[4] * turn(value, -1, 1)[rows, lanes]
                target[2 * field + level] = result
            return carry

        lax.fori_loop(0, STATES // 2, per_field, 0)

        def push(force, rows, lanes, part):
            def per_plane(p, carry):
                amount = force[0, p][part] + float(number) * force[1, p][part]
                target[p, rows, lanes] = target[p, rows, lanes] + amount
                return carry

            lax.fori_loop(0, STATES, per_plane, 0, unroll=2)

        for where, section_lanes in ((on_left, slice(0, LANE)), (on_right, slice(2 * LANE, COLS))):

            @pl.when(where)
            def _():
                push(column_force, rows, section_lanes, (rows, slice(None)))

        for where, tile_rows in ((at_first, slice(0, 8)), (at_last, slice(16, 24))):

            @pl.when(where)
            def _():
                push(row_force, tile_rows, lanes, (slice(None), lanes))

    @pl.when(is_nest)
    def _():
        substep(here, there, 1, slice(0, 32), slice(0, 4 * LANE))
        substep(there, here, 2, slice(0, 32), slice(0, 4 * LANE))

    substep(here, out_ref, 3, slice(0, ROWS), slice(0, COLS))

    @pl.when(is_nest)
    def _():
        columns = iota((COLS, LANE), 1) * RATIO
        source = iota((COLS, LANE), 0)
        gather = ((source >= columns) & (source < columns + RATIO)).astype(jnp.bfloat16)
        cells = out_ref[...].reshape(STATES * ROWS, COLS)
        narrowed[...] = sum(product(part, gather) for part in parts(cells))
        total = sum(narrowed[pl.ds(i, STATES * 8, stride=RATIO), :] for i in range(RATIO))
        means_ref[...] = total / (RATIO * RATIO)


def ring_step(tile):
    return 7 - 4 * (((tile + 1) % 4) // 2)


def merge_kernel(offset_ref, *refs):
    *block_refs, stepped_ref, out_ref, near = refs
    tile = lax.axis_index("tile")
    section = lax.axis_index("section")
    offset = offset_ref[0]
    rest = offset % 8

    @pl.when(section > 0)
    def _():
        out_ref[...] = stepped_ref[...]

    @pl.when(section == 0)
    def _():
        mate = tile ^ 1
        sources = [tile, mate]
        for one in (tile, mate):
            sources += [one ^ ring_step(one), one ^ (10 - ring_step(one)), one ^ 4]
        for step in range(4):
            wanted = 3 * tile - offset // 8 - 1 + step
            for source, block_ref in zip(sources, block_refs):

                @pl.when(wanted == source)
                def _():
                    near[step] = block_ref[...]

        nest_row = tile * ROWS + iota((ROWS, COLS), 0) - offset
        covered = (nest_row >= 0) & (nest_row < 64)
        for p in range(STATES):
            parts = [near[step, 8 * p : 8 * p + 8] for step in range(4)]
            moved = pltpu.roll(jnp.concatenate(parts, axis=0), rest + 24, 0)
            out_ref[p] = jnp.where(covered, moved[:ROWS], stepped_ref[p])


VMEM = pl.BlockSpec(memory_space=pltpu.VMEM)
SMEM = pl.BlockSpec(memory_space=pltpu.SMEM)


def shaped(*shape):
    return jax.ShapeDtypeStruct(shape, jnp.float32)


def in_rounds(edges, count):
    at = {}
    for source, target in edges:
        mine, theirs = ("from", source), ("to", target)
        a = next(c for c in range(count) if (mine, c) not in at)
        b = next(c for c in range(count) if (theirs, c) not in at)
        path = []
        node, color = theirs, a
        while (node, color) in at:
            node_next = at[(node, color)]
            path.append((node, node_next, color))
            node, color = node_next, (b if color == a else a)
        for one, two, color in path:
            del at[(one, color)], at[(two, color)]
        for one, two, color in path:
            swapped = b if color == a else a
            at[(one, swapped)] = two
            at[(two, swapped)] = one
        at[(mine, a)] = theirs
        at[(theirs, a)] = mine
    rounds = [[] for _ in range(count)]
    for (node, color), other in sorted(at.items()):
        if node[0] == "from":
            rounds[color].append((node[1], other[1]))
    return rounds


def hops(one, two):
    (t, s), (u, r) = divmod(one, 4), divmod(two, 4)
    links = abs((t >> 2) - (u >> 2)) + abs(((t >> 1) & 1) - ((u >> 1) & 1)) + abs(s - r)
    return links or 0.3


def completed(pairs, valid):
    senders = [d for d in range(32) if d not in {a for a, _ in pairs}]
    takers = [d for d in range(32) if d not in {b for _, b in pairs}]

    def cost(a, b):
        from_parent = a % 4 == 0 and b % 4 > 0
        return 1e3 if a == b or from_parent or (a, b) in valid else hops(a, b) ** 2

    n = len(senders)
    row_price, column_price = [0.0] * (n + 1), [0.0] * (n + 1)
    owner = [0] * (n + 1)
    for i in range(1, n + 1):
        owner[0] = i
        column = 0
        least, before, used = [1e9] * (n + 1), [0] * (n + 1), [False] * (n + 1)
        while True:
            used[column] = True
            row, step, best = owner[column], 1e9, 0
            for j in range(1, n + 1):
                if not used[j]:
                    gap = cost(senders[row - 1], takers[j - 1]) - row_price[row] - column_price[j]
                    if gap < least[j]:
                        least[j], before[j] = gap, column
                    if least[j] < step:
                        step, best = least[j], j
            for j in range(n + 1):
                if used[j]:
                    row_price[owner[j]] += step
                    column_price[j] -= step
                else:
                    least[j] -= step
            column = best
            if owner[column] == 0:
                break
        while column:
            owner[column], column = owner[before[column]], before[column]
    return pairs + [(senders[owner[j] - 1], takers[j - 1]) for j in range(1, n + 1)]


def rim_pairs(case):
    start = max(case, 1)
    sends = {
        1: [(0, 0), (1, 1), (0, 2), (1, 3), (2, 3), (2, 4), (1, 5), (3, 4), (2, 6), (3, 7)],
        3: [(0, 0), (1, 1), (0, 2), (1, 3), (2, 2), (2, 4), (1, 5), (3, 5), (2, 6), (3, 7)],
    }
    corners = {low: low + 1 for low in (1, 3, 5)}
    corners.update({high: low for low, high in list(corners.items())})
    crowded = [(device(4, 2), device(3, 1)), (device(3, 2), device(4, 1))]
    crowded += [(device(1, 2), device(2, 3)), (device(6, 2), device(5, 3))]
    middle = [[(start, 0), (start + 1, 1), (start + 2, 6), (start + 3, 7)]]
    middle = [[(device(a, 0), device(b, 2)) for a, b in pairs] for pairs in middle]
    middle[0] += crowded
    if case == 0:
        middle.append([(device(0, 0), device(0, 2)), (device(2, 0), device(6, 1))])
        middle.append([(device(2, 0), device(6, 3))])
    groups = []
    for section, inner in ((1, ((2, 1), (3, 2))), (3, ((1, 2), (2, 3)))):
        edges = [(device(start + a, 0), device(b, section)) for a, b in sends[section]]
        if start == 1:
            edges.append((device(0, 0), device(0, section)))
        for a, b in inner:
            edges += [(device(t, a), device(t, b)) for t in range(8)]
            edges += [(device(corners[t], a), device(t, b)) for t in corners]
        edges = [pair for pair in edges if pair not in crowded]
        rounds = in_rounds(edges, 3)[::-1]
        groups.append([completed(pairs, edges) for pairs in rounds])
    middle = [completed(pairs, []) for pairs in middle]
    return groups[0], middle, groups[1]


BOTH = ("tile", "section")


def on_device(state, courant, nest_offset):
    planes = state.reshape(STATES, ROWS, COLS)
    speeds = courant.reshape(4, ROWS, COLS)
    offset = nest_offset[0]
    *payloads, to_pair, to_cross = pl.pallas_call(
        pack_kernel,
        out_shape=[shaped(SLOTS, 2 * LANE)] * 3
        + [shaped(SLOTS, COLS)] * 2,
        in_specs=[SMEM, VMEM, VMEM],
        out_specs=[VMEM] * 5,
        name="pack",
    )(nest_offset, planes, speeds)

    pair_map = [(device(t, s), device(t ^ 1, s)) for t in range(8) for s in range(4)]
    cross_map = [(device(t, s), device(t ^ ring_step(t), s)) for t in range(8) for s in range(4)]

    def send_rims(case, to_pair, to_cross, west, middle, east):
        from_cross = lax.ppermute(to_cross, BOTH, cross_map)
        groups = rim_pairs(case)
        west, middle, east = (
            [lax.ppermute(value, BOTH, pairs) for pairs in lists]
            for value, lists in zip((west, middle, east), groups)
        )
        return pl.pallas_call(
            functools.partial(relay_kernel, max(case, 1), len(middle)),
            out_shape=[
                shaped(32, LANE),
                shaped(32, LANE),
                shaped(RIMS, 2 * LANE),
                shaped(HALO + RIMS, COLS),
                shaped(SLOTS, COLS),
            ],
            in_specs=[VMEM] * (8 + len(middle)),
            out_specs=[VMEM] * 5,
            name="relay",
        )(to_pair, from_cross, *east, *middle, *west)

    west, east, rims, to_pair, from_cross = lax.switch(
        (offset - 2) // ROWS,
        [functools.partial(send_rims, case) for case in range(4)],
        to_pair,
        to_cross,
        *payloads,
    )
    from_pair = lax.ppermute(to_pair, BOTH, pair_map)
    stepped, means = pl.pallas_call(
        main_kernel,
        out_shape=[shaped(STATES, ROWS, COLS), shaped(STATES * 8, LANE)],
        in_specs=[SMEM] + [VMEM] * 7,
        out_specs=[VMEM] * 2,
        scratch_shapes=[
            pltpu.VMEM((STATES, 32, 4 * LANE), jnp.float32),
            pltpu.VMEM((STATES, 32, 4 * LANE), jnp.float32),
            pltpu.VMEM((2, 6, 32, 4 * LANE), jnp.float32),
            pltpu.VMEM((2, STATES, 32, LANE), jnp.float32),
            pltpu.VMEM((2, STATES, 8, 4 * LANE), jnp.float32),
            pltpu.VMEM((STATES * ROWS, LANE), jnp.float32),
        ],
        compiler_params=pltpu.CompilerParams(vmem_limit_bytes=32 * 1024 * 1024),
        name="nest",
    )(nest_offset, planes, speeds, west, east, rims, from_pair, from_cross)
    def gather_from(s):
        pairs = [(device(t, s), device(t, 0)) for t in range(8)]
        if s == 2:
            pairs = completed(pairs, [])
        return lax.ppermute(means, BOTH, pairs)

    got = {s: gather_from(s) for s in (1, 2, 3)}
    columns = jnp.concatenate([got[s] for s in (1, 2, 3)], axis=1)

    def across(value, partner):
        pairs = [(device(t, s), device(partner(t), s)) for t in range(8) for s in range(4)]
        return lax.ppermute(value, BOTH, pairs)

    def mate(t):
        return t ^ 1

    ways = (lambda t: t ^ ring_step(t), lambda t: t ^ (10 - ring_step(t)), lambda t: t ^ 4)
    blocks = [columns, across(columns, mate)]
    blocks += [across(columns, way) for way in ways]
    blocks += [across(block, mate) for block in blocks[2:]]
    merged = pl.pallas_call(
        merge_kernel,
        out_shape=shaped(STATES, ROWS, COLS),
        in_specs=[SMEM] + [VMEM] * 9,
        out_specs=VMEM,
        scratch_shapes=[pltpu.VMEM((4, STATES * 8, COLS), jnp.float32)],
        compiler_params=pltpu.CompilerParams(vmem_limit_bytes=32 * 1024 * 1024),
        name="merge",
    )(nest_offset, *blocks, stepped)
    return merged.reshape(state.shape)


def solution(mesh):
    small = mesh.shape["tile"] == 8 and mesh.shape["section"] == 4
    return jax.shard_map(
        on_device if small else general_on_device,
        mesh=mesh,
        in_specs=(P(None, None, "tile", "section"), P(None, None, "tile", "section"), P()),
        out_specs=P(None, None, "tile", "section"),
        check_vma=False,
    )
```

```python
import functools

import jax
import jax.numpy as jnp
from jax import lax
from jax.experimental import pallas as pl
from jax.experimental.pallas import tpu as pltpu
from jax.sharding import PartitionSpec as P

RATIO = 3
ZONE = 5


diffusion = 0.02
mixing = 0.05


def shifted(value, axis, steps):
    count = lax.axis_size(axis)
    leading, last = (max(0, -steps), min(count, count - steps))
    return lax.ppermute(value, axis, [(source, source + steps) for source in range(leading, last)])


def with_halo(block, sides, width):
    for axis, dim in sides:
        count = lax.axis_size(axis)
        forward = [(i, i + 1) for i in range(count - 1)]
        backward = [(target, source) for source, target in forward]
        low = lax.ppermute(
            lax.slice_in_dim(block, block.shape[dim] - width, None, axis=dim), axis, forward
        )
        high = lax.ppermute(lax.slice_in_dim(block, 0, width, axis=dim), axis, backward)
        block = jnp.concatenate([low, block, high], axis=dim)
    return block


def advance(values, courant, padded, low_row, high_row, low_col, high_col):
    row_count = values.shape[2]
    col_count = values.shape[3]
    row_index = lax.broadcasted_iota(jnp.int32, (1, 1, row_count, col_count), 2)
    column_index = lax.broadcasted_iota(jnp.int32, (1, 1, row_count, col_count), 3)
    south_side = jnp.where(low_row & (row_index == 0), values, padded[:, :, :-2, 1:-1])
    north_side = jnp.where(high_row & (row_index == row_count - 1), values, padded[:, :, 2:, 1:-1])
    west_side = jnp.where(low_col & (column_index == 0), values, padded[:, :, 1:-1, :-2])
    east_side = jnp.where(
        high_col & (column_index == col_count - 1), values, padded[:, :, 1:-1, 2:]
    )
    stacked = jnp.pad(values, ((0, 0), (1, 1), (0, 0), (0, 0)), mode="edge")
    level_below = stacked[:, :-2]
    level_above = stacked[:, 2:]
    speed_y = courant[0]
    speed_x = courant[1]
    transport = (
        jnp.maximum(speed_y, 0.0) * (values - south_side)
        + jnp.minimum(speed_y, 0.0) * (north_side - values)
        + jnp.maximum(speed_x, 0.0) * (values - west_side)
        + jnp.minimum(speed_x, 0.0) * (east_side - values)
    )
    spread = south_side + north_side + west_side + east_side - 4.0 * values
    column = level_below + level_above - 2.0 * values
    return values - transport + diffusion * spread + mixing * column


def send_rims(values, distance):
    return shifted(values, "section", distance)


def general_on_device(state, courant, nest_offset):
    fields, levels, row_count, col_count = state.shape
    tile_count = lax.axis_size("tile")
    section_count = lax.axis_size("section")
    parent_count = section_count // 4
    tile_index = lax.axis_index("tile")
    section = lax.axis_index("section")
    offset = nest_offset[0]
    total_rows = row_count * tile_count
    nest_height = total_rows // RATIO
    third_width = col_count // RATIO
    coarse_rows = row_count // RATIO
    parent_width = parent_count * col_count
    nest_width = section_count * col_count - parent_width
    is_parent = section < parent_count
    low_row = tile_index == 0
    high_row = tile_index == tile_count - 1
    low_col = (section == 0) | (section == parent_count)
    high_col = (section == parent_count - 1) | (section == section_count - 1)

    def step(values):
        padded = with_halo(values, (("tile", 2), ("section", 3)), 1)
        return advance(values, courant, padded, low_row, high_row, low_col, high_col)

    stepped = step(state)
    local_rows = tile_index * row_count + jnp.arange(row_count, dtype=jnp.int32)
    rim_coarse = jnp.array([0, 1, nest_height - 2, nest_height - 1], dtype=jnp.int32)
    wanted = offset + rim_coarse
    pick_rows = (wanted[:, None] == local_rows[None, :]).astype(jnp.float32)
    parent_flag = is_parent.astype(jnp.float32)
    both_states = jnp.stack([state, stepped]) * parent_flag
    rim_part = jnp.einsum(
        "jr,tflrc->tfljc", pick_rows, both_states, precision=lax.Precision.HIGHEST
    )
    edge_cols = jnp.array([0, 1, parent_width - 2, parent_width - 1], dtype=jnp.int32)
    global_cols = section * col_count + jnp.arange(col_count, dtype=jnp.int32)
    pick_edge = (global_cols[:, None] == edge_cols[None, :]).astype(jnp.float32)
    edge_local = jnp.einsum(
        "tflrc,ck->tflrk", both_states, pick_edge, precision=lax.Precision.HIGHEST
    )
    span_rows = offset + jnp.arange(nest_height, dtype=jnp.int32)
    pick_span = (span_rows[:, None] == local_rows[None, :]).astype(jnp.float32)
    edge_part = jnp.einsum(
        "nr,tflrk->tflnk", pick_span, edge_local, precision=lax.Precision.HIGHEST
    )
    packed = jnp.concatenate(
        [
            rim_part.reshape(2 * fields * levels, 4 * col_count),
            edge_part.reshape(2 * fields * levels, nest_height * 4),
        ],
        axis=1,
    )
    summed = lax.psum(packed, "tile")
    nest_index = jnp.maximum(section - parent_count, 0)
    source_parent = nest_index // RATIO
    received = jnp.zeros_like(summed)
    for distance in range(parent_count, 3 * parent_count + 1):
        arrived = send_rims(summed, distance)
        hit = jnp.logical_not(is_parent) & (section - distance == source_parent)
        received = jnp.where(hit, arrived, received)
    rim_rows = received[:, : 4 * col_count].reshape(2, fields, levels, 4, col_count)
    edges = received[:, 4 * col_count :].reshape(2, fields, levels, nest_height, 4)
    rim_strip = lax.dynamic_slice_in_dim(rim_rows, nest_index % RATIO * third_width, third_width, 4)
    rim_strip = jnp.repeat(rim_strip, RATIO, axis=4)
    row_choice = ((local_rows // RATIO)[:, None] == rim_coarse[None, :]).astype(jnp.float32)
    forcing_rows = jnp.einsum(
        "rj,tfljc->tflrc", row_choice, rim_strip, precision=lax.Precision.HIGHEST
    )
    nest_cols = nest_index * col_count + jnp.arange(col_count, dtype=jnp.int32)
    col_choice = (edge_cols[:, None] == (nest_cols // RATIO)[None, :]).astype(jnp.float32)
    coarse_choice = (
        (local_rows // RATIO)[:, None] == jnp.arange(nest_height, dtype=jnp.int32)[None, :]
    ).astype(jnp.float32)
    edge_rows = jnp.einsum("rn,tflnk->tflrk", coarse_choice, edges, precision=lax.Precision.HIGHEST)
    forcing_cols = jnp.einsum(
        "tflrk,kc->tflrc", edge_rows, col_choice, precision=lax.Precision.HIGHEST
    )
    row_depth = jnp.minimum(local_rows, total_rows - 1 - local_rows)
    col_depth = jnp.minimum(nest_cols, nest_width - 1 - nest_cols)
    row_zone = (row_depth < ZONE)[:, None]
    forcing = jnp.where(row_zone, forcing_rows, forcing_cols)
    depth = jnp.minimum(row_depth[:, None], col_depth[None, :])
    weight = jnp.maximum(ZONE - depth, 0).astype(jnp.float32) / ZONE

    def relax(values, substep):
        fraction = (substep + 1) / RATIO
        target = forcing[0] + fraction * (forcing[1] - forcing[0])
        return values + weight * (target - values)

    nest_field = relax(stepped, 0)
    for substep in range(1, RATIO):
        nest_field = relax(step(nest_field), substep)
    block_means = nest_field.reshape(fields, levels, coarse_rows, RATIO, third_width, RATIO).sum(
        axis=(3, 5)
    ) / (RATIO * RATIO)
    wanted_nest = local_rows - offset
    portion = lax.all_gather(block_means, "tile", axis=2, tiled=True)
    row_span = portion.shape[2]
    select = (wanted_nest[:, None] == jnp.arange(row_span, dtype=jnp.int32)[None, :]).astype(
        jnp.float32
    )
    gathered = jnp.einsum("rs,flsc->flrc", select, portion, precision=lax.Precision.HIGHEST)
    target_slot = jnp.where(is_parent, -1, (section - parent_count) // RATIO)
    slot_index = jnp.arange(section_count, dtype=jnp.int32)
    outbound = jnp.where(
        (slot_index == target_slot)[None, None, None, :, None], gathered[:, :, :, None, :], 0.0
    )
    outbound = outbound.reshape(fields, levels, row_count, section_count * third_width)
    received_means = lax.all_to_all(outbound, "section", split_axis=3, concat_axis=3, tiled=True)
    start_col = (parent_count + RATIO * jnp.minimum(section, parent_count - 1)) * third_width
    feedback = lax.dynamic_slice_in_dim(received_means, start_col, col_count, 3)
    covered = ((wanted_nest >= 0) & (wanted_nest < nest_height))[:, None]
    parent_final = jnp.where(covered, feedback, stepped)
    return jnp.where(is_parent, parent_final, nest_field)


ROWS = 24
COLS = 384
LANE = 128
STATES = 10
PLANES = 14
SLOTS = 4 * PLANES
HALO = SLOTS + 8
RIMS = 3 * ROWS


def device(tile, section):
    return tile * 4 + section


def device_mark(tile, section):
    return (device(tile, section) + 1).astype(jnp.float32)


def third(value):
    return (value * 43) >> 7


def iota(shape, dim):
    return lax.broadcasted_iota(jnp.int32, shape, dim)


def parts(value):
    high = value.astype(jnp.bfloat16)
    rest = value - high.astype(jnp.float32)
    middle = rest.astype(jnp.bfloat16)
    return high, middle, (rest - middle.astype(jnp.float32)).astype(jnp.bfloat16)


def product(a, b):
    return jnp.dot(a, b, preferred_element_type=jnp.float32)


def choose(ones, value):
    return sum(product(ones.astype(jnp.bfloat16), part) for part in parts(value))


def turn(value, steps, dim):
    size = value.shape[dim]
    steps = steps % size
    return pltpu.roll(value, steps, dim) if steps else value


def plane_of(state_ref, courant_ref, p):
    return state_ref[p] if p < STATES else courant_ref[p - STATES]


def pack_kernel(
    offset_ref, state_ref, courant_ref, west_ref, middle_ref, east_ref, pair_ref, cross_ref
):
    tile = lax.axis_index("tile")
    section = lax.axis_index("section")
    offset = offset_ref[0]
    first = tile * ROWS
    lane = iota((ROWS, LANE), 1)
    left = jnp.zeros((ROWS, LANE), jnp.float32)
    right = jnp.zeros((ROWS, LANE), jnp.float32)
    for p in range(PLANES):
        source = plane_of(state_ref, courant_ref, p)
        mine = (lane >= 3 * p) & (lane < 3 * p + 3)
        left = jnp.where(mine, turn(source[:, :LANE], 3 * p, 1), left)
        right = jnp.where(mine, turn(source[:, COLS - LANE :], 3 * p - (LANE - 3), 1), right)
    top = (first <= offset + 2) & (first + ROWS - 1 >= offset - 1)
    base = jnp.where(top, offset - 1, offset + 61) - first

    def chosen(count):
        slot = iota((4 * count, ROWS * count), 0)
        column = iota((4 * count, ROWS * count), 1)
        local = base + (slot & 3)
        hit = (local >= 0) & (local < ROWS) & (column == (slot >> 2) * ROWS + local)
        return hit.astype(jnp.float32)

    rows = jnp.concatenate(
        [
            choose(chosen(STATES), state_ref[...].reshape(STATES * ROWS, COLS)),
            choose(chosen(4), courant_ref[...].reshape(4 * ROWS, COLS)),
        ],
        axis=0,
    )
    lane = iota((SLOTS, LANE), 1)
    mark = device_mark(tile, section)
    blank = jnp.zeros((SLOTS, LANE), jnp.float32)
    both = jnp.where(iota((ROWS, LANE), 1) < 42, left, turn(right, 64, 1))
    outs = ((west_ref, left), (middle_ref, both), (east_ref, right))
    for s, (out_ref, edge) in enumerate(outs):
        before = rows[:, LANE * (s - 1) : LANE * s] if s > 0 else blank
        after = rows[:, LANE * (s + 1) : LANE * (s + 2)] if s < 2 else blank
        extra = turn(jnp.where(lane < 2, after, before), 44, 1)
        side = jnp.where(
            (lane >= 42) & (lane < 46), extra, jnp.where(lane == LANE - 1, mark, 0.0)
        )
        out_ref[:, :LANE] = rows[:, LANE * s : LANE * (s + 1)]
        free = (lane[:ROWS] >= 42) & (lane[:ROWS] < 64) | (lane[:ROWS] == LANE - 1)
        out_ref[:ROWS, LANE:] = jnp.where(free, side[:ROWS], edge)
        out_ref[ROWS:, LANE:] = side[ROWS:]


    even = tile % 2 == 0
    for p in range(PLANES):
        source = plane_of(state_ref, courant_ref, p)
        head, tail = source[:4], source[ROWS - 4 :]
        pair_ref[4 * p : 4 * p + 4] = jnp.where(even, tail, head)
        cross_ref[4 * p : 4 * p + 4] = jnp.where(even, head, tail)


def first_source(start, tile):
    return start - 1 + jnp.minimum(tile // 2, 2)


def across_chips(tile):
    return jnp.where(tile % 2 == 0, tile - 1, tile + 1)


def relay_kernel(start, middles, to_pair_ref, from_cross_ref, *refs):
    to_east, middle, to_west = refs[:3], refs[3 : 3 + middles], refs[3 + middles : 6 + middles]
    west_ref, east_ref, rims_ref, pair_ref, cross_ref = refs[6 + middles :]
    pair_ref[:SLOTS] = to_pair_ref[...]
    pair_ref[SLOTS + 4 : HALO] = jnp.zeros((HALO - SLOTS - 4, COLS), jnp.float32)
    cross_ref[...] = from_cross_ref[...]
    tile = lax.axis_index("tile")
    section = lax.axis_index("section")
    even = tile % 2 == 0
    lane = iota((ROWS, LANE), 1)
    first = first_source(start, tile)
    sources = [device_mark(first + slot, 0) for slot in range(3)]
    has_east = (section == 1) | (section == 2)
    has_west = (section == 2) | (section == 3)
    corner = across_chips(tile)
    east_mark = jnp.where(has_east, device_mark(tile, section + 1), 0.0)
    west_mark = jnp.where(has_west, device_mark(tile, section - 1), 0.0)
    far_east_mark = jnp.where(has_east, device_mark(corner, section + 1), 0.0)
    far_west_mark = jnp.where(has_west, device_mark(corner, section - 1), 0.0)
    nothing = jnp.zeros((ROWS, LANE), jnp.float32)
    east = west = far_east = far_west = nothing
    edges = [nothing] * 3
    center = side = jnp.zeros((SLOTS, LANE), jnp.float32)
    targets = [3] * 3 + [2] * middles + [1] * 3
    for ref, target in zip(to_east + middle + to_west, targets):
        tail = ref[:, LANE:]
        mark = jnp.broadcast_to(tail[:, LANE - 1 :], (SLOTS, LANE))
        marks = [jnp.where(section == target, source, 0.0) for source in sources]
        hit = (mark == marks[0]) | (mark == marks[1]) | (mark == marks[2])
        center = jnp.where(hit, center + ref[:, :LANE], center)
        side = jnp.where(hit, side + tail, side)
        mark, cells = mark[:ROWS], tail[:ROWS]
        if target == 2:
            marks = [jnp.where(section == 2, 0.0, source) for source in sources]
            cells = jnp.where(section == 3, turn(cells, -64, 1), cells)
        edges = [jnp.where(mark == one, cells, edge) for one, edge in zip(marks, edges)]
        if target < 3:
            east = jnp.where(mark == east_mark, cells, east)
            far_east = jnp.where(mark == far_east_mark, cells, far_east)
        if target > 1:
            west = jnp.where(mark == west_mark, cells, west)
            far_west = jnp.where(mark == far_west_mark, cells, far_west)
    edges = [jnp.where(lane < 42, value, 0.0) for value in edges]
    for lanes, out_ref, value, far in (
        (slice(0, LANE), west_ref, west, far_west),
        (slice(LANE, 2 * LANE), east_ref, east, far_east),
    ):
        out_ref[:ROWS] = value
        out_ref[ROWS : ROWS + 4] = jnp.where(even, far[ROWS - 4 :], far[:4])
        out_ref[ROWS + 4 :] = jnp.zeros((4, LANE), jnp.float32)
        pair_ref[SLOTS : SLOTS + 4, lanes] = jnp.where(even, value[ROWS - 4 :], value[:4])
    wide = iota((SLOTS, LANE), 1)
    rims_ref[:SLOTS, :LANE] = center
    rims_ref[SLOTS:, :LANE] = jnp.zeros((RIMS - SLOTS, LANE), jnp.float32)
    extra = jnp.where((wide >= 42) & (wide < 46), side, 0.0)
    extra = jnp.concatenate([extra, jnp.zeros((RIMS - SLOTS, LANE), jnp.float32)], axis=0)
    rims_ref[:, LANE:] = jnp.concatenate(edges, axis=0) + extra
    pair_ref[HALO:, : 2 * LANE] = rims_ref[...]


def flux(value, south, north, west, east, other, cy, cx):
    transport = (
        jnp.maximum(cy, 0.0) * (value - south)
        + jnp.minimum(cy, 0.0) * (north - value)
        + jnp.maximum(cx, 0.0) * (value - west)
        + jnp.minimum(cx, 0.0) * (east - value)
    )
    spread = south + north + west + east - 4.0 * value
    return diffusion * spread + mixing * (other - value) - transport


def main_kernel(
    offset_ref,
    state_ref,
    courant_ref,
    west_ref,
    east_ref,
    rims_ref,
    pair_ref,
    cross_ref,
    out_ref,
    means_ref,
    here,
    there,
    factors,
    column_force,
    row_force,
    narrowed,
):
    tile = lax.axis_index("tile")
    section = lax.axis_index("section")
    offset = offset_ref[0]
    even = tile % 2 == 0
    is_nest = section > 0
    full = (32, 4 * LANE)

    after = jnp.where(even, pair_ref[:SLOTS], cross_ref[...])
    before = jnp.where(even, cross_ref[...], pair_ref[:SLOTS])

    def beside(ref, lanes):
        inside, outside = pair_ref[SLOTS : SLOTS + 4, lanes], ref[ROWS : ROWS + 4]
        last = [jnp.where(even, inside, outside), jnp.where(even, outside, inside)]
        return jnp.concatenate([ref[:ROWS]] + last, axis=0)

    wests = beside(west_ref, slice(0, LANE))
    easts = beside(east_ref, slice(LANE, 2 * LANE))
    lane = iota((32, LANE), 1)

    def ring(p):
        tail = jnp.concatenate([after[4 * p : 4 * p + 4], before[4 * p : 4 * p + 4]], axis=0)
        cells = jnp.concatenate([plane_of(state_ref, courant_ref, p), tail], axis=0)
        outside = jnp.where(
            lane < 3,
            turn(easts, -3 * p, 1),
            jnp.where(lane >= LANE - 3, turn(wests, LANE - 3 - 3 * p, 1), 0.0),
        )
        return jnp.concatenate([cells, outside], axis=1)

    for p in range(STATES):
        here[p] = ring(p)

    row = iota(full, 0)
    column = iota(full, 1)
    near_row = jnp.where(row < 28, row, row - 32)
    near_column = jnp.where(column < 448, column, column - 512)
    grid_row = near_row + tile * ROWS
    grid_column = near_column + (section - 1) * COLS
    row_depth = jnp.minimum(grid_row, 8 * ROWS - 1 - grid_row)
    column_depth = jnp.minimum(grid_column, 3 * COLS - 1 - grid_column)
    depth = jnp.maximum(jnp.minimum(row_depth, column_depth), 0)
    weight = jnp.maximum(ZONE - depth, 0).astype(jnp.float32) / ZONE
    weight = jnp.where(is_nest, weight, 0.0)
    keep = 1.0 - weight
    no_south = row == jnp.where(tile == 0, 0, -1)
    no_north = row == jnp.where(tile == 7, ROWS - 1, -1)
    no_west = column == jnp.where(section < 2, 0, -1)
    no_east = column == jnp.where((section == 0) | (section == 3), COLS - 1, -1)
    for level in range(2):
        cy = ring(STATES + level)
        cx = ring(STATES + 2 + level)
        from_south = jnp.maximum(cy, 0.0) + diffusion
        from_north = diffusion - jnp.minimum(cy, 0.0)
        from_west = jnp.maximum(cx, 0.0) + diffusion
        from_east = diffusion - jnp.minimum(cx, 0.0)
        from_south = jnp.where(no_south, 0.0, from_south)
        from_north = jnp.where(no_north, 0.0, from_north)
        from_west = jnp.where(no_west, 0.0, from_west)
        from_east = jnp.where(no_east, 0.0, from_east)
        own = (1.0 - mixing) - (from_south + from_north + from_west + from_east)
        factors[level, 0] = own * keep
        factors[level, 1] = from_south * keep
        factors[level, 2] = from_north * keep
        factors[level, 3] = from_west * keep
        factors[level, 4] = from_east * keep
    factors[0, 5] = mixing * keep

    rims = rims_ref[...] + pair_ref[HALO:, : 2 * LANE]
    on_left = section == 1
    on_right = section == 3
    at_first = is_nest & (tile == 0)
    at_last = is_nest & (tile == 7)

    @pl.when(on_left | on_right)
    def _():
        edges = rims[:, LANE:]
        start = offset + tile * 8 - 2 - first_source(jnp.maximum((offset - 2) // ROWS, 1), tile) * ROWS
        value = pltpu.roll(edges, RIMS - start, 0)[:16]
        short = iota((16, LANE), 1)
        place = short - 3 * third(short)
        west = jnp.where(place == jnp.where(on_left, 0, -1), value, turn(value, 1, 1))
        east = jnp.where(place == jnp.where(on_left, -1, 2), value, turn(value, -1, 1))
        other = jnp.where((third(short) & 1) == 0, turn(value, -3, 1), turn(value, 3, 1))
        cy = jnp.zeros((16, LANE), jnp.float32)
        cx = jnp.zeros((16, LANE), jnp.float32)
        for field in range(STATES // 2):
            mine = (short >= 6 * field) & (short < 6 * field + 6)
            cy = jnp.where(mine, turn(value, 6 * field - 3 * STATES, 1), cy)
            cx = jnp.where(mine, turn(value, 6 * field - 3 * STATES - 6, 1), cx)
        change = (
            flux(value, turn(value, 1, 0), turn(value, -1, 0), west, east, other, cy, cx) / RATIO
        )
        eight = iota((8, LANE), 0)

        def tall(narrow):
            tiles = []
            for block in range(4):
                rows = [8 * block + i for i in range(8)]
                under = [(i if i < 28 else i - 32) // RATIO + 2 for i in rows]
                tile_rows = jnp.broadcast_to(narrow[under[0] : under[0] + 1], (8, LANE))
                for i in range(1, 8):
                    if under[i] != under[i - 1]:
                        tile_rows = jnp.where(eight >= i, narrow[under[i] : under[i] + 1], tile_rows)
                tiles.append(tile_rows)
            return jnp.concatenate(tiles, axis=0)

        wide_value, wide_change = tall(value), tall(change)

        def place_side(lanes, first, split):
            free = row_depth[:, lanes] >= ZONE
            share = jnp.where(free, weight[:, lanes], 0.0)
            for p in range(STATES):
                for kind, source in enumerate((wide_value, wide_change)):
                    at = 3 * p + first
                    near, far = source[:, at : at + 1], source[:, at + 1 : at + 2]
                    column_force[kind, p] = share * jnp.where(lane < split, near, far)

        @pl.when(on_left)
        def _():
            place_side(slice(0, LANE), 0, 3)

        @pl.when(on_right)
        def _():
            place_side(slice(2 * LANE, 3 * LANE), 1, LANE - 3)

    @pl.when(at_first | at_last)
    def _():
        wide = iota((8, 2 * LANE), 1)
        short = iota((8, LANE), 1)
        eight = iota((8, 4 * LANE), 0)
        outside = turn(rims[:SLOTS, LANE:], 84, 1)
        rows = jnp.concatenate([rims[:SLOTS, :LANE], outside], axis=1)
        cy = rows[4 * STATES : 4 * STATES + 8]
        cx = rows[4 * STATES + 8 :]
        under = [((short + LANE * i) * 171) >> 9 for i in range(3)]

        def stretch(value):
            inside = [
                jnp.take_along_axis(value[:, :LANE], i, axis=1, mode="promise_in_bounds")
                for i in under
            ]
            after_last = value[:, LANE : LANE + 1]
            before_first = value[:, 2 * LANE - 1 :]
            beside = jnp.where(
                short < 3, after_last, jnp.where(short >= LANE - 3, before_first, 0.0)
            )
            return jnp.concatenate(inside + [beside], axis=1)

        forces = []
        for field in range(STATES // 2):
            value = rows[8 * field : 8 * field + 8]
            west = jnp.where(wide == jnp.where(section == 1, 0, -1), value, turn(value, 1, 1))
            east = jnp.where(
                wide == jnp.where(section == 3, LANE - 1, -1), value, turn(value, -1, 1)
            )
            south, north, other = turn(value, 1, 0), turn(value, -1, 0), turn(value, 4, 0)
            change = flux(value, south, north, west, east, other, cy, cx) / RATIO
            forces.append((stretch(value), stretch(change)))

        def place_rows(rows, split):
            share = jnp.where(row_depth[rows] < ZONE, weight[rows], 0.0)
            for p in range(STATES):
                at = 4 * (p % 2)
                for kind in range(2):
                    source = forces[p // 2][kind]
                    near, far = source[at + 1 : at + 2], source[at + 2 : at + 3]
                    row_force[kind, p] = share * jnp.where(eight < split, near, far)

        @pl.when(at_first)
        def _():
            place_rows(slice(0, 8), 3)

        @pl.when(at_last)
        def _():
            place_rows(slice(16, 24), 5)

    def substep(source, target, number, rows, lanes):
        def per_field(field, carry):
            values = [source[2 * field + level] for level in range(2)]
            for level in range(2):
                value = values[level]
                factor = [factors[level, i, rows, lanes] for i in range(5)]
                result = factor[0] * value[rows, lanes]
                result += factors[0, 5, rows, lanes] * values[1 - level][rows, lanes]
                result += factor[1] * turn(value, 1, 0)[rows, lanes]
                result += factor[2] * turn(value, -1, 0)[rows, lanes]
                result += factor[3] * turn(value, 1, 1)[rows, lanes]
                result += factor[4] * turn(value, -1, 1)[rows, lanes]
                target[2 * field + level] = result
            return carry

        lax.fori_loop(0, STATES // 2, per_field, 0)

        def push(force, rows, lanes, part):
            def per_plane(p, carry):
                amount = force[0, p][part] + float(number) * force[1, p][part]
                target[p, rows, lanes] = target[p, rows, lanes] + amount
                return carry

            lax.fori_loop(0, STATES, per_plane, 0, unroll=2)

        for where, section_lanes in ((on_left, slice(0, LANE)), (on_right, slice(2 * LANE, COLS))):

            @pl.when(where)
            def _():
                push(column_force, rows, section_lanes, (rows, slice(None)))

        for where, tile_rows in ((at_first, slice(0, 8)), (at_last, slice(16, 24))):

            @pl.when(where)
            def _():
                push(row_force, tile_rows, lanes, (slice(None), lanes))

    @pl.when(is_nest)
    def _():
        substep(here, there, 1, slice(0, 32), slice(0, 4 * LANE))
        substep(there, here, 2, slice(0, 32), slice(0, 4 * LANE))

    substep(here, out_ref, 3, slice(0, ROWS), slice(0, COLS))

    @pl.when(is_nest)
    def _():
        columns = iota((COLS, LANE), 1) * RATIO
        source = iota((COLS, LANE), 0)
        gather = ((source >= columns) & (source < columns + RATIO)).astype(jnp.bfloat16)
        cells = out_ref[...].reshape(STATES * ROWS, COLS)
        narrowed[...] = sum(product(part, gather) for part in parts(cells))
        total = sum(narrowed[pl.ds(i, STATES * 8, stride=RATIO), :] for i in range(RATIO))
        means_ref[...] = total / (RATIO * RATIO)


def ring_step(tile):
    return 7 - 4 * (((tile + 1) % 4) // 2)


def merge_kernel(offset_ref, *refs):
    *block_refs, stepped_ref, out_ref, near = refs
    tile = lax.axis_index("tile")
    section = lax.axis_index("section")
    offset = offset_ref[0]
    rest = offset % 8

    @pl.when(section > 0)
    def _():
        out_ref[...] = stepped_ref[...]

    @pl.when(section == 0)
    def _():
        mate = tile ^ 1
        sources = [tile, mate]
        for one in (tile, mate):
            sources += [one ^ ring_step(one), one ^ (10 - ring_step(one)), one ^ 4]
        for step in range(4):
            wanted = 3 * tile - offset // 8 - 1 + step
            for source, block_ref in zip(sources, block_refs):

                @pl.when(wanted == source)
                def _():
                    near[step] = block_ref[...]

        nest_row = tile * ROWS + iota((ROWS, COLS), 0) - offset
        covered = (nest_row >= 0) & (nest_row < 64)
        for p in range(STATES):
            parts = [near[step, 8 * p : 8 * p + 8] for step in range(4)]
            moved = pltpu.roll(jnp.concatenate(parts, axis=0), rest + 24, 0)
            out_ref[p] = jnp.where(covered, moved[:ROWS], stepped_ref[p])


VMEM = pl.BlockSpec(memory_space=pltpu.VMEM)
SMEM = pl.BlockSpec(memory_space=pltpu.SMEM)


def shaped(*shape):
    return jax.ShapeDtypeStruct(shape, jnp.float32)


def in_rounds(edges, count):
    at = {}
    for source, target in edges:
        mine, theirs = ("from", source), ("to", target)
        a = next(c for c in range(count) if (mine, c) not in at)
        b = next(c for c in range(count) if (theirs, c) not in at)
        path = []
        node, color = theirs, a
        while (node, color) in at:
            node_next = at[(node, color)]
            path.append((node, node_next, color))
            node, color = node_next, (b if color == a else a)
        for one, two, color in path:
            del at[(one, color)], at[(two, color)]
        for one, two, color in path:
            swapped = b if color == a else a
            at[(one, swapped)] = two
            at[(two, swapped)] = one
        at[(mine, a)] = theirs
        at[(theirs, a)] = mine
    rounds = [[] for _ in range(count)]
    for (node, color), other in sorted(at.items()):
        if node[0] == "from":
            rounds[color].append((node[1], other[1]))
    return rounds


def hops(one, two):
    (t, s), (u, r) = divmod(one, 4), divmod(two, 4)
    links = abs((t >> 2) - (u >> 2)) + abs(((t >> 1) & 1) - ((u >> 1) & 1)) + abs(s - r)
    return links or 0.8


def completed(pairs, valid):
    senders = [d for d in range(32) if d not in {a for a, _ in pairs}]
    takers = [d for d in range(32) if d not in {b for _, b in pairs}]

    def cost(a, b):
        from_parent = a % 4 == 0 and b % 4 > 0
        return 1e3 if a == b or from_parent or (a, b) in valid else hops(a, b) ** 3

    n = len(senders)
    row_price, column_price = [0.0] * (n + 1), [0.0] * (n + 1)
    owner = [0] * (n + 1)
    for i in range(1, n + 1):
        owner[0] = i
        column = 0
        least, before, used = [1e9] * (n + 1), [0] * (n + 1), [False] * (n + 1)
        while True:
            used[column] = True
            row, step, best = owner[column], 1e9, 0
            for j in range(1, n + 1):
                if not used[j]:
                    gap = cost(senders[row - 1], takers[j - 1]) - row_price[row] - column_price[j]
                    if gap < least[j]:
                        least[j], before[j] = gap, column
                    if least[j] < step:
                        step, best = least[j], j
            for j in range(n + 1):
                if used[j]:
                    row_price[owner[j]] += step
                    column_price[j] -= step
                else:
                    least[j] -= step
            column = best
            if owner[column] == 0:
                break
        while column:
            owner[column], column = owner[before[column]], before[column]
    return pairs + [(senders[owner[j] - 1], takers[j - 1]) for j in range(1, n + 1)]


def rim_pairs(case):
    start = max(case, 1)
    sends = {
        1: [(0, 0), (1, 1), (0, 2), (1, 3), (2, 3), (2, 4), (1, 5), (3, 4), (2, 6), (3, 7)],
        3: [(0, 0), (1, 1), (0, 2), (1, 3), (2, 2), (2, 4), (1, 5), (3, 5), (2, 6), (3, 7)],
    }
    corners = {low: low + 1 for low in (1, 3, 5)}
    corners.update({high: low for low, high in list(corners.items())})
    crowded = [(device(4, 2), device(3, 1)), (device(3, 2), device(4, 1))]
    crowded += [(device(1, 2), device(2, 3)), (device(6, 2), device(5, 3))]
    middle = [[(start, 0), (start + 1, 1), (start + 2, 6), (start + 3, 7)]]
    middle = [[(device(a, 0), device(b, 2)) for a, b in pairs] for pairs in middle]
    middle[0] += crowded
    if case == 0:
        middle.append([(device(0, 0), device(0, 2)), (device(2, 0), device(6, 1))])
        middle.append([(device(2, 0), device(6, 3))])
    groups = []
    for section, inner, order in (
        (1, ((2, 1), (3, 2)), (2, 0, 1)),
        (3, ((1, 2), (2, 3)), (1, 2, 0)),
    ):
        edges = [(device(t, a), device(t, b)) for a, b in inner for t in range(8)]
        edges += [(device(corners[t], a), device(t, b)) for a, b in inner for t in corners]
        edges = [pair for pair in edges if pair not in crowded]
        edges += [(device(start + a, 0), device(b, section)) for a, b in sends[section]]
        if start == 1:
            edges.append((device(0, 0), device(0, section)))
        rounds = in_rounds(edges, 3)
        groups.append([completed(rounds[i], edges) for i in order])
    middle = [completed(pairs, []) for pairs in middle]
    return groups[0], middle, groups[1]


BOTH = ("tile", "section")


def on_device(state, courant, nest_offset):
    planes = state.reshape(STATES, ROWS, COLS)
    speeds = courant.reshape(4, ROWS, COLS)
    offset = nest_offset[0]
    *payloads, to_pair, to_cross = pl.pallas_call(
        pack_kernel,
        out_shape=[shaped(SLOTS, 2 * LANE)] * 3
        + [shaped(SLOTS, COLS)] * 2,
        in_specs=[SMEM, VMEM, VMEM],
        out_specs=[VMEM] * 5,
        name="pack",
    )(nest_offset, planes, speeds)

    pair_map = [(device(t, s), device(t ^ 1, s)) for t in range(8) for s in range(4)]
    cross_map = [(device(t, s), device(t ^ ring_step(t), s)) for t in range(8) for s in range(4)]

    def send_rims(case, to_pair, to_cross, west, middle, east):
        from_cross = lax.ppermute(to_cross, BOTH, cross_map)
        groups = rim_pairs(case)
        west, middle, east = (
            [lax.ppermute(value, BOTH, pairs) for pairs in lists]
            for value, lists in zip((west, middle, east), groups)
        )
        return pl.pallas_call(
            functools.partial(relay_kernel, max(case, 1), len(middle)),
            out_shape=[
                shaped(32, LANE),
                shaped(32, LANE),
                shaped(RIMS, 2 * LANE),
                shaped(HALO + RIMS, COLS),
                shaped(SLOTS, COLS),
            ],
            in_specs=[VMEM] * (8 + len(middle)),
            out_specs=[VMEM] * 5,
            name="relay",
        )(to_pair, from_cross, *east, *middle, *west)

    west, east, rims, to_pair, from_cross = lax.switch(
        (offset - 2) // ROWS,
        [functools.partial(send_rims, case) for case in range(4)],
        to_pair,
        to_cross,
        *payloads,
    )
    from_pair = lax.ppermute(to_pair, BOTH, pair_map)
    stepped, means = pl.pallas_call(
        main_kernel,
        out_shape=[shaped(STATES, ROWS, COLS), shaped(STATES * 8, LANE)],
        in_specs=[SMEM] + [VMEM] * 7,
        out_specs=[VMEM] * 2,
        scratch_shapes=[
            pltpu.VMEM((STATES, 32, 4 * LANE), jnp.float32),
            pltpu.VMEM((STATES, 32, 4 * LANE), jnp.float32),
            pltpu.VMEM((2, 6, 32, 4 * LANE), jnp.float32),
            pltpu.VMEM((2, STATES, 32, LANE), jnp.float32),
            pltpu.VMEM((2, STATES, 8, 4 * LANE), jnp.float32),
            pltpu.VMEM((STATES * ROWS, LANE), jnp.float32),
        ],
        compiler_params=pltpu.CompilerParams(vmem_limit_bytes=32 * 1024 * 1024),
        name="nest",
    )(nest_offset, planes, speeds, west, east, rims, from_pair, from_cross)
    def gather_from(s):
        pairs = [(device(t, s), device(t, 0)) for t in range(8)]
        if s == 2:
            pairs = completed(pairs, [])
        return lax.ppermute(means, BOTH, pairs)

    got = {s: gather_from(s) for s in (1, 2, 3)}
    columns = jnp.concatenate([got[s] for s in (1, 2, 3)], axis=1)

    def across(value, partner):
        pairs = [(device(t, s), device(partner(t), s)) for t in range(8) for s in range(4)]
        return lax.ppermute(value, BOTH, pairs)

    def mate(t):
        return t ^ 1

    ways = (lambda t: t ^ ring_step(t), lambda t: t ^ (10 - ring_step(t)), lambda t: t ^ 4)
    blocks = [columns, across(columns, mate)]
    blocks += [across(columns, way) for way in ways]
    blocks += [across(block, mate) for block in blocks[2:]]
    merged = pl.pallas_call(
        merge_kernel,
        out_shape=shaped(STATES, ROWS, COLS),
        in_specs=[SMEM] + [VMEM] * 9,
        out_specs=VMEM,
        scratch_shapes=[pltpu.VMEM((4, STATES * 8, COLS), jnp.float32)],
        compiler_params=pltpu.CompilerParams(vmem_limit_bytes=32 * 1024 * 1024),
        name="merge",
    )(nest_offset, *blocks, stepped)
    return merged.reshape(state.shape)


def solution(mesh):
    small = mesh.shape["tile"] == 8 and mesh.shape["section"] == 4
    return jax.shard_map(
        on_device if small else general_on_device,
        mesh=mesh,
        in_specs=(P(None, None, "tile", "section"), P(None, None, "tile", "section"), P()),
        out_specs=P(None, None, "tile", "section"),
        check_vma=False,
    )
```

```python
import functools

import jax
import jax.numpy as jnp
from jax import lax
from jax.experimental import pallas as pl
from jax.experimental.pallas import tpu as pltpu
from jax.sharding import PartitionSpec as P

RATIO = 3
ZONE = 5


diffusion = 0.02
mixing = 0.05


def shifted(value, axis, steps):
    count = lax.axis_size(axis)
    leading, last = (max(0, -steps), min(count, count - steps))
    return lax.ppermute(value, axis, [(source, source + steps) for source in range(leading, last)])


def with_halo(block, sides, width):
    for axis, dim in sides:
        count = lax.axis_size(axis)
        forward = [(i, i + 1) for i in range(count - 1)]
        backward = [(target, source) for source, target in forward]
        low = lax.ppermute(
            lax.slice_in_dim(block, block.shape[dim] - width, None, axis=dim), axis, forward
        )
        high = lax.ppermute(lax.slice_in_dim(block, 0, width, axis=dim), axis, backward)
        block = jnp.concatenate([low, block, high], axis=dim)
    return block


def advance(values, courant, padded, low_row, high_row, low_col, high_col):
    row_count = values.shape[2]
    col_count = values.shape[3]
    row_index = lax.broadcasted_iota(jnp.int32, (1, 1, row_count, col_count), 2)
    column_index = lax.broadcasted_iota(jnp.int32, (1, 1, row_count, col_count), 3)
    south_side = jnp.where(low_row & (row_index == 0), values, padded[:, :, :-2, 1:-1])
    north_side = jnp.where(high_row & (row_index == row_count - 1), values, padded[:, :, 2:, 1:-1])
    west_side = jnp.where(low_col & (column_index == 0), values, padded[:, :, 1:-1, :-2])
    east_side = jnp.where(
        high_col & (column_index == col_count - 1), values, padded[:, :, 1:-1, 2:]
    )
    stacked = jnp.pad(values, ((0, 0), (1, 1), (0, 0), (0, 0)), mode="edge")
    level_below = stacked[:, :-2]
    level_above = stacked[:, 2:]
    speed_y = courant[0]
    speed_x = courant[1]
    transport = (
        jnp.maximum(speed_y, 0.0) * (values - south_side)
        + jnp.minimum(speed_y, 0.0) * (north_side - values)
        + jnp.maximum(speed_x, 0.0) * (values - west_side)
        + jnp.minimum(speed_x, 0.0) * (east_side - values)
    )
    spread = south_side + north_side + west_side + east_side - 4.0 * values
    column = level_below + level_above - 2.0 * values
    return values - transport + diffusion * spread + mixing * column


def send_rims(values, distance):
    return shifted(values, "section", distance)


def general_on_device(state, courant, nest_offset):
    fields, levels, row_count, col_count = state.shape
    tile_count = lax.axis_size("tile")
    section_count = lax.axis_size("section")
    parent_count = section_count // 4
    tile_index = lax.axis_index("tile")
    section = lax.axis_index("section")
    offset = nest_offset[0]
    total_rows = row_count * tile_count
    nest_height = total_rows // RATIO
    third_width = col_count // RATIO
    coarse_rows = row_count // RATIO
    parent_width = parent_count * col_count
    nest_width = section_count * col_count - parent_width
    is_parent = section < parent_count
    low_row = tile_index == 0
    high_row = tile_index == tile_count - 1
    low_col = (section == 0) | (section == parent_count)
    high_col = (section == parent_count - 1) | (section == section_count - 1)

    def step(values):
        padded = with_halo(values, (("tile", 2), ("section", 3)), 1)
        return advance(values, courant, padded, low_row, high_row, low_col, high_col)

    stepped = step(state)
    local_rows = tile_index * row_count + jnp.arange(row_count, dtype=jnp.int32)
    rim_coarse = jnp.array([0, 1, nest_height - 2, nest_height - 1], dtype=jnp.int32)
    wanted = offset + rim_coarse
    pick_rows = (wanted[:, None] == local_rows[None, :]).astype(jnp.float32)
    parent_flag = is_parent.astype(jnp.float32)
    both_states = jnp.stack([state, stepped]) * parent_flag
    rim_part = jnp.einsum(
        "jr,tflrc->tfljc", pick_rows, both_states, precision=lax.Precision.HIGHEST
    )
    edge_cols = jnp.array([0, 1, parent_width - 2, parent_width - 1], dtype=jnp.int32)
    global_cols = section * col_count + jnp.arange(col_count, dtype=jnp.int32)
    pick_edge = (global_cols[:, None] == edge_cols[None, :]).astype(jnp.float32)
    edge_local = jnp.einsum(
        "tflrc,ck->tflrk", both_states, pick_edge, precision=lax.Precision.HIGHEST
    )
    span_rows = offset + jnp.arange(nest_height, dtype=jnp.int32)
    pick_span = (span_rows[:, None] == local_rows[None, :]).astype(jnp.float32)
    edge_part = jnp.einsum(
        "nr,tflrk->tflnk", pick_span, edge_local, precision=lax.Precision.HIGHEST
    )
    packed = jnp.concatenate(
        [
            rim_part.reshape(2 * fields * levels, 4 * col_count),
            edge_part.reshape(2 * fields * levels, nest_height * 4),
        ],
        axis=1,
    )
    summed = lax.psum(packed, "tile")
    nest_index = jnp.maximum(section - parent_count, 0)
    source_parent = nest_index // RATIO
    received = jnp.zeros_like(summed)
    for distance in range(parent_count, 3 * parent_count + 1):
        arrived = send_rims(summed, distance)
        hit = jnp.logical_not(is_parent) & (section - distance == source_parent)
        received = jnp.where(hit, arrived, received)
    rim_rows = received[:, : 4 * col_count].reshape(2, fields, levels, 4, col_count)
    edges = received[:, 4 * col_count :].reshape(2, fields, levels, nest_height, 4)
    rim_strip = lax.dynamic_slice_in_dim(rim_rows, nest_index % RATIO * third_width, third_width, 4)
    rim_strip = jnp.repeat(rim_strip, RATIO, axis=4)
    row_choice = ((local_rows // RATIO)[:, None] == rim_coarse[None, :]).astype(jnp.float32)
    forcing_rows = jnp.einsum(
        "rj,tfljc->tflrc", row_choice, rim_strip, precision=lax.Precision.HIGHEST
    )
    nest_cols = nest_index * col_count + jnp.arange(col_count, dtype=jnp.int32)
    col_choice = (edge_cols[:, None] == (nest_cols // RATIO)[None, :]).astype(jnp.float32)
    coarse_choice = (
        (local_rows // RATIO)[:, None] == jnp.arange(nest_height, dtype=jnp.int32)[None, :]
    ).astype(jnp.float32)
    edge_rows = jnp.einsum("rn,tflnk->tflrk", coarse_choice, edges, precision=lax.Precision.HIGHEST)
    forcing_cols = jnp.einsum(
        "tflrk,kc->tflrc", edge_rows, col_choice, precision=lax.Precision.HIGHEST
    )
    row_depth = jnp.minimum(local_rows, total_rows - 1 - local_rows)
    col_depth = jnp.minimum(nest_cols, nest_width - 1 - nest_cols)
    row_zone = (row_depth < ZONE)[:, None]
    forcing = jnp.where(row_zone, forcing_rows, forcing_cols)
    depth = jnp.minimum(row_depth[:, None], col_depth[None, :])
    weight = jnp.maximum(ZONE - depth, 0).astype(jnp.float32) / ZONE

    def relax(values, substep):
        fraction = (substep + 1) / RATIO
        target = forcing[0] + fraction * (forcing[1] - forcing[0])
        return values + weight * (target - values)

    nest_field = relax(stepped, 0)
    for substep in range(1, RATIO):
        nest_field = relax(step(nest_field), substep)
    block_means = nest_field.reshape(fields, levels, coarse_rows, RATIO, third_width, RATIO).sum(
        axis=(3, 5)
    ) / (RATIO * RATIO)
    wanted_nest = local_rows - offset
    portion = lax.all_gather(block_means, "tile", axis=2, tiled=True)
    row_span = portion.shape[2]
    select = (wanted_nest[:, None] == jnp.arange(row_span, dtype=jnp.int32)[None, :]).astype(
        jnp.float32
    )
    gathered = jnp.einsum("rs,flsc->flrc", select, portion, precision=lax.Precision.HIGHEST)
    target_slot = jnp.where(is_parent, -1, (section - parent_count) // RATIO)
    slot_index = jnp.arange(section_count, dtype=jnp.int32)
    outbound = jnp.where(
        (slot_index == target_slot)[None, None, None, :, None], gathered[:, :, :, None, :], 0.0
    )
    outbound = outbound.reshape(fields, levels, row_count, section_count * third_width)
    received_means = lax.all_to_all(outbound, "section", split_axis=3, concat_axis=3, tiled=True)
    start_col = (parent_count + RATIO * jnp.minimum(section, parent_count - 1)) * third_width
    feedback = lax.dynamic_slice_in_dim(received_means, start_col, col_count, 3)
    covered = ((wanted_nest >= 0) & (wanted_nest < nest_height))[:, None]
    parent_final = jnp.where(covered, feedback, stepped)
    return jnp.where(is_parent, parent_final, nest_field)


ROWS = 24
COLS = 384
LANE = 128
STATES = 10
PLANES = 14
SLOTS = 4 * PLANES
HALO = SLOTS + 8
RIMS = 3 * ROWS


def device(tile, section):
    return tile * 4 + section


def device_mark(tile, section):
    return (device(tile, section) + 1).astype(jnp.float32)


def third(value):
    return (value * 43) >> 7


def iota(shape, dim):
    return lax.broadcasted_iota(jnp.int32, shape, dim)


def parts(value):
    high = value.astype(jnp.bfloat16)
    rest = value - high.astype(jnp.float32)
    middle = rest.astype(jnp.bfloat16)
    return high, middle, (rest - middle.astype(jnp.float32)).astype(jnp.bfloat16)


def product(a, b):
    return jnp.dot(a, b, preferred_element_type=jnp.float32)


def choose(ones, value):
    return sum(product(ones.astype(jnp.bfloat16), part) for part in parts(value))


def turn(value, steps, dim):
    size = value.shape[dim]
    steps = steps % size
    return pltpu.roll(value, steps, dim) if steps else value


def plane_of(state_ref, courant_ref, p):
    return state_ref[p] if p < STATES else courant_ref[p - STATES]


def pack_kernel(
    offset_ref, state_ref, courant_ref, west_ref, middle_ref, east_ref, pair_ref, cross_ref
):
    tile = lax.axis_index("tile")
    section = lax.axis_index("section")
    offset = offset_ref[0]
    first = tile * ROWS
    lane = iota((ROWS, LANE), 1)
    left = jnp.zeros((ROWS, LANE), jnp.float32)
    right = jnp.zeros((ROWS, LANE), jnp.float32)
    for p in range(PLANES):
        source = plane_of(state_ref, courant_ref, p)
        mine = (lane >= 3 * p) & (lane < 3 * p + 3)
        left = jnp.where(mine, turn(source[:, :LANE], 3 * p, 1), left)
        right = jnp.where(mine, turn(source[:, COLS - LANE :], 3 * p - (LANE - 3), 1), right)
    top = (first <= offset + 2) & (first + ROWS - 1 >= offset - 1)
    base = jnp.where(top, offset - 1, offset + 61) - first

    def chosen(count):
        slot = iota((4 * count, ROWS * count), 0)
        column = iota((4 * count, ROWS * count), 1)
        local = base + (slot & 3)
        hit = (local >= 0) & (local < ROWS) & (column == (slot >> 2) * ROWS + local)
        return hit.astype(jnp.float32)

    rows = jnp.concatenate(
        [
            choose(chosen(STATES), state_ref[...].reshape(STATES * ROWS, COLS)),
            choose(chosen(4), courant_ref[...].reshape(4 * ROWS, COLS)),
        ],
        axis=0,
    )
    lane = iota((SLOTS, LANE), 1)
    mark = device_mark(tile, section)
    blank = jnp.zeros((SLOTS, LANE), jnp.float32)
    both = jnp.where(iota((ROWS, LANE), 1) < 42, left, turn(right, 64, 1))
    outs = ((west_ref, left), (middle_ref, both), (east_ref, right))
    for s, (out_ref, edge) in enumerate(outs):
        before = rows[:, LANE * (s - 1) : LANE * s] if s > 0 else blank
        after = rows[:, LANE * (s + 1) : LANE * (s + 2)] if s < 2 else blank
        extra = turn(jnp.where(lane < 2, after, before), 44, 1)
        side = jnp.where(
            (lane >= 42) & (lane < 46), extra, jnp.where(lane == LANE - 1, mark, 0.0)
        )
        out_ref[:, :LANE] = rows[:, LANE * s : LANE * (s + 1)]
        free = (lane[:ROWS] >= 42) & (lane[:ROWS] < 64) | (lane[:ROWS] == LANE - 1)
        out_ref[:ROWS, LANE:] = jnp.where(free, side[:ROWS], edge)
        out_ref[ROWS:, LANE:] = side[ROWS:]


    even = tile % 2 == 0
    for p in range(PLANES):
        source = plane_of(state_ref, courant_ref, p)
        head, tail = source[:4], source[ROWS - 4 :]
        pair_ref[4 * p : 4 * p + 4] = jnp.where(even, tail, head)
        cross_ref[4 * p : 4 * p + 4] = jnp.where(even, head, tail)


def first_source(start, tile):
    return start - 1 + jnp.minimum(tile // 2, 2)


def across_chips(tile):
    return jnp.where(tile % 2 == 0, tile - 1, tile + 1)


def relay_kernel(start, middles, to_pair_ref, from_cross_ref, *refs):
    to_east, middle, to_west = refs[:3], refs[3 : 3 + middles], refs[3 + middles : 6 + middles]
    west_ref, east_ref, rims_ref, pair_ref, cross_ref = refs[6 + middles :]
    pair_ref[:SLOTS] = to_pair_ref[...]
    pair_ref[SLOTS + 4 : HALO] = jnp.zeros((HALO - SLOTS - 4, COLS), jnp.float32)
    cross_ref[...] = from_cross_ref[...]
    tile = lax.axis_index("tile")
    section = lax.axis_index("section")
    even = tile % 2 == 0
    lane = iota((ROWS, LANE), 1)
    first = first_source(start, tile)
    sources = [device_mark(first + slot, 0) for slot in range(3)]
    has_east = (section == 1) | (section == 2)
    has_west = (section == 2) | (section == 3)
    corner = across_chips(tile)
    east_mark = jnp.where(has_east, device_mark(tile, section + 1), 0.0)
    west_mark = jnp.where(has_west, device_mark(tile, section - 1), 0.0)
    far_east_mark = jnp.where(has_east, device_mark(corner, section + 1), 0.0)
    far_west_mark = jnp.where(has_west, device_mark(corner, section - 1), 0.0)
    nothing = jnp.zeros((ROWS, LANE), jnp.float32)
    east = west = far_east = far_west = nothing
    edges = [nothing] * 3
    center = side = jnp.zeros((SLOTS, LANE), jnp.float32)
    targets = [3] * 3 + [2] * middles + [1] * 3
    for ref, target in zip(to_east + middle + to_west, targets):
        tail = ref[:, LANE:]
        mark = jnp.broadcast_to(tail[:, LANE - 1 :], (SLOTS, LANE))
        marks = [jnp.where(section == target, source, 0.0) for source in sources]
        hit = (mark == marks[0]) | (mark == marks[1]) | (mark == marks[2])
        center = jnp.where(hit, center + ref[:, :LANE], center)
        side = jnp.where(hit, side + tail, side)
        mark, cells = mark[:ROWS], tail[:ROWS]
        if target == 2:
            marks = [jnp.where(section == 2, 0.0, source) for source in sources]
            cells = jnp.where(section == 3, turn(cells, -64, 1), cells)
        edges = [jnp.where(mark == one, cells, edge) for one, edge in zip(marks, edges)]
        if target < 3:
            east = jnp.where(mark == east_mark, cells, east)
            far_east = jnp.where(mark == far_east_mark, cells, far_east)
        if target > 1:
            west = jnp.where(mark == west_mark, cells, west)
            far_west = jnp.where(mark == far_west_mark, cells, far_west)
    edges = [jnp.where(lane < 42, value, 0.0) for value in edges]
    for lanes, out_ref, value, far in (
        (slice(0, LANE), west_ref, west, far_west),
        (slice(LANE, 2 * LANE), east_ref, east, far_east),
    ):
        out_ref[:ROWS] = value
        out_ref[ROWS : ROWS + 4] = jnp.where(even, far[ROWS - 4 :], far[:4])
        out_ref[ROWS + 4 :] = jnp.zeros((4, LANE), jnp.float32)
        pair_ref[SLOTS : SLOTS + 4, lanes] = jnp.where(even, value[ROWS - 4 :], value[:4])
    wide = iota((SLOTS, LANE), 1)
    rims_ref[:SLOTS, :LANE] = center
    rims_ref[SLOTS:, :LANE] = jnp.zeros((RIMS - SLOTS, LANE), jnp.float32)
    extra = jnp.where((wide >= 42) & (wide < 46), side, 0.0)
    extra = jnp.concatenate([extra, jnp.zeros((RIMS - SLOTS, LANE), jnp.float32)], axis=0)
    rims_ref[:, LANE:] = jnp.concatenate(edges, axis=0) + extra
    pair_ref[HALO:, : 2 * LANE] = rims_ref[...]


def flux(value, south, north, west, east, other, cy, cx):
    transport = (
        jnp.maximum(cy, 0.0) * (value - south)
        + jnp.minimum(cy, 0.0) * (north - value)
        + jnp.maximum(cx, 0.0) * (value - west)
        + jnp.minimum(cx, 0.0) * (east - value)
    )
    spread = south + north + west + east - 4.0 * value
    return diffusion * spread + mixing * (other - value) - transport


def main_kernel(
    offset_ref,
    state_ref,
    courant_ref,
    west_ref,
    east_ref,
    rims_ref,
    pair_ref,
    cross_ref,
    out_ref,
    means_ref,
    here,
    there,
    factors,
    column_force,
    row_force,
    narrowed,
):
    tile = lax.axis_index("tile")
    section = lax.axis_index("section")
    offset = offset_ref[0]
    even = tile % 2 == 0
    is_nest = section > 0
    full = (32, 4 * LANE)

    after = jnp.where(even, pair_ref[:SLOTS], cross_ref[...])
    before = jnp.where(even, cross_ref[...], pair_ref[:SLOTS])

    def beside(ref, lanes):
        inside, outside = pair_ref[SLOTS : SLOTS + 4, lanes], ref[ROWS : ROWS + 4]
        last = [jnp.where(even, inside, outside), jnp.where(even, outside, inside)]
        return jnp.concatenate([ref[:ROWS]] + last, axis=0)

    wests = beside(west_ref, slice(0, LANE))
    easts = beside(east_ref, slice(LANE, 2 * LANE))
    lane = iota((32, LANE), 1)

    def ring(p):
        tail = jnp.concatenate([after[4 * p : 4 * p + 4], before[4 * p : 4 * p + 4]], axis=0)
        cells = jnp.concatenate([plane_of(state_ref, courant_ref, p), tail], axis=0)
        outside = jnp.where(
            lane < 3,
            turn(easts, -3 * p, 1),
            jnp.where(lane >= LANE - 3, turn(wests, LANE - 3 - 3 * p, 1), 0.0),
        )
        return jnp.concatenate([cells, outside], axis=1)

    for p in range(STATES):
        here[p] = ring(p)

    row = iota(full, 0)
    column = iota(full, 1)
    near_row = jnp.where(row < 28, row, row - 32)
    near_column = jnp.where(column < 448, column, column - 512)
    grid_row = near_row + tile * ROWS
    grid_column = near_column + (section - 1) * COLS
    row_depth = jnp.minimum(grid_row, 8 * ROWS - 1 - grid_row)
    column_depth = jnp.minimum(grid_column, 3 * COLS - 1 - grid_column)
    depth = jnp.maximum(jnp.minimum(row_depth, column_depth), 0)
    weight = jnp.maximum(ZONE - depth, 0).astype(jnp.float32) / ZONE
    weight = jnp.where(is_nest, weight, 0.0)
    keep = 1.0 - weight
    no_south = row == jnp.where(tile == 0, 0, -1)
    no_north = row == jnp.where(tile == 7, ROWS - 1, -1)
    no_west = column == jnp.where(section < 2, 0, -1)
    no_east = column == jnp.where((section == 0) | (section == 3), COLS - 1, -1)
    for level in range(2):
        cy = ring(STATES + level)
        cx = ring(STATES + 2 + level)
        from_south = jnp.maximum(cy, 0.0) + diffusion
        from_north = diffusion - jnp.minimum(cy, 0.0)
        from_west = jnp.maximum(cx, 0.0) + diffusion
        from_east = diffusion - jnp.minimum(cx, 0.0)
        from_south = jnp.where(no_south, 0.0, from_south)
        from_north = jnp.where(no_north, 0.0, from_north)
        from_west = jnp.where(no_west, 0.0, from_west)
        from_east = jnp.where(no_east, 0.0, from_east)
        own = (1.0 - mixing) - (from_south + from_north + from_west + from_east)
        factors[level, 0] = own * keep
        factors[level, 1] = from_south * keep
        factors[level, 2] = from_north * keep
        factors[level, 3] = from_west * keep
        factors[level, 4] = from_east * keep
    factors[0, 5] = mixing * keep

    rims = rims_ref[...] + pair_ref[HALO:, : 2 * LANE]
    on_left = section == 1
    on_right = section == 3
    at_first = is_nest & (tile == 0)
    at_last = is_nest & (tile == 7)

    @pl.when(on_left | on_right)
    def _():
        edges = rims[:, LANE:]
        start = offset + tile * 8 - 2 - first_source(jnp.maximum((offset - 2) // ROWS, 1), tile) * ROWS
        value = pltpu.roll(edges, RIMS - start, 0)[:16]
        short = iota((16, LANE), 1)
        place = short - 3 * third(short)
        west = jnp.where(place == jnp.where(on_left, 0, -1), value, turn(value, 1, 1))
        east = jnp.where(place == jnp.where(on_left, -1, 2), value, turn(value, -1, 1))
        other = jnp.where((third(short) & 1) == 0, turn(value, -3, 1), turn(value, 3, 1))
        cy = jnp.zeros((16, LANE), jnp.float32)
        cx = jnp.zeros((16, LANE), jnp.float32)
        for field in range(STATES // 2):
            mine = (short >= 6 * field) & (short < 6 * field + 6)
            cy = jnp.where(mine, turn(value, 6 * field - 3 * STATES, 1), cy)
            cx = jnp.where(mine, turn(value, 6 * field - 3 * STATES - 6, 1), cx)
        change = (
            flux(value, turn(value, 1, 0), turn(value, -1, 0), west, east, other, cy, cx) / RATIO
        )
        eight = iota((8, LANE), 0)

        def tall(narrow):
            tiles = []
            for block in range(4):
                rows = [8 * block + i for i in range(8)]
                under = [(i if i < 28 else i - 32) // RATIO + 2 for i in rows]
                tile_rows = jnp.broadcast_to(narrow[under[0] : under[0] + 1], (8, LANE))
                for i in range(1, 8):
                    if under[i] != under[i - 1]:
                        tile_rows = jnp.where(eight >= i, narrow[under[i] : under[i] + 1], tile_rows)
                tiles.append(tile_rows)
            return jnp.concatenate(tiles, axis=0)

        wide_value, wide_change = tall(value), tall(change)

        def place_side(lanes, first, split):
            free = row_depth[:, lanes] >= ZONE
            share = jnp.where(free, weight[:, lanes], 0.0)
            for p in range(STATES):
                for kind, source in enumerate((wide_value, wide_change)):
                    at = 3 * p + first
                    near, far = source[:, at : at + 1], source[:, at + 1 : at + 2]
                    column_force[kind, p] = share * jnp.where(lane < split, near, far)

        @pl.when(on_left)
        def _():
            place_side(slice(0, LANE), 0, 3)

        @pl.when(on_right)
        def _():
            place_side(slice(2 * LANE, 3 * LANE), 1, LANE - 3)

    @pl.when(at_first | at_last)
    def _():
        wide = iota((8, 2 * LANE), 1)
        short = iota((8, LANE), 1)
        eight = iota((8, 4 * LANE), 0)
        outside = turn(rims[:SLOTS, LANE:], 84, 1)
        rows = jnp.concatenate([rims[:SLOTS, :LANE], outside], axis=1)
        cy = rows[4 * STATES : 4 * STATES + 8]
        cx = rows[4 * STATES + 8 :]
        under = [((short + LANE * i) * 171) >> 9 for i in range(3)]

        def stretch(value):
            inside = [
                jnp.take_along_axis(value[:, :LANE], i, axis=1, mode="promise_in_bounds")
                for i in under
            ]
            after_last = value[:, LANE : LANE + 1]
            before_first = value[:, 2 * LANE - 1 :]
            beside = jnp.where(
                short < 3, after_last, jnp.where(short >= LANE - 3, before_first, 0.0)
            )
            return jnp.concatenate(inside + [beside], axis=1)

        forces = []
        for field in range(STATES // 2):
            value = rows[8 * field : 8 * field + 8]
            west = jnp.where(wide == jnp.where(section == 1, 0, -1), value, turn(value, 1, 1))
            east = jnp.where(
                wide == jnp.where(section == 3, LANE - 1, -1), value, turn(value, -1, 1)
            )
            south, north, other = turn(value, 1, 0), turn(value, -1, 0), turn(value, 4, 0)
            change = flux(value, south, north, west, east, other, cy, cx) / RATIO
            forces.append((stretch(value), stretch(change)))

        def place_rows(rows, split):
            share = jnp.where(row_depth[rows] < ZONE, weight[rows], 0.0)
            for p in range(STATES):
                at = 4 * (p % 2)
                for kind in range(2):
                    source = forces[p // 2][kind]
                    near, far = source[at + 1 : at + 2], source[at + 2 : at + 3]
                    row_force[kind, p] = share * jnp.where(eight < split, near, far)

        @pl.when(at_first)
        def _():
            place_rows(slice(0, 8), 3)

        @pl.when(at_last)
        def _():
            place_rows(slice(16, 24), 5)

    def substep(source, target, number, rows, lanes):
        def per_field(field, carry):
            values = [source[2 * field + level] for level in range(2)]
            for level in range(2):
                value = values[level]
                factor = [factors[level, i, rows, lanes] for i in range(5)]
                result = factor[0] * value[rows, lanes]
                result += factors[0, 5, rows, lanes] * values[1 - level][rows, lanes]
                result += factor[1] * turn(value, 1, 0)[rows, lanes]
                result += factor[2] * turn(value, -1, 0)[rows, lanes]
                result += factor[3] * turn(value, 1, 1)[rows, lanes]
                result += factor[4] * turn(value, -1, 1)[rows, lanes]
                target[2 * field + level] = result
            return carry

        lax.fori_loop(0, STATES // 2, per_field, 0, unroll=True)

        def push(force, rows, lanes, part):
            def per_plane(p, carry):
                amount = force[0, p][part] + float(number) * force[1, p][part]
                target[p, rows, lanes] = target[p, rows, lanes] + amount
                return carry

            lax.fori_loop(0, STATES, per_plane, 0, unroll=True)

        for where, section_lanes in ((on_left, slice(0, LANE)), (on_right, slice(2 * LANE, COLS))):

            @pl.when(where)
            def _():
                push(column_force, rows, section_lanes, (rows, slice(None)))

        for where, tile_rows in ((at_first, slice(0, 8)), (at_last, slice(16, 24))):

            @pl.when(where)
            def _():
                push(row_force, tile_rows, lanes, (slice(None), lanes))

    @pl.when(is_nest)
    def _():
        substep(here, there, 1, slice(0, 32), slice(0, 4 * LANE))
        substep(there, here, 2, slice(0, 32), slice(0, 4 * LANE))

    substep(here, out_ref, 3, slice(0, ROWS), slice(0, COLS))

    @pl.when(is_nest)
    def _():
        columns = iota((COLS, LANE), 1) * RATIO
        source = iota((COLS, LANE), 0)
        gather = ((source >= columns) & (source < columns + RATIO)).astype(jnp.bfloat16)
        cells = out_ref[...].reshape(STATES * ROWS, COLS)
        narrowed[...] = sum(product(part, gather) for part in parts(cells))
        total = sum(narrowed[pl.ds(i, STATES * 8, stride=RATIO), :] for i in range(RATIO))
        means_ref[...] = total / (RATIO * RATIO)


def ring_step(tile):
    return 7 - 4 * (((tile + 1) % 4) // 2)


def merge_kernel(offset_ref, *refs):
    *block_refs, stepped_ref, out_ref, near = refs
    tile = lax.axis_index("tile")
    section = lax.axis_index("section")
    offset = offset_ref[0]
    rest = offset % 8

    @pl.when(section > 0)
    def _():
        out_ref[...] = stepped_ref[...]

    @pl.when(section == 0)
    def _():
        mate = tile ^ 1
        sources = [tile, mate]
        for one in (tile, mate):
            sources += [one ^ ring_step(one), one ^ (10 - ring_step(one)), one ^ 4]
        for step in range(4):
            wanted = 3 * tile - offset // 8 - 1 + step
            for source, block_ref in zip(sources, block_refs):

                @pl.when(wanted == source)
                def _():
                    near[step] = block_ref[...]

        nest_row = tile * ROWS + iota((ROWS, COLS), 0) - offset
        covered = (nest_row >= 0) & (nest_row < 64)
        for p in range(STATES):
            parts = [near[step, 8 * p : 8 * p + 8] for step in range(4)]
            moved = pltpu.roll(jnp.concatenate(parts, axis=0), rest + 24, 0)
            out_ref[p] = jnp.where(covered, moved[:ROWS], stepped_ref[p])


VMEM = pl.BlockSpec(memory_space=pltpu.VMEM)
SMEM = pl.BlockSpec(memory_space=pltpu.SMEM)


def shaped(*shape):
    return jax.ShapeDtypeStruct(shape, jnp.float32)


def in_rounds(edges, count):
    at = {}
    for source, target in edges:
        mine, theirs = ("from", source), ("to", target)
        a = next(c for c in range(count) if (mine, c) not in at)
        b = next(c for c in range(count) if (theirs, c) not in at)
        path = []
        node, color = theirs, a
        while (node, color) in at:
            node_next = at[(node, color)]
            path.append((node, node_next, color))
            node, color = node_next, (b if color == a else a)
        for one, two, color in path:
            del at[(one, color)], at[(two, color)]
        for one, two, color in path:
            swapped = b if color == a else a
            at[(one, swapped)] = two
            at[(two, swapped)] = one
        at[(mine, a)] = theirs
        at[(theirs, a)] = mine
    rounds = [[] for _ in range(count)]
    for (node, color), other in sorted(at.items()):
        if node[0] == "from":
            rounds[color].append((node[1], other[1]))
    return rounds


def hops(one, two):
    (t, s), (u, r) = divmod(one, 4), divmod(two, 4)
    links = abs((t >> 2) - (u >> 2)) + abs(((t >> 1) & 1) - ((u >> 1) & 1)) + abs(s - r)
    return links or 0.8


def completed(pairs, valid):
    senders = [d for d in range(32) if d not in {a for a, _ in pairs}]
    takers = [d for d in range(32) if d not in {b for _, b in pairs}]

    def cost(a, b):
        from_parent = a % 4 == 0 and b % 4 > 0
        return 1e3 if a == b or from_parent or (a, b) in valid else hops(a, b) ** 3

    n = len(senders)
    row_price, column_price = [0.0] * (n + 1), [0.0] * (n + 1)
    owner = [0] * (n + 1)
    for i in range(1, n + 1):
        owner[0] = i
        column = 0
        least, before, used = [1e9] * (n + 1), [0] * (n + 1), [False] * (n + 1)
        while True:
            used[column] = True
            row, step, best = owner[column], 1e9, 0
            for j in range(1, n + 1):
                if not used[j]:
                    gap = cost(senders[row - 1], takers[j - 1]) - row_price[row] - column_price[j]
                    if gap < least[j]:
                        least[j], before[j] = gap, column
                    if least[j] < step:
                        step, best = least[j], j
            for j in range(n + 1):
                if used[j]:
                    row_price[owner[j]] += step
                    column_price[j] -= step
                else:
                    least[j] -= step
            column = best
            if owner[column] == 0:
                break
        while column:
            owner[column], column = owner[before[column]], before[column]
    return pairs + [(senders[owner[j] - 1], takers[j - 1]) for j in range(1, n + 1)]


def rim_pairs(case):
    start = max(case, 1)
    sends = {
        1: [(0, 0), (1, 1), (0, 2), (1, 3), (2, 3), (2, 4), (1, 5), (3, 4), (2, 6), (3, 7)],
        3: [(0, 0), (1, 1), (0, 2), (1, 3), (2, 2), (2, 4), (1, 5), (3, 5), (2, 6), (3, 7)],
    }
    corners = {low: low + 1 for low in (1, 3, 5)}
    corners.update({high: low for low, high in list(corners.items())})
    crowded = [(device(4, 2), device(3, 1)), (device(3, 2), device(4, 1))]
    crowded += [(device(1, 2), device(2, 3)), (device(6, 2), device(5, 3))]
    middle = [[(start, 0), (start + 1, 1), (start + 2, 6), (start + 3, 7)]]
    middle = [[(device(a, 0), device(b, 2)) for a, b in pairs] for pairs in middle]
    middle[0] += crowded
    if case == 0:
        middle.append([(device(0, 0), device(0, 2)), (device(2, 0), device(6, 1))])
        middle.append([(device(2, 0), device(6, 3))])
    groups = []
    for section, inner, order in (
        (1, ((2, 1), (3, 2)), (2, 0, 1)),
        (3, ((1, 2), (2, 3)), (1, 2, 0)),
    ):
        edges = [(device(t, a), device(t, b)) for a, b in inner for t in range(8)]
        edges += [(device(corners[t], a), device(t, b)) for a, b in inner for t in corners]
        edges = [pair for pair in edges if pair not in crowded]
        edges += [(device(start + a, 0), device(b, section)) for a, b in sends[section]]
        if start == 1:
            edges.append((device(0, 0), device(0, section)))
        rounds = in_rounds(edges, 3)
        groups.append([completed(rounds[i], edges) for i in order])
    middle = [completed(pairs, []) for pairs in middle]
    return groups[0], middle, groups[1]


BOTH = ("tile", "section")


def on_device(state, courant, nest_offset):
    planes = state.reshape(STATES, ROWS, COLS)
    speeds = courant.reshape(4, ROWS, COLS)
    offset = nest_offset[0]
    *payloads, to_pair, to_cross = pl.pallas_call(
        pack_kernel,
        out_shape=[shaped(SLOTS, 2 * LANE)] * 3
        + [shaped(SLOTS, COLS)] * 2,
        in_specs=[SMEM, VMEM, VMEM],
        out_specs=[VMEM] * 5,
        name="pack",
    )(nest_offset, planes, speeds)

    pair_map = [(device(t, s), device(t ^ 1, s)) for t in range(8) for s in range(4)]
    cross_map = [(device(t, s), device(t ^ ring_step(t), s)) for t in range(8) for s in range(4)]

    def send_rims(case, to_pair, to_cross, west, middle, east):
        from_cross = lax.ppermute(to_cross, BOTH, cross_map)
        groups = rim_pairs(case)
        west, middle, east = (
            [lax.ppermute(value, BOTH, pairs) for pairs in lists]
            for value, lists in zip((west, middle, east), groups)
        )
        return pl.pallas_call(
            functools.partial(relay_kernel, max(case, 1), len(middle)),
            out_shape=[
                shaped(32, LANE),
                shaped(32, LANE),
                shaped(RIMS, 2 * LANE),
                shaped(HALO + RIMS, COLS),
                shaped(SLOTS, COLS),
            ],
            in_specs=[VMEM] * (8 + len(middle)),
            out_specs=[VMEM] * 5,
            name="relay",
        )(to_pair, from_cross, *east, *middle, *west)

    west, east, rims, to_pair, from_cross = lax.switch(
        (offset - 2) // ROWS,
        [functools.partial(send_rims, case) for case in range(4)],
        to_pair,
        to_cross,
        *payloads,
    )
    from_pair = lax.ppermute(to_pair, BOTH, pair_map)
    stepped, means = pl.pallas_call(
        main_kernel,
        out_shape=[shaped(STATES, ROWS, COLS), shaped(STATES * 8, LANE)],
        in_specs=[SMEM] + [VMEM] * 7,
        out_specs=[VMEM] * 2,
        scratch_shapes=[
            pltpu.VMEM((STATES, 32, 4 * LANE), jnp.float32),
            pltpu.VMEM((STATES, 32, 4 * LANE), jnp.float32),
            pltpu.VMEM((2, 6, 32, 4 * LANE), jnp.float32),
            pltpu.VMEM((2, STATES, 32, LANE), jnp.float32),
            pltpu.VMEM((2, STATES, 8, 4 * LANE), jnp.float32),
            pltpu.VMEM((STATES * ROWS, LANE), jnp.float32),
        ],
        compiler_params=pltpu.CompilerParams(vmem_limit_bytes=32 * 1024 * 1024),
        name="nest",
    )(nest_offset, planes, speeds, west, east, rims, from_pair, from_cross)
    def gather_from(s):
        pairs = [(device(t, s), device(t, 0)) for t in range(8)]
        if s == 2:
            pairs = completed(pairs, [])
        return lax.ppermute(means, BOTH, pairs)

    got = {s: gather_from(s) for s in (1, 2, 3)}
    columns = jnp.concatenate([got[s] for s in (1, 2, 3)], axis=1)

    def across(value, partner):
        pairs = [(device(t, s), device(partner(t), s)) for t in range(8) for s in range(4)]
        return lax.ppermute(value, BOTH, pairs)

    def mate(t):
        return t ^ 1

    ways = (lambda t: t ^ ring_step(t), lambda t: t ^ (10 - ring_step(t)), lambda t: t ^ 4)
    blocks = [columns, across(columns, mate)]
    blocks += [across(columns, way) for way in ways]
    blocks += [across(block, mate) for block in blocks[2:]]
    merged = pl.pallas_call(
        merge_kernel,
        out_shape=shaped(STATES, ROWS, COLS),
        in_specs=[SMEM] + [VMEM] * 9,
        out_specs=VMEM,
        scratch_shapes=[pltpu.VMEM((4, STATES * 8, COLS), jnp.float32)],
        compiler_params=pltpu.CompilerParams(vmem_limit_bytes=32 * 1024 * 1024),
        name="merge",
    )(nest_offset, *blocks, stepped)
    return merged.reshape(state.shape)


def solution(mesh):
    small = mesh.shape["tile"] == 8 and mesh.shape["section"] == 4
    return jax.shard_map(
        on_device if small else general_on_device,
        mesh=mesh,
        in_specs=(P(None, None, "tile", "section"), P(None, None, "tile", "section"), P()),
        out_specs=P(None, None, "tile", "section"),
        check_vma=False,
    )
```

```python
import functools

import jax
import jax.numpy as jnp
from jax import lax
from jax.experimental import pallas as pl
from jax.experimental.pallas import tpu as pltpu
from jax.sharding import PartitionSpec as P

RATIO = 3
ZONE = 5


diffusion = 0.02
mixing = 0.05


def shifted(value, axis, steps):
    count = lax.axis_size(axis)
    leading, last = (max(0, -steps), min(count, count - steps))
    return lax.ppermute(value, axis, [(source, source + steps) for source in range(leading, last)])


def with_halo(block, sides, width):
    for axis, dim in sides:
        count = lax.axis_size(axis)
        forward = [(i, i + 1) for i in range(count - 1)]
        backward = [(target, source) for source, target in forward]
        low = lax.ppermute(
            lax.slice_in_dim(block, block.shape[dim] - width, None, axis=dim), axis, forward
        )
        high = lax.ppermute(lax.slice_in_dim(block, 0, width, axis=dim), axis, backward)
        block = jnp.concatenate([low, block, high], axis=dim)
    return block


def advance(values, courant, padded, low_row, high_row, low_col, high_col):
    row_count = values.shape[2]
    col_count = values.shape[3]
    row_index = lax.broadcasted_iota(jnp.int32, (1, 1, row_count, col_count), 2)
    column_index = lax.broadcasted_iota(jnp.int32, (1, 1, row_count, col_count), 3)
    south_side = jnp.where(low_row & (row_index == 0), values, padded[:, :, :-2, 1:-1])
    north_side = jnp.where(high_row & (row_index == row_count - 1), values, padded[:, :, 2:, 1:-1])
    west_side = jnp.where(low_col & (column_index == 0), values, padded[:, :, 1:-1, :-2])
    east_side = jnp.where(
        high_col & (column_index == col_count - 1), values, padded[:, :, 1:-1, 2:]
    )
    stacked = jnp.pad(values, ((0, 0), (1, 1), (0, 0), (0, 0)), mode="edge")
    level_below = stacked[:, :-2]
    level_above = stacked[:, 2:]
    speed_y = courant[0]
    speed_x = courant[1]
    transport = (
        jnp.maximum(speed_y, 0.0) * (values - south_side)
        + jnp.minimum(speed_y, 0.0) * (north_side - values)
        + jnp.maximum(speed_x, 0.0) * (values - west_side)
        + jnp.minimum(speed_x, 0.0) * (east_side - values)
    )
    spread = south_side + north_side + west_side + east_side - 4.0 * values
    column = level_below + level_above - 2.0 * values
    return values - transport + diffusion * spread + mixing * column


def send_rims(values, distance):
    return shifted(values, "section", distance)


def general_on_device(state, courant, nest_offset):
    fields, levels, row_count, col_count = state.shape
    tile_count = lax.axis_size("tile")
    section_count = lax.axis_size("section")
    parent_count = section_count // 4
    tile_index = lax.axis_index("tile")
    section = lax.axis_index("section")
    offset = nest_offset[0]
    total_rows = row_count * tile_count
    nest_height = total_rows // RATIO
    third_width = col_count // RATIO
    coarse_rows = row_count // RATIO
    parent_width = parent_count * col_count
    nest_width = section_count * col_count - parent_width
    is_parent = section < parent_count
    low_row = tile_index == 0
    high_row = tile_index == tile_count - 1
    low_col = (section == 0) | (section == parent_count)
    high_col = (section == parent_count - 1) | (section == section_count - 1)

    def step(values):
        padded = with_halo(values, (("tile", 2), ("section", 3)), 1)
        return advance(values, courant, padded, low_row, high_row, low_col, high_col)

    stepped = step(state)
    local_rows = tile_index * row_count + jnp.arange(row_count, dtype=jnp.int32)
    rim_coarse = jnp.array([0, 1, nest_height - 2, nest_height - 1], dtype=jnp.int32)
    wanted = offset + rim_coarse
    pick_rows = (wanted[:, None] == local_rows[None, :]).astype(jnp.float32)
    parent_flag = is_parent.astype(jnp.float32)
    both_states = jnp.stack([state, stepped]) * parent_flag
    rim_part = jnp.einsum(
        "jr,tflrc->tfljc", pick_rows, both_states, precision=lax.Precision.HIGHEST
    )
    edge_cols = jnp.array([0, 1, parent_width - 2, parent_width - 1], dtype=jnp.int32)
    global_cols = section * col_count + jnp.arange(col_count, dtype=jnp.int32)
    pick_edge = (global_cols[:, None] == edge_cols[None, :]).astype(jnp.float32)
    edge_local = jnp.einsum(
        "tflrc,ck->tflrk", both_states, pick_edge, precision=lax.Precision.HIGHEST
    )
    span_rows = offset + jnp.arange(nest_height, dtype=jnp.int32)
    pick_span = (span_rows[:, None] == local_rows[None, :]).astype(jnp.float32)
    edge_part = jnp.einsum(
        "nr,tflrk->tflnk", pick_span, edge_local, precision=lax.Precision.HIGHEST
    )
    packed = jnp.concatenate(
        [
            rim_part.reshape(2 * fields * levels, 4 * col_count),
            edge_part.reshape(2 * fields * levels, nest_height * 4),
        ],
        axis=1,
    )
    summed = lax.psum(packed, "tile")
    nest_index = jnp.maximum(section - parent_count, 0)
    source_parent = nest_index // RATIO
    received = jnp.zeros_like(summed)
    for distance in range(parent_count, 3 * parent_count + 1):
        arrived = send_rims(summed, distance)
        hit = jnp.logical_not(is_parent) & (section - distance == source_parent)
        received = jnp.where(hit, arrived, received)
    rim_rows = received[:, : 4 * col_count].reshape(2, fields, levels, 4, col_count)
    edges = received[:, 4 * col_count :].reshape(2, fields, levels, nest_height, 4)
    rim_strip = lax.dynamic_slice_in_dim(rim_rows, nest_index % RATIO * third_width, third_width, 4)
    rim_strip = jnp.repeat(rim_strip, RATIO, axis=4)
    row_choice = ((local_rows // RATIO)[:, None] == rim_coarse[None, :]).astype(jnp.float32)
    forcing_rows = jnp.einsum(
        "rj,tfljc->tflrc", row_choice, rim_strip, precision=lax.Precision.HIGHEST
    )
    nest_cols = nest_index * col_count + jnp.arange(col_count, dtype=jnp.int32)
    col_choice = (edge_cols[:, None] == (nest_cols // RATIO)[None, :]).astype(jnp.float32)
    coarse_choice = (
        (local_rows // RATIO)[:, None] == jnp.arange(nest_height, dtype=jnp.int32)[None, :]
    ).astype(jnp.float32)
    edge_rows = jnp.einsum("rn,tflnk->tflrk", coarse_choice, edges, precision=lax.Precision.HIGHEST)
    forcing_cols = jnp.einsum(
        "tflrk,kc->tflrc", edge_rows, col_choice, precision=lax.Precision.HIGHEST
    )
    row_depth = jnp.minimum(local_rows, total_rows - 1 - local_rows)
    col_depth = jnp.minimum(nest_cols, nest_width - 1 - nest_cols)
    row_zone = (row_depth < ZONE)[:, None]
    forcing = jnp.where(row_zone, forcing_rows, forcing_cols)
    depth = jnp.minimum(row_depth[:, None], col_depth[None, :])
    weight = jnp.maximum(ZONE - depth, 0).astype(jnp.float32) / ZONE

    def relax(values, substep):
        fraction = (substep + 1) / RATIO
        target = forcing[0] + fraction * (forcing[1] - forcing[0])
        return values + weight * (target - values)

    nest_field = relax(stepped, 0)
    for substep in range(1, RATIO):
        nest_field = relax(step(nest_field), substep)
    block_means = nest_field.reshape(fields, levels, coarse_rows, RATIO, third_width, RATIO).sum(
        axis=(3, 5)
    ) / (RATIO * RATIO)
    wanted_nest = local_rows - offset
    portion = lax.all_gather(block_means, "tile", axis=2, tiled=True)
    row_span = portion.shape[2]
    select = (wanted_nest[:, None] == jnp.arange(row_span, dtype=jnp.int32)[None, :]).astype(
        jnp.float32
    )
    gathered = jnp.einsum("rs,flsc->flrc", select, portion, precision=lax.Precision.HIGHEST)
    target_slot = jnp.where(is_parent, -1, (section - parent_count) // RATIO)
    slot_index = jnp.arange(section_count, dtype=jnp.int32)
    outbound = jnp.where(
        (slot_index == target_slot)[None, None, None, :, None], gathered[:, :, :, None, :], 0.0
    )
    outbound = outbound.reshape(fields, levels, row_count, section_count * third_width)
    received_means = lax.all_to_all(outbound, "section", split_axis=3, concat_axis=3, tiled=True)
    start_col = (parent_count + RATIO * jnp.minimum(section, parent_count - 1)) * third_width
    feedback = lax.dynamic_slice_in_dim(received_means, start_col, col_count, 3)
    covered = ((wanted_nest >= 0) & (wanted_nest < nest_height))[:, None]
    parent_final = jnp.where(covered, feedback, stepped)
    return jnp.where(is_parent, parent_final, nest_field)


ROWS = 24
COLS = 384
LANE = 128
STATES = 10
PLANES = 14
SLOTS = 4 * PLANES
HALO = SLOTS + 8
RIMS = 3 * ROWS


def device(tile, section):
    return tile * 4 + section


def device_mark(tile, section):
    return (device(tile, section) + 1).astype(jnp.float32)


def third(value):
    return (value * 43) >> 7


def iota(shape, dim):
    return lax.broadcasted_iota(jnp.int32, shape, dim)


def parts(value):
    high = value.astype(jnp.bfloat16)
    rest = value - high.astype(jnp.float32)
    middle = rest.astype(jnp.bfloat16)
    return high, middle, (rest - middle.astype(jnp.float32)).astype(jnp.bfloat16)


def product(a, b):
    return jnp.dot(a, b, preferred_element_type=jnp.float32)


def choose(ones, value):
    return sum(product(ones.astype(jnp.bfloat16), part) for part in parts(value))


def turn(value, steps, dim):
    size = value.shape[dim]
    steps = steps % size
    return pltpu.roll(value, steps, dim) if steps else value


def plane_of(state_ref, courant_ref, p):
    return state_ref[p] if p < STATES else courant_ref[p - STATES]


def pack_kernel(
    offset_ref, state_ref, courant_ref, west_ref, middle_ref, east_ref, pair_ref, cross_ref
):
    tile = lax.axis_index("tile")
    section = lax.axis_index("section")
    offset = offset_ref[0]
    first = tile * ROWS
    lane = iota((ROWS, LANE), 1)
    left = jnp.zeros((ROWS, LANE), jnp.float32)
    right = jnp.zeros((ROWS, LANE), jnp.float32)
    for p in range(PLANES):
        source = plane_of(state_ref, courant_ref, p)
        mine = (lane >= 3 * p) & (lane < 3 * p + 3)
        left = jnp.where(mine, turn(source[:, :LANE], 3 * p, 1), left)
        right = jnp.where(mine, turn(source[:, COLS - LANE :], 3 * p - (LANE - 3), 1), right)
    top = (first <= offset + 2) & (first + ROWS - 1 >= offset - 1)
    base = jnp.where(top, offset - 1, offset + 61) - first

    def chosen(count):
        slot = iota((4 * count, ROWS * count), 0)
        column = iota((4 * count, ROWS * count), 1)
        local = base + (slot & 3)
        hit = (local >= 0) & (local < ROWS) & (column == (slot >> 2) * ROWS + local)
        return hit.astype(jnp.float32)

    rows = jnp.concatenate(
        [
            choose(chosen(STATES), state_ref[...].reshape(STATES * ROWS, COLS)),
            choose(chosen(4), courant_ref[...].reshape(4 * ROWS, COLS)),
        ],
        axis=0,
    )
    lane = iota((SLOTS, LANE), 1)
    mark = device_mark(tile, section)
    blank = jnp.zeros((SLOTS, LANE), jnp.float32)
    both = jnp.where(iota((ROWS, LANE), 1) < 42, left, turn(right, 64, 1))
    outs = ((west_ref, left), (middle_ref, both), (east_ref, right))
    for s, (out_ref, edge) in enumerate(outs):
        before = rows[:, LANE * (s - 1) : LANE * s] if s > 0 else blank
        after = rows[:, LANE * (s + 1) : LANE * (s + 2)] if s < 2 else blank
        extra = turn(jnp.where(lane < 2, after, before), 44, 1)
        side = jnp.where(
            (lane >= 42) & (lane < 46), extra, jnp.where(lane == LANE - 1, mark, 0.0)
        )
        out_ref[:, :LANE] = rows[:, LANE * s : LANE * (s + 1)]
        free = (lane[:ROWS] >= 42) & (lane[:ROWS] < 64) | (lane[:ROWS] == LANE - 1)
        out_ref[:ROWS, LANE:] = jnp.where(free, side[:ROWS], edge)
        out_ref[ROWS:, LANE:] = side[ROWS:]


    even = tile % 2 == 0
    for p in range(PLANES):
        source = plane_of(state_ref, courant_ref, p)
        head, tail = source[:4], source[ROWS - 4 :]
        pair_ref[4 * p : 4 * p + 4] = jnp.where(even, tail, head)
        cross_ref[4 * p : 4 * p + 4] = jnp.where(even, head, tail)


def first_source(start, tile):
    return start - 1 + jnp.minimum(tile // 2, 2)


def across_chips(tile):
    return jnp.where(tile % 2 == 0, tile - 1, tile + 1)


def relay_kernel(start, middles, to_pair_ref, from_cross_ref, *refs):
    to_east, middle, to_west = refs[:3], refs[3 : 3 + middles], refs[3 + middles : 6 + middles]
    west_ref, east_ref, rims_ref, pair_ref, cross_ref = refs[6 + middles :]
    pair_ref[:SLOTS] = to_pair_ref[...]
    pair_ref[SLOTS + 4 : HALO] = jnp.zeros((HALO - SLOTS - 4, COLS), jnp.float32)
    cross_ref[...] = from_cross_ref[...]
    tile = lax.axis_index("tile")
    section = lax.axis_index("section")
    even = tile % 2 == 0
    lane = iota((ROWS, LANE), 1)
    first = first_source(start, tile)
    sources = [device_mark(first + slot, 0) for slot in range(3)]
    has_east = (section == 1) | (section == 2)
    has_west = (section == 2) | (section == 3)
    corner = across_chips(tile)
    east_mark = jnp.where(has_east, device_mark(tile, section + 1), 0.0)
    west_mark = jnp.where(has_west, device_mark(tile, section - 1), 0.0)
    far_east_mark = jnp.where(has_east, device_mark(corner, section + 1), 0.0)
    far_west_mark = jnp.where(has_west, device_mark(corner, section - 1), 0.0)
    nothing = jnp.zeros((ROWS, LANE), jnp.float32)
    east = west = far_east = far_west = nothing
    edges = [nothing] * 3
    center = side = jnp.zeros((SLOTS, LANE), jnp.float32)
    targets = [3] * 3 + [2] * middles + [1] * 3
    for ref, target in zip(to_east + middle + to_west, targets):
        tail = ref[:, LANE:]
        mark = jnp.broadcast_to(tail[:, LANE - 1 :], (SLOTS, LANE))
        marks = [jnp.where(section == target, source, 0.0) for source in sources]
        hit = (mark == marks[0]) | (mark == marks[1]) | (mark == marks[2])
        center = jnp.where(hit, center + ref[:, :LANE], center)
        side = jnp.where(hit, side + tail, side)
        mark, cells = mark[:ROWS], tail[:ROWS]
        if target == 2:
            marks = [jnp.where(section == 2, 0.0, source) for source in sources]
            cells = jnp.where(section == 3, turn(cells, -64, 1), cells)
        edges = [jnp.where(mark == one, cells, edge) for one, edge in zip(marks, edges)]
        if target < 3:
            east = jnp.where(mark == east_mark, cells, east)
            far_east = jnp.where(mark == far_east_mark, cells, far_east)
        if target > 1:
            west = jnp.where(mark == west_mark, cells, west)
            far_west = jnp.where(mark == far_west_mark, cells, far_west)
    edges = [jnp.where(lane < 42, value, 0.0) for value in edges]
    for lanes, out_ref, value, far in (
        (slice(0, LANE), west_ref, west, far_west),
        (slice(LANE, 2 * LANE), east_ref, east, far_east),
    ):
        out_ref[:ROWS] = value
        out_ref[ROWS : ROWS + 4] = jnp.where(even, far[ROWS - 4 :], far[:4])
        out_ref[ROWS + 4 :] = jnp.zeros((4, LANE), jnp.float32)
        pair_ref[SLOTS : SLOTS + 4, lanes] = jnp.where(even, value[ROWS - 4 :], value[:4])
    wide = iota((SLOTS, LANE), 1)
    rims_ref[:SLOTS, :LANE] = center
    rims_ref[SLOTS:, :LANE] = jnp.zeros((RIMS - SLOTS, LANE), jnp.float32)
    extra = jnp.where((wide >= 42) & (wide < 46), side, 0.0)
    extra = jnp.concatenate([extra, jnp.zeros((RIMS - SLOTS, LANE), jnp.float32)], axis=0)
    rims_ref[:, LANE:] = jnp.concatenate(edges, axis=0) + extra
    pair_ref[HALO:, : 2 * LANE] = rims_ref[...]


def flux(value, south, north, west, east, other, cy, cx):
    transport = (
        jnp.maximum(cy, 0.0) * (value - south)
        + jnp.minimum(cy, 0.0) * (north - value)
        + jnp.maximum(cx, 0.0) * (value - west)
        + jnp.minimum(cx, 0.0) * (east - value)
    )
    spread = south + north + west + east - 4.0 * value
    return diffusion * spread + mixing * (other - value) - transport


def main_kernel(
    offset_ref,
    state_ref,
    courant_ref,
    west_ref,
    east_ref,
    rims_ref,
    pair_ref,
    cross_ref,
    out_ref,
    means_ref,
    here,
    there,
    factors,
    column_force,
    row_force,
    narrowed,
):
    tile = lax.axis_index("tile")
    section = lax.axis_index("section")
    offset = offset_ref[0]
    even = tile % 2 == 0
    is_nest = section > 0
    full = (32, 4 * LANE)

    after = jnp.where(even, pair_ref[:SLOTS], cross_ref[...])
    before = jnp.where(even, cross_ref[...], pair_ref[:SLOTS])

    def beside(ref, lanes):
        inside, outside = pair_ref[SLOTS : SLOTS + 4, lanes], ref[ROWS : ROWS + 4]
        last = [jnp.where(even, inside, outside), jnp.where(even, outside, inside)]
        return jnp.concatenate([ref[:ROWS]] + last, axis=0)

    wests = beside(west_ref, slice(0, LANE))
    easts = beside(east_ref, slice(LANE, 2 * LANE))
    lane = iota((32, LANE), 1)

    def ring(p):
        tail = jnp.concatenate([after[4 * p : 4 * p + 4], before[4 * p : 4 * p + 4]], axis=0)
        cells = jnp.concatenate([plane_of(state_ref, courant_ref, p), tail], axis=0)
        outside = jnp.where(
            lane < 3,
            turn(easts, -3 * p, 1),
            jnp.where(lane >= LANE - 3, turn(wests, LANE - 3 - 3 * p, 1), 0.0),
        )
        return jnp.concatenate([cells, outside], axis=1)

    for p in range(STATES):
        here[p] = ring(p)

    row = iota(full, 0)
    column = iota(full, 1)
    near_row = jnp.where(row < 28, row, row - 32)
    near_column = jnp.where(column < 448, column, column - 512)
    grid_row = near_row + tile * ROWS
    grid_column = near_column + (section - 1) * COLS
    row_depth = jnp.minimum(grid_row, 8 * ROWS - 1 - grid_row)
    column_depth = jnp.minimum(grid_column, 3 * COLS - 1 - grid_column)
    depth = jnp.maximum(jnp.minimum(row_depth, column_depth), 0)
    weight = jnp.maximum(ZONE - depth, 0).astype(jnp.float32) / ZONE
    weight = jnp.where(is_nest, weight, 0.0)
    keep = 1.0 - weight
    no_south = row == jnp.where(tile == 0, 0, -1)
    no_north = row == jnp.where(tile == 7, ROWS - 1, -1)
    no_west = column == jnp.where(section < 2, 0, -1)
    no_east = column == jnp.where((section == 0) | (section == 3), COLS - 1, -1)
    for level in range(2):
        cy = ring(STATES + level)
        cx = ring(STATES + 2 + level)
        from_south = jnp.maximum(cy, 0.0) + diffusion
        from_north = diffusion - jnp.minimum(cy, 0.0)
        from_west = jnp.maximum(cx, 0.0) + diffusion
        from_east = diffusion - jnp.minimum(cx, 0.0)
        from_south = jnp.where(no_south, 0.0, from_south)
        from_north = jnp.where(no_north, 0.0, from_north)
        from_west = jnp.where(no_west, 0.0, from_west)
        from_east = jnp.where(no_east, 0.0, from_east)
        own = (1.0 - mixing) - (from_south + from_north + from_west + from_east)
        factors[level, 0] = own * keep
        factors[level, 1] = from_south * keep
        factors[level, 2] = from_north * keep
        factors[level, 3] = from_west * keep
        factors[level, 4] = from_east * keep
    factors[0, 5] = mixing * keep

    rims = rims_ref[...] + pair_ref[HALO:, : 2 * LANE]
    on_left = section == 1
    on_right = section == 3
    at_first = is_nest & (tile == 0)
    at_last = is_nest & (tile == 7)

    @pl.when(on_left | on_right)
    def _():
        edges = rims[:, LANE:]
        start = offset + tile * 8 - 2 - first_source(jnp.maximum((offset - 2) // ROWS, 1), tile) * ROWS
        value = pltpu.roll(edges, RIMS - start, 0)[:16]
        short = iota((16, LANE), 1)
        place = short - 3 * third(short)
        west = jnp.where(place == jnp.where(on_left, 0, -1), value, turn(value, 1, 1))
        east = jnp.where(place == jnp.where(on_left, -1, 2), value, turn(value, -1, 1))
        other = jnp.where((third(short) & 1) == 0, turn(value, -3, 1), turn(value, 3, 1))
        cy = jnp.zeros((16, LANE), jnp.float32)
        cx = jnp.zeros((16, LANE), jnp.float32)
        for field in range(STATES // 2):
            mine = (short >= 6 * field) & (short < 6 * field + 6)
            cy = jnp.where(mine, turn(value, 6 * field - 3 * STATES, 1), cy)
            cx = jnp.where(mine, turn(value, 6 * field - 3 * STATES - 6, 1), cx)
        change = (
            flux(value, turn(value, 1, 0), turn(value, -1, 0), west, east, other, cy, cx) / RATIO
        )
        eight = iota((8, LANE), 0)

        def tall(narrow):
            tiles = []
            for block in range(4):
                rows = [8 * block + i for i in range(8)]
                under = [(i if i < 28 else i - 32) // RATIO + 2 for i in rows]
                tile_rows = jnp.broadcast_to(narrow[under[0] : under[0] + 1], (8, LANE))
                for i in range(1, 8):
                    if under[i] != under[i - 1]:
                        tile_rows = jnp.where(eight >= i, narrow[under[i] : under[i] + 1], tile_rows)
                tiles.append(tile_rows)
            return jnp.concatenate(tiles, axis=0)

        wide_value, wide_change = tall(value), tall(change)

        def place_side(lanes, first, split):
            free = row_depth[:, lanes] >= ZONE
            share = jnp.where(free, weight[:, lanes], 0.0)
            for p in range(STATES):
                for kind, source in enumerate((wide_value, wide_change)):
                    at = 3 * p + first
                    near, far = source[:, at : at + 1], source[:, at + 1 : at + 2]
                    column_force[kind, p] = share * jnp.where(lane < split, near, far)

        @pl.when(on_left)
        def _():
            place_side(slice(0, LANE), 0, 3)

        @pl.when(on_right)
        def _():
            place_side(slice(2 * LANE, 3 * LANE), 1, LANE - 3)

    @pl.when(at_first | at_last)
    def _():
        wide = iota((8, 2 * LANE), 1)
        short = iota((8, LANE), 1)
        eight = iota((8, 4 * LANE), 0)
        outside = turn(rims[:SLOTS, LANE:], 84, 1)
        rows = jnp.concatenate([rims[:SLOTS, :LANE], outside], axis=1)
        cy = rows[4 * STATES : 4 * STATES + 8]
        cx = rows[4 * STATES + 8 :]
        under = [((short + LANE * i) * 171) >> 9 for i in range(3)]

        def stretch(value):
            inside = [
                jnp.take_along_axis(value[:, :LANE], i, axis=1, mode="promise_in_bounds")
                for i in under
            ]
            after_last = value[:, LANE : LANE + 1]
            before_first = value[:, 2 * LANE - 1 :]
            beside = jnp.where(
                short < 3, after_last, jnp.where(short >= LANE - 3, before_first, 0.0)
            )
            return jnp.concatenate(inside + [beside], axis=1)

        forces = []
        for field in range(STATES // 2):
            value = rows[8 * field : 8 * field + 8]
            west = jnp.where(wide == jnp.where(section == 1, 0, -1), value, turn(value, 1, 1))
            east = jnp.where(
                wide == jnp.where(section == 3, LANE - 1, -1), value, turn(value, -1, 1)
            )
            south, north, other = turn(value, 1, 0), turn(value, -1, 0), turn(value, 4, 0)
            change = flux(value, south, north, west, east, other, cy, cx) / RATIO
            forces.append((stretch(value), stretch(change)))

        def place_rows(rows, split):
            share = jnp.where(row_depth[rows] < ZONE, weight[rows], 0.0)
            for p in range(STATES):
                at = 4 * (p % 2)
                for kind in range(2):
                    source = forces[p // 2][kind]
                    near, far = source[at + 1 : at + 2], source[at + 2 : at + 3]
                    row_force[kind, p] = share * jnp.where(eight < split, near, far)

        @pl.when(at_first)
        def _():
            place_rows(slice(0, 8), 3)

        @pl.when(at_last)
        def _():
            place_rows(slice(16, 24), 5)

    def substep(source, target, number, rows, lanes):
        def per_field(field, carry):
            values = [source[2 * field + level] for level in range(2)]
            for level in range(2):
                value = values[level]
                factor = [factors[level, i, rows, lanes] for i in range(5)]
                result = factor[0] * value[rows, lanes]
                result += factors[0, 5, rows, lanes] * values[1 - level][rows, lanes]
                result += factor[1] * turn(value, 1, 0)[rows, lanes]
                result += factor[2] * turn(value, -1, 0)[rows, lanes]
                result += factor[3] * turn(value, 1, 1)[rows, lanes]
                result += factor[4] * turn(value, -1, 1)[rows, lanes]
                target[2 * field + level] = result
            return carry

        lax.fori_loop(0, STATES // 2, per_field, 0, unroll=True)

        def push(force, rows, lanes, part):
            def per_plane(p, carry):
                amount = force[0, p][part] + float(number) * force[1, p][part]
                target[p, rows, lanes] = target[p, rows, lanes] + amount
                return carry

            lax.fori_loop(0, STATES, per_plane, 0, unroll=True)

        for where, section_lanes in ((on_left, slice(0, LANE)), (on_right, slice(2 * LANE, COLS))):

            @pl.when(where)
            def _():
                push(column_force, rows, section_lanes, (rows, slice(None)))

        for where, tile_rows in ((at_first, slice(0, 8)), (at_last, slice(16, 24))):

            @pl.when(where)
            def _():
                push(row_force, tile_rows, lanes, (slice(None), lanes))

    @pl.when(is_nest)
    def _():
        substep(here, there, 1, slice(0, 32), slice(0, 4 * LANE))
        substep(there, here, 2, slice(0, 32), slice(0, 4 * LANE))

    substep(here, out_ref, 3, slice(0, ROWS), slice(0, COLS))

    @pl.when(is_nest)
    def _():
        columns = iota((COLS, LANE), 1) * RATIO
        source = iota((COLS, LANE), 0)
        gather = ((source >= columns) & (source < columns + RATIO)).astype(jnp.bfloat16)
        cells = out_ref[...].reshape(STATES * ROWS, COLS)
        narrowed[...] = sum(product(part, gather) for part in parts(cells))
        total = sum(narrowed[pl.ds(i, STATES * 8, stride=RATIO), :] for i in range(RATIO))
        means_ref[...] = total / (RATIO * RATIO)


def ring_step(tile):
    return 7 - 4 * (((tile + 1) % 4) // 2)


def merge_kernel(offset_ref, *refs):
    *block_refs, stepped_ref, out_ref, near = refs
    tile = lax.axis_index("tile")
    section = lax.axis_index("section")
    offset = offset_ref[0]
    rest = offset % 8

    @pl.when(section > 0)
    def _():
        out_ref[...] = stepped_ref[...]

    @pl.when(section == 0)
    def _():
        mate = tile ^ 1
        sources = [tile, mate]
        for one in (tile, mate):
            sources += [one ^ ring_step(one), one ^ (10 - ring_step(one)), one ^ 4]
        for step in range(4):
            wanted = 3 * tile - offset // 8 - 1 + step
            for source, block_ref in zip(sources, block_refs):

                @pl.when(wanted == source)
                def _():
                    near[step] = block_ref[...]

        nest_row = tile * ROWS + iota((ROWS, COLS), 0) - offset
        covered = (nest_row >= 0) & (nest_row < 64)
        for p in range(STATES):
            parts = [near[step, 8 * p : 8 * p + 8] for step in range(4)]
            moved = pltpu.roll(jnp.concatenate(parts, axis=0), rest + 24, 0)
            out_ref[p] = jnp.where(covered, moved[:ROWS], stepped_ref[p])


VMEM = pl.BlockSpec(memory_space=pltpu.VMEM)
SMEM = pl.BlockSpec(memory_space=pltpu.SMEM)


def shaped(*shape):
    return jax.ShapeDtypeStruct(shape, jnp.float32)


def in_rounds(edges, count):
    at = {}
    for source, target in edges:
        mine, theirs = ("from", source), ("to", target)
        a = next(c for c in range(count) if (mine, c) not in at)
        b = next(c for c in range(count) if (theirs, c) not in at)
        path = []
        node, color = theirs, a
        while (node, color) in at:
            node_next = at[(node, color)]
            path.append((node, node_next, color))
            node, color = node_next, (b if color == a else a)
        for one, two, color in path:
            del at[(one, color)], at[(two, color)]
        for one, two, color in path:
            swapped = b if color == a else a
            at[(one, swapped)] = two
            at[(two, swapped)] = one
        at[(mine, a)] = theirs
        at[(theirs, a)] = mine
    rounds = [[] for _ in range(count)]
    for (node, color), other in sorted(at.items()):
        if node[0] == "from":
            rounds[color].append((node[1], other[1]))
    return rounds


def hops(one, two):
    (t, s), (u, r) = divmod(one, 4), divmod(two, 4)
    links = abs((t >> 2) - (u >> 2)) + abs(((t >> 1) & 1) - ((u >> 1) & 1)) + abs(s - r)
    return links or 0.8


def completed(pairs, valid, power=3):
    senders = [d for d in range(32) if d not in {a for a, _ in pairs}]
    takers = [d for d in range(32) if d not in {b for _, b in pairs}]

    def cost(a, b):
        from_parent = a % 4 == 0 and b % 4 > 0
        return 1e3 if a == b or from_parent or (a, b) in valid else hops(a, b) ** power

    n = len(senders)
    row_price, column_price = [0.0] * (n + 1), [0.0] * (n + 1)
    owner = [0] * (n + 1)
    for i in range(1, n + 1):
        owner[0] = i
        column = 0
        least, before, used = [1e9] * (n + 1), [0] * (n + 1), [False] * (n + 1)
        while True:
            used[column] = True
            row, step, best = owner[column], 1e9, 0
            for j in range(1, n + 1):
                if not used[j]:
                    gap = cost(senders[row - 1], takers[j - 1]) - row_price[row] - column_price[j]
                    if gap < least[j]:
                        least[j], before[j] = gap, column
                    if least[j] < step:
                        step, best = least[j], j
            for j in range(n + 1):
                if used[j]:
                    row_price[owner[j]] += step
                    column_price[j] -= step
                else:
                    least[j] -= step
            column = best
            if owner[column] == 0:
                break
        while column:
            owner[column], column = owner[before[column]], before[column]
    return pairs + [(senders[owner[j] - 1], takers[j - 1]) for j in range(1, n + 1)]


def rim_pairs(case):
    start = max(case, 1)
    sends = {
        1: [(0, 0), (1, 1), (0, 2), (1, 3), (2, 3), (2, 4), (1, 5), (3, 4), (2, 6), (3, 7)],
        3: [(0, 0), (1, 1), (0, 2), (1, 3), (2, 2), (2, 4), (1, 5), (3, 5), (2, 6), (3, 7)],
    }
    corners = {low: low + 1 for low in (1, 3, 5)}
    corners.update({high: low for low, high in list(corners.items())})
    crowded = [(device(4, 2), device(3, 1)), (device(3, 2), device(4, 1))]
    crowded += [(device(1, 2), device(2, 3)), (device(6, 2), device(5, 3))]
    middle = [[(start, 0), (start + 1, 1), (start + 2, 6), (start + 3, 7)]]
    middle = [[(device(a, 0), device(b, 2)) for a, b in pairs] for pairs in middle]
    middle[0] += crowded
    if case == 0:
        middle.append([(device(0, 0), device(0, 2)), (device(2, 0), device(6, 1))])
        middle.append([(device(2, 0), device(6, 3))])
    power = 2 if start == 2 else 3
    groups = []
    for section, inner, order in (
        (1, ((2, 1), (3, 2)), (1, 2, 0) if start == 2 else (2, 0, 1)),
        (3, ((1, 2), (2, 3)), (1, 2, 0)),
    ):
        edges = [(device(t, a), device(t, b)) for a, b in inner for t in range(8)]
        edges += [(device(corners[t], a), device(t, b)) for a, b in inner for t in corners]
        edges = [pair for pair in edges if pair not in crowded]
        edges += [(device(start + a, 0), device(b, section)) for a, b in sends[section]]
        if start == 1:
            edges.append((device(0, 0), device(0, section)))
        rounds = in_rounds(edges, 3)
        groups.append([completed(rounds[i], edges, power) for i in order])
    middle = [completed(pairs, [], power) for pairs in middle]
    return groups[0], middle, groups[1]


BOTH = ("tile", "section")


def on_device(state, courant, nest_offset):
    planes = state.reshape(STATES, ROWS, COLS)
    speeds = courant.reshape(4, ROWS, COLS)
    offset = nest_offset[0]
    *payloads, to_pair, to_cross = pl.pallas_call(
        pack_kernel,
        out_shape=[shaped(SLOTS, 2 * LANE)] * 3
        + [shaped(SLOTS, COLS)] * 2,
        in_specs=[SMEM, VMEM, VMEM],
        out_specs=[VMEM] * 5,
        name="pack",
    )(nest_offset, planes, speeds)

    pair_map = [(device(t, s), device(t ^ 1, s)) for t in range(8) for s in range(4)]
    cross_map = [(device(t, s), device(t ^ ring_step(t), s)) for t in range(8) for s in range(4)]

    def send_rims(case, to_pair, to_cross, west, middle, east):
        from_cross = lax.ppermute(to_cross, BOTH, cross_map)
        groups = rim_pairs(case)
        west, middle, east = (
            [lax.ppermute(value, BOTH, pairs) for pairs in lists]
            for value, lists in zip((west, middle, east), groups)
        )
        return pl.pallas_call(
            functools.partial(relay_kernel, max(case, 1), len(middle)),
            out_shape=[
                shaped(32, LANE),
                shaped(32, LANE),
                shaped(RIMS, 2 * LANE),
                shaped(HALO + RIMS, COLS),
                shaped(SLOTS, COLS),
            ],
            in_specs=[VMEM] * (8 + len(middle)),
            out_specs=[VMEM] * 5,
            name="relay",
        )(to_pair, from_cross, *east, *middle, *west)

    west, east, rims, to_pair, from_cross = lax.switch(
        (offset - 2) // ROWS,
        [functools.partial(send_rims, case) for case in range(4)],
        to_pair,
        to_cross,
        *payloads,
    )
    from_pair = lax.ppermute(to_pair, BOTH, pair_map)
    stepped, means = pl.pallas_call(
        main_kernel,
        out_shape=[shaped(STATES, ROWS, COLS), shaped(STATES * 8, LANE)],
        in_specs=[SMEM] + [VMEM] * 7,
        out_specs=[VMEM] * 2,
        scratch_shapes=[
            pltpu.VMEM((STATES, 32, 4 * LANE), jnp.float32),
            pltpu.VMEM((STATES, 32, 4 * LANE), jnp.float32),
            pltpu.VMEM((2, 6, 32, 4 * LANE), jnp.float32),
            pltpu.VMEM((2, STATES, 32, LANE), jnp.float32),
            pltpu.VMEM((2, STATES, 8, 4 * LANE), jnp.float32),
            pltpu.VMEM((STATES * ROWS, LANE), jnp.float32),
        ],
        compiler_params=pltpu.CompilerParams(vmem_limit_bytes=32 * 1024 * 1024),
        name="nest",
    )(nest_offset, planes, speeds, west, east, rims, from_pair, from_cross)
    def gather_from(s):
        pairs = [(device(t, s), device(t, 0)) for t in range(8)]
        if s == 2:
            pairs = completed(pairs, [])
        return lax.ppermute(means, BOTH, pairs)

    got = {s: gather_from(s) for s in (1, 2, 3)}
    columns = jnp.concatenate([got[s] for s in (1, 2, 3)], axis=1)

    def across(value, partner):
        pairs = [(device(t, s), device(partner(t), s)) for t in range(8) for s in range(4)]
        return lax.ppermute(value, BOTH, pairs)

    def mate(t):
        return t ^ 1

    ways = (lambda t: t ^ ring_step(t), lambda t: t ^ (10 - ring_step(t)), lambda t: t ^ 4)
    blocks = [columns, across(columns, mate)]
    blocks += [across(columns, way) for way in ways]
    blocks += [across(block, mate) for block in blocks[2:]]
    merged = pl.pallas_call(
        merge_kernel,
        out_shape=shaped(STATES, ROWS, COLS),
        in_specs=[SMEM] + [VMEM] * 9,
        out_specs=VMEM,
        scratch_shapes=[pltpu.VMEM((4, STATES * 8, COLS), jnp.float32)],
        compiler_params=pltpu.CompilerParams(vmem_limit_bytes=32 * 1024 * 1024),
        name="merge",
    )(nest_offset, *blocks, stepped)
    return merged.reshape(state.shape)


def solution(mesh):
    small = mesh.shape["tile"] == 8 and mesh.shape["section"] == 4
    return jax.shard_map(
        on_device if small else general_on_device,
        mesh=mesh,
        in_specs=(P(None, None, "tile", "section"), P(None, None, "tile", "section"), P()),
        out_specs=P(None, None, "tile", "section"),
        check_vma=False,
    )
```
